32 devices in a mesh: leaf: 4 (over x, core), row: 8 (over z, y).
Axes of the slice: x: 2, y: 2, z: 4, core: 2. Of those that a mesh axis runs over, the one named last changes fastest.
Arguments:
- loc_rhs: float32 [4, 8, 512, 128], P('leaf', 'row'), may hold values from -6 to 6
- loc_inverse: float32 [4, 8, 512, 512], P('leaf', 'row'), may hold values from -0.25 to 0.25
- loc_coupling: float32 [4, 8, 512, 512], P('leaf', 'row'), may hold values from -0.09375 to 0.09375
- loc_pivots: float32 [4, 8, 512], P('leaf', 'row'), may hold values from 0.5 to 4
- pattern: int32 [4, 8, 4], P('leaf', 'row'), may hold values from 0 to 13, as said below
- win_rhs: float32 [3, 1024, 128], P(None, ('leaf', 'row')), may hold values from -6 to 6
- win_pivots: float32 [3, 1024], P(None, ('leaf', 'row')), may hold values from 0.5 to 4
- win_inverse: float32 [8, 224, 1024], P('row', None, 'leaf'), may hold values from -0.1875 to 0.1875
- win_coupling: float32 [8, 192, 1024], P('row', None, 'leaf'), may hold values from -0.1875 to 0.1875
Outputs:
- loc_solution: float32 [4, 8, 512, 128], P('leaf', 'row')
- win_solution: float32 [3, 1024, 128], P(None, ('leaf', 'row'))
The draws below stay inside these ranges and needn't reach their ends.
Inputs may be any that keep to these rules, and one draw needn't show every extreme that they name: `pattern`: on each device the 4 tile numbers are distinct; number p stands for rows p * 128 to (p + 1) * 128 - 1 of the path of the device's leaf index.
All inputs are finite; a program needn't handle non-finite values.
Results may differ from the reference program's by a relative error of at most 0.0001.
Values sent between devices are 32-bit elements; how exact they have to be, the bound alone decides.
No kernel may reach another device: no remote copies, remote signals or barrier semaphores. Data moves between devices by JAX's collectives and lax.ppermute only.
A program may use at most 64 MiB of HBM per device.

```python
import math
import jax
import jax.numpy as jnp
from jax import lax

RHS = 128
BASE = 256
LOC = 512
TILE = 128
TILES = 4
LEAVES = 4
RANKS = 8
LEVELS = 3
PIECE = 32
PTILES = 14


def choose_tiles(single):
    return jax.random.permutation(single, PTILES)[:TILES]


def draw_pattern(key, part):
    subkeys = jax.random.split(key, LEAVES * RANKS)
    chosen = jax.vmap(choose_tiles)(subkeys)
    return chosen.reshape(LEAVES, RANKS, TILES).astype(jnp.int32)


def shard_levels(stream_key, dims, cuts, low, largest):
    factor_of, own = 1.0, jax.random.fold_in(stream_key, 6)
    for dim, blocks in cuts:
        draws = jnp.exp(jax.random.uniform(jax.random.fold_in(own, dim), (blocks,), jnp.float32, low / len(cuts), largest / len(cuts)))
        factor_of = factor_of * jnp.repeat(draws, dims[dim] // blocks).reshape([-1 if axis == dim else 1 for axis in range(len(dims))])
    return factor_of


def normal_values(stream_key, dims, width, reach, cuts=(), held_as=jnp.bfloat16):
    array = width * jax.random.normal(stream_key, dims, jnp.float32)
    if cuts:
        array = array * shard_levels(stream_key, dims, cuts, -0.22, 0.18)
    return jnp.clip(array, -reach, reach).astype(held_as)


def setup_inputs(seed: int = 0) -> dict:
    seeds = jax.random.split(jax.random.key(seed), 10)
    loc_rhs = normal_values(seeds[0], (LEAVES, RANKS, LOC, RHS), 1.0, 6.0, ((0, 4), (1, 8)), jnp.float32)
    loc_inverse = normal_values(seeds[1], (LEAVES, RANKS, LOC, LOC), LOC ** -0.5, 0.25, ((0, 4), (1, 8)), jnp.float32)
    loc_coupling = normal_values(seeds[2], (LEAVES, RANKS, TILES * TILE, LOC), (8 * LOC) ** -0.5, 0.09375, ((0, 4), (1, 8)), jnp.float32)
    loc_pivots = jnp.clip(jnp.exp(math.log(4.0) - 2.0794415 * jax.random.uniform(seeds[3], (LEAVES, RANKS, LOC), jnp.float32) ** shard_levels(seeds[3], (LEAVES, RANKS, LOC), ((0, 4), (1, 8)), -0.2, 0.2)), 0.5, 4.0)
    pattern = draw_pattern(jax.random.fold_in(seeds[9], 71), 0)
    win_rhs = normal_values(seeds[5], (LEVELS, LEAVES * BASE, RHS), 1.0, 6.0, ((1, 32),), jnp.float32)
    win_pivots = jnp.clip(jnp.exp(math.log(4.0) - 2.0794415 * jax.random.uniform(seeds[6], (LEVELS, LEAVES * BASE), jnp.float32) ** shard_levels(seeds[6], (LEVELS, LEAVES * BASE), ((1, 32),), -0.2, 0.2)), 0.5, 4.0)
    win_inverse = normal_values(seeds[7], (RANKS, (2 * LEAVES - 1) * PIECE, LEAVES * BASE), (LEAVES * BASE) ** -0.5, 0.1875, ((0, 8), (2, 4)), jnp.float32)
    win_coupling = normal_values(seeds[8], (RANKS, (2 * LEAVES - 2) * PIECE, LEAVES * BASE), (LEAVES * BASE) ** -0.5, 0.1875, ((0, 8), (2, 4)), jnp.float32)
    return {"loc_rhs": loc_rhs, "loc_inverse": loc_inverse, "loc_coupling": loc_coupling, "loc_pivots": loc_pivots, "pattern": pattern, "win_rhs": win_rhs, "win_pivots": win_pivots, "win_inverse": win_inverse, "win_coupling": win_coupling}


PRECISE = lax.Precision.HIGHEST


def strict_lower(matrix):
    extent = matrix.shape[-1]
    row_ids = jnp.arange(extent, dtype=jnp.int32)[:, None]
    col_ids = jnp.arange(extent, dtype=jnp.int32)[None, :]
    return jnp.where(col_ids < row_ids, matrix, jnp.zeros_like(matrix))


def level_rows(stacked, offset, group_span):
    chosen = stacked[:, offset:offset + group_span * PIECE, :]
    chosen = chosen.reshape(RANKS, group_span, PIECE, LEAVES * BASE)
    chosen = jnp.transpose(chosen, (1, 0, 2, 3))
    return chosen.reshape(group_span * BASE, LEAVES * BASE)


def node_blocks(matrix):
    node_width = matrix.shape[0]
    node_count = matrix.shape[1] // node_width
    return jnp.transpose(matrix.reshape(node_width, node_count, node_width), (1, 0, 2))


def local_forward(operands):
    right_side, inverse, coupling = operands
    solved = right_side + jnp.dot(strict_lower(inverse), right_side, precision=PRECISE)
    return solved, jnp.dot(coupling, solved, precision=PRECISE)


def local_backward(operands):
    scaled, inverse, coupling, picked = operands
    remainder = scaled - jnp.dot(coupling.T, picked, precision=PRECISE)
    return remainder + jnp.dot(strict_lower(inverse).T, remainder, precision=PRECISE)


def reference(loc_rhs, loc_inverse, loc_coupling, loc_pivots, pattern, win_rhs, win_pivots, win_inverse, win_coupling):
    devices = LEAVES * RANKS
    inverses = loc_inverse.reshape(devices, LOC, LOC)
    couplings = loc_coupling.reshape(devices, TILES * TILE, LOC)
    solved_loc, loc_terms = lax.map(local_forward, (loc_rhs.reshape(devices, LOC, RHS), inverses, couplings))
    leaf_ids = jnp.broadcast_to(jnp.arange(LEAVES, dtype=jnp.int32)[:, None, None], (LEAVES, RANKS, TILES))
    path_rows = jnp.zeros((LEAVES, PTILES, TILE, RHS), jnp.float32)
    path_rows = path_rows.at[leaf_ids, pattern].add(loc_terms.reshape(LEAVES, RANKS, TILES, TILE, RHS))
    path_rows = path_rows.reshape(LEAVES, PTILES * TILE, RHS)
    diagonals = []
    links = []
    local_sums = []
    for height in range(LEVELS):
        group_span = 2 ** height
        node_width = BASE * group_span
        diagonals.append(strict_lower(node_blocks(level_rows(win_inverse, (group_span - 1) * PIECE, group_span))))
        if height + 1 < LEVELS:
            links.append(node_blocks(level_rows(win_coupling, (2 * group_span - 2) * PIECE, 2 * group_span)))
        segment = path_rows[:, BASE * (group_span - 1):BASE * (2 * group_span - 1)]
        segment = segment.reshape(LEAVES // group_span, group_span, node_width, RHS).sum(axis=1)
        local_sums.append(segment.reshape(LEAVES * BASE, RHS))
    from_children = jnp.zeros((LEAVES * BASE, RHS), jnp.float32)
    solved = []
    for height in range(LEVELS):
        node_width = BASE * 2 ** height
        residual = (win_rhs[height] - local_sums[height] - from_children).reshape(-1, node_width, RHS)
        current = residual + jnp.einsum("kab,kbx->kax", diagonals[height], residual, precision=PRECISE)
        solved.append(current.reshape(LEAVES * BASE, RHS))
        if height + 1 < LEVELS:
            stacked = current.reshape(-1, 2 * node_width, RHS)
            from_children = jnp.einsum("kab,kbx->kax", links[height], stacked, precision=PRECISE).reshape(LEAVES * BASE, RHS)
    from_parent = jnp.zeros((LEAVES * BASE, RHS), jnp.float32)
    results = [None] * LEVELS
    for height in reversed(range(LEVELS)):
        node_width = BASE * 2 ** height
        wanted = (solved[height] / win_pivots[height][:, None] - from_parent).reshape(-1, node_width, RHS)
        current = wanted + jnp.einsum("kba,kbx->kax", diagonals[height], wanted, precision=PRECISE)
        results[height] = current.reshape(LEAVES * BASE, RHS)
        if height > 0:
            from_parent = jnp.einsum("kba,kbx->kax", links[height - 1], current, precision=PRECISE).reshape(LEAVES * BASE, RHS)
    pieces = []
    for height in range(LEVELS):
        group_span = 2 ** height
        node_vecs = results[height].reshape(LEAVES // group_span, BASE * group_span, RHS)
        pieces.append(jnp.repeat(node_vecs, group_span, axis=0))
    full_path = jnp.concatenate(pieces, axis=1).reshape(LEAVES, PTILES, TILE, RHS)
    picked = full_path[leaf_ids, pattern].reshape(devices, TILES * TILE, RHS)
    scaled_loc = solved_loc / loc_pivots.reshape(devices, LOC)[:, :, None]
    answer = lax.map(local_backward, (scaled_loc, inverses, couplings, picked))
    return answer.reshape(LEAVES, RANKS, LOC, RHS), jnp.stack(results)
```

```python
import jax
import jax.numpy as jnp
from jax import lax
from jax.sharding import PartitionSpec as P

TILE = 128
NEAR = lax.Precision.HIGH


def dot(left, right, left_dim, right_dim):
    return lax.dot_general(left, right, (((left_dim,), (right_dim,)), ((), ())), precision=NEAR)


def swap(value, axis, count, offset):
    return lax.ppermute(value, axis, [(i, i ^ offset) for i in range(count)])


def gather_rows(block, count, me):
    parts = [(0, block)]
    step = count // 2
    while step:
        stacked = jnp.stack([p for _, p in parts])
        other = swap(stacked, "row", count, step)
        parts = parts + [(o ^ step, other[i]) for i, (o, _) in enumerate(parts)]
        step //= 2
    parts.sort(key=lambda pair: pair[0])
    stacked = jnp.stack([p for _, p in parts])
    return jnp.stack(
        [lax.dynamic_index_in_dim(stacked, me ^ r, 0, keepdims=False) for r in range(count)]
    )


def shards(
    loc_rhs,
    loc_inverse,
    loc_coupling,
    loc_pivots,
    pattern,
    win_rhs,
    win_pivots,
    win_inverse,
    win_coupling,
):
    leaves = lax.axis_size("leaf")
    ranks = lax.axis_size("row")
    leaf = lax.axis_index("leaf")
    rank = lax.axis_index("row")
    levels, piece, columns = win_rhs.shape
    base = piece * ranks
    share = columns // ranks
    path_tiles = (2 * leaves - 1) * base // TILE
    tiles = pattern.shape[2]
    local = loc_rhs.shape[2]

    def group_swaps(value, height):
        return [value] + [swap(value, "leaf", leaves, j) for j in range(1, 2**height)]

    def group_sum(value, height):
        return sum(group_swaps(value, height))

    def group_gather(value, height):
        span = 2**height
        stacked = jnp.stack(group_swaps(value, height))
        return jnp.concatenate(
            [
                lax.dynamic_index_in_dim(stacked, leaf % span ^ q, 0, keepdims=False)
                for q in range(span)
            ],
            -1,
        )

    def own(value, height):
        start = leaf % 2**height * base
        return lax.dynamic_slice_in_dim(value, start, base, 1)

    early = jnp.concatenate(
        [
            win_rhs.transpose(2, 0, 1).reshape(ranks, share, levels * piece),
            jnp.broadcast_to(win_pivots.reshape(1, 1, -1), (ranks, 1, levels * piece)),
            jnp.broadcast_to(
                jnp.pad(pattern[0].astype(jnp.float32), ((0, 0), (0, levels * piece - tiles))),
                (ranks, 1, levels * piece),
            ),
        ],
        1,
    )
    early = lax.all_to_all(early, "row", 0, 0, tiled=True)
    known = early[:, share + 1, :tiles].astype(jnp.int32)
    early = early[:, : share + 1].reshape(ranks, share + 1, levels, piece)
    early = early.transpose(2, 1, 0, 3).reshape(levels, share + 1, base)
    rhs, pivots = early[:, :share], early[:, share:]

    def stacked_rows(block, span):
        block = gather_rows(block, ranks, rank).reshape(ranks, span, piece, base)
        return block.transpose(1, 0, 2, 3).reshape(span * base, base)

    diagonals, links = [], []
    for height in range(levels):
        span = 2**height
        block = stacked_rows(win_inverse[0, (span - 1) * piece : (2 * span - 1) * piece], span)
        row_ids = jnp.arange(span * base)[:, None]
        col_ids = leaf % span * base + jnp.arange(base)[None, :]
        diagonals.append(jnp.where(col_ids < row_ids, block, 0.0))
        if height + 1 < levels:
            links.append(
                stacked_rows(
                    win_coupling[0, (2 * span - 2) * piece : (4 * span - 2) * piece], 2 * span
                )
            )

    rhs_loc = loc_rhs[0, 0]
    inverse = loc_inverse[0, 0]
    coupling = loc_coupling[0, 0]
    positions = jnp.arange(local)
    strict = jnp.where(positions[None, :] < positions[:, None], inverse, 0.0)
    solved_loc = rhs_loc.T + dot(rhs_loc, strict, 0, 1)
    terms = dot(solved_loc, coupling, 1, 1).reshape(ranks, share, tiles * TILE)
    terms = lax.all_to_all(terms, "row", 0, 0, tiled=True)
    hits = (known[:, :, None] == jnp.arange(path_tiles)).astype(jnp.float32)
    path = jnp.einsum(
        "bcti,btp->cpi",
        terms.reshape(ranks, share, tiles, TILE),
        hits,
        precision=lax.Precision.HIGHEST,
    ).reshape(share, path_tiles * TILE)

    ahead = jnp.zeros((share, base), jnp.float32)
    solved = []
    for height in range(levels):
        span = 2**height
        partial = -path[:, (span - 1) * base : (2 * span - 1) * base] - ahead
        partial = partial.reshape(share, span, base)
        mine = (jnp.arange(span) == leaf % span)[None, :, None]
        partial = (partial + jnp.where(mine, rhs[height][:, None], 0.0)).reshape(share, span * base)
        residual = group_sum(partial, height)
        product = dot(own(residual, height), diagonals[height], 1, 1)
        current = own(residual + group_sum(product, height), height)
        solved.append(current)
        if height + 1 < levels:
            ahead = dot(current, links[height], 1, 1)

    above = jnp.zeros((share, base), jnp.float32)
    results = [None] * levels
    wholes = [None] * levels
    for height in reversed(range(levels)):
        wanted = solved[height] / pivots[height] - above
        full = group_gather(wanted, height)
        results[height] = wanted + dot(full, diagonals[height], 1, 0)
        wholes[height] = group_gather(results[height], height)
        if height > 0:
            above = dot(wholes[height], links[height - 1], 1, 0)
    whole = jnp.concatenate(wholes, 1).reshape(share, path_tiles, TILE)

    reply = jnp.einsum(
        "cpi,btp->bcti", whole, hits, precision=lax.Precision.HIGHEST
    ).reshape(ranks, share, tiles * TILE)
    final = jnp.stack(results).reshape(levels, share, ranks, piece)
    final = final.transpose(2, 1, 0, 3).reshape(ranks, share, levels * piece)
    back = lax.all_to_all(jnp.concatenate([reply, final], 2), "row", 0, 0, tiled=True)
    back = back.reshape(columns, tiles * TILE + levels * piece)
    picked = back[:, : tiles * TILE]
    final = back[:, tiles * TILE :].reshape(columns, levels, piece).transpose(1, 2, 0)

    remainder = solved_loc / loc_pivots[0] - dot(picked, coupling, 1, 0)
    answer = remainder.T + dot(strict, remainder, 0, 1)
    return answer[None, None], final


def solution(mesh):
    return jax.shard_map(
        shards,
        mesh=mesh,
        in_specs=(
            P("leaf", "row", None, None),
            P("leaf", "row", None, None),
            P("leaf", "row", None, None),
            P("leaf", "row", None),
            P("leaf", "row", None),
            P(None, ("leaf", "row"), None),
            P(None, ("leaf", "row")),
            P("row", None, "leaf"),
            P("row", None, "leaf"),
        ),
        out_specs=(P("leaf", "row", None, None), P(None, ("leaf", "row"), None)),
        check_vma=False,
    )
```

```python
import jax
import jax.numpy as jnp
from jax import lax
from jax.experimental import pallas as pl
from jax.experimental.pallas import tpu as pltpu
from jax.sharding import PartitionSpec as P

TILE = 128
EXACT = lax.Precision.HIGHEST
F32 = jnp.float32
BF16 = jnp.bfloat16


def swap(value, axis, count, offset):
    return lax.ppermute(value, axis, [(i, i ^ offset) for i in range(count)])


def gather_parts(block, count):
    parts = {0: block}
    step = count // 2
    while step:
        for offset in list(parts):
            parts[offset ^ step] = swap(parts[offset], "row", count, step)
        step //= 2
    return [parts[offset] for offset in range(count)]


def call(body, outs, arrays, scalars=(), scratch=()):
    return pl.pallas_call(
        body,
        out_shape=[jax.ShapeDtypeStruct(*o) for o in outs],
        in_specs=[pl.BlockSpec(memory_space=pltpu.SMEM)] * len(scalars)
        + [pl.BlockSpec(memory_space=pltpu.VMEM)] * len(arrays),
        out_specs=[pl.BlockSpec(memory_space=pltpu.VMEM)] * len(outs),
        scratch_shapes=list(scratch),
        compiler_params=pltpu.CompilerParams(vmem_limit_bytes=40 << 20),
    )(*scalars, *arrays)


def split(value):
    high = value.astype(BF16).astype(F32)
    return high, value - high


def times(value, high, low, right_dim):
    rows = value.shape[0]
    dims = (((1,), (right_dim,)), ((), ()))

    def product(part):
        return lax.dot_general(part, high, dims, preferred_element_type=F32) + lax.dot_general(
            part, low, dims, preferred_element_type=F32
        )

    first, second = split(value)
    if rows % 8:
        return product(first.astype(BF16)) + product(second.astype(BF16))
    both = product(jnp.concatenate([first, second], 0).astype(BF16))
    return both[:rows] + both[rows:]


def strict_lower(block):
    row_ids = lax.broadcasted_iota(jnp.int32, block.shape, 0)
    col_ids = lax.broadcasted_iota(jnp.int32, block.shape, 1)
    return jnp.where(col_ids < row_ids, block, 0.0)


def shards(
    loc_rhs,
    loc_inverse,
    loc_coupling,
    loc_pivots,
    pattern,
    win_rhs,
    win_pivots,
    win_inverse,
    win_coupling,
):
    leaves = lax.axis_size("leaf")
    ranks = lax.axis_size("row")
    leaf = lax.axis_index("leaf")
    rank = lax.axis_index("row")
    levels, piece, columns = win_rhs.shape
    base = piece * ranks
    share = columns // ranks
    halves = base // TILE
    path_tiles = (2 * leaves - 1) * halves
    tiles = pattern.shape[2]
    local = loc_rhs.shape[2]
    top = levels - 1
    ids = jnp.stack([leaf, rank]).astype(jnp.int32)
    wide = (share, base)

    def leaf_swaps(values):
        return [values[0]] + [swap(v, "leaf", leaves, j) for j, v in enumerate(values) if j]

    def inverse_rows(level):
        return (2**level - 1) * piece, (2 ** (level + 1) - 1) * piece

    def coupling_rows(level):
        return (2 ** (level + 1) - 2) * piece, (2 ** (level + 2) - 2) * piece

    def gathered(names):
        rows = []
        for kind, level in names:
            source = win_inverse if kind == "A" else win_coupling
            low, high = inverse_rows(level) if kind == "A" else coupling_rows(level)
            rows.append(source[0, low:high])
        return gather_parts(jnp.concatenate(rows, 0), ranks)

    def assemble(parts, names):
        spans = [2**level if kind == "A" else 2 ** (level + 1) for kind, level in names]

        def body(ids_ref, *refs):
            parts_refs, outs = refs[:ranks], refs[ranks:-1]
            natural = refs[-1]
            me, group = ids_ref[1], ids_ref[0]
            for offset, ref in enumerate(parts_refs):
                start = pl.multiple_of((me ^ offset) * piece, 8)
                for slot in range(sum(spans)):
                    natural[slot, pl.ds(start, piece), :] = ref[
                        slot * piece : (slot + 1) * piece, :
                    ]
            first = 0
            for index, ((kind, level), span) in enumerate(zip(names, spans)):
                for slot in range(span):
                    block = natural[first + slot]
                    if kind == "A":
                        row_ids = lax.broadcasted_iota(jnp.int32, block.shape, 0) + slot * base
                        col_ids = lax.broadcasted_iota(jnp.int32, block.shape, 1)
                        col_ids = col_ids + group % span * base
                        block = jnp.where(col_ids < row_ids, block, 0.0)
                    high, low = split(block)
                    outs[2 * index][slot] = high.astype(BF16)
                    outs[2 * index + 1][slot] = low.astype(BF16)
                first += span

        outs = [((span, base, base), BF16) for span in spans for _ in range(2)]
        made = call(
            body, outs, parts, (ids,), [pltpu.VMEM((sum(spans), base, base), F32)]
        )
        return {name: made[2 * i : 2 * i + 2] for i, name in enumerate(names)}

    lower_names = [("A", level) for level in range(top)]
    lower_names += [("B", level) for level in range(top - 1)]
    upper_names = [("B", top - 1), ("A", top)]
    lower_parts = gathered(lower_names)
    upper_parts = gathered(upper_names)

    def local_forward(rhs_ref, inverse_ref, coupling_ref, solved_ref, terms_ref):
        rhs = rhs_ref[...]
        solved = rhs + jnp.dot(strict_lower(inverse_ref[...]), rhs, precision=EXACT)
        solved_ref[...] = solved.T
        terms_ref[...] = jnp.dot(coupling_ref[...], solved, precision=EXACT).T

    solved_loc, terms = call(
        local_forward,
        [((columns, local), F32), ((columns, tiles * TILE), F32)],
        (loc_rhs[0, 0], loc_inverse[0, 0], loc_coupling[0, 0]),
    )
    terms = lax.all_to_all(
        terms.reshape(ranks, share, tiles * TILE), "row", 0, 0, tiled=True
    )

    extra = jnp.pad(pattern[0].astype(F32), ((0, 0), (0, levels * piece - tiles)))
    early = jnp.concatenate(
        [
            win_rhs.transpose(2, 0, 1).reshape(ranks, share, levels * piece),
            jnp.broadcast_to(win_pivots.reshape(1, 1, -1), (ranks, 1, levels * piece)),
            jnp.broadcast_to(extra, (ranks, 1, levels * piece)),
        ],
        1,
    )
    early = lax.all_to_all(early, "row", 0, 0, tiled=True)
    known = early[:, share + 1, :tiles].astype(jnp.int32).reshape(-1)
    early = early[:, : share + 1].reshape(ranks, share + 1, levels, piece)
    early = early.transpose(2, 1, 0, 3).reshape(levels, share + 1, base)
    rhs, pivots = early[:, :share], early[:, share:]
    top_pivots = leaf_swaps([pivots[top]] * leaves)

    lower = assemble(lower_parts, lower_names)
    upper = assemble(upper_parts, upper_names)
    blocks = {**lower, **upper}

    def scatter(ids_ref, known_ref, terms_ref, rhs_ref, *refs):
        outs, path = refs[:-1], refs[-1]
        path[...] = jnp.zeros_like(path)
        for source in range(ranks):
            for tile in range(tiles):
                place = known_ref[source * tiles + tile]
                path[place] = path[place] - terms_ref[source, :, tile * TILE : (tile + 1) * TILE]
        for level in range(levels):
            span = 2**level
            for slot in range(span):
                first = (span - 1 + slot) * halves
                outs[level][slot] = jnp.concatenate([path[first + h] for h in range(halves)], 1)
            own = ids_ref[0] % span
            outs[level][own] = outs[level][own] + rhs_ref[level]

    rest = call(
        scatter,
        [((2**level, *wide), F32) for level in range(levels)],
        (terms, rhs),
        (ids, known),
        [pltpu.VMEM((path_tiles, share, TILE), F32)],
    )

    def total(refs):
        value = refs[0][...]
        for ref in refs[1:]:
            value = value + ref[...]
        return value

    def diagonal(level, chunks):
        span = 2**level
        high, low = blocks["A", level]

        def body(ids_ref, *refs):
            chunk_refs, (high_ref, low_ref) = refs[:span], refs[span : span + 2]
            outs, parts = refs[span + 2 : -1], refs[-1]
            own = ids_ref[0] % span
            value = total(chunk_refs)
            for slot in range(span):
                parts[slot] = times(value, high_ref[slot], low_ref[slot], 1)
            parts[own] = parts[own] + value
            if level == top:
                outs[0][...] = parts[...]
            else:
                for offset, out in enumerate(outs):
                    out[...] = parts[own ^ offset]

        outs = [((span, *wide), F32)] if level == top else [(wide, F32)] * span
        return call(
            body, outs, (*chunks, high, low), (ids,), [pltpu.VMEM((span, *wide), F32)]
        )

    def link(level, chunks):
        span, above = 2**level, 2 ** (level + 1)
        high, low = blocks["B", level]

        def body(ids_ref, *refs):
            chunk_refs = refs[:span]
            high_ref, low_ref, rest_ref, solved_ref = refs[span : span + 4]
            outs, parts = refs[span + 4 : -1], refs[-1]
            value = total(chunk_refs)
            solved_ref[...] = value
            for slot in range(above):
                parts[slot] = rest_ref[slot] - times(value, high_ref[slot], low_ref[slot], 1)
            own = ids_ref[0] % above
            for offset, out in enumerate(outs):
                out[...] = parts[own ^ offset]

        made = call(
            body,
            [(wide, F32)] * (above + 1),
            (*chunks, high, low, rest[level + 1]),
            (ids,),
            [pltpu.VMEM((above, *wide), F32)],
        )
        return made[0], made[1:]

    chunks = [rest[0][0]]
    solved = []
    for level in range(top):
        chunks = leaf_swaps(diagonal(level, chunks))
        value, chunks = link(level, chunks)
        solved.append(value)
        chunks = leaf_swaps(chunks)
    sums = leaf_swaps(diagonal(top, chunks) * leaves)

    def peak(ids_ref, *refs):
        sum_refs, pivot_refs = refs[:leaves], refs[leaves : 2 * leaves]
        high_ref, low_ref, out, wanted = refs[2 * leaves :]
        own = ids_ref[0] % leaves
        wanted[...] = total(sum_refs)
        for offset, ref in enumerate(pivot_refs):
            wanted[own ^ offset] = wanted[own ^ offset] / ref[...]
        value = wanted[own]
        for slot in range(leaves):
            value = value + times(wanted[slot], high_ref[slot], low_ref[slot], 0)
        out[...] = value

    current = call(
        peak,
        [(wide, F32)],
        (*sums, *top_pivots, *blocks["A", top]),
        (ids,),
        [pltpu.VMEM((leaves, *wide), F32)],
    )

    def ordered(own, refs, held):
        for offset, ref in enumerate(refs):
            held[own ^ offset] = ref[...]

    def against(held, high_ref, low_ref, span):
        value = times(held[0], high_ref[0], low_ref[0], 0)
        for slot in range(1, span):
            value = value + times(held[slot], high_ref[slot], low_ref[slot], 0)
        return value

    def descend(level, parts):
        span = 2**level

        def body(ids_ref, *refs):
            part_refs = refs[:span]
            high_ref, low_ref, solved_ref, pivot_ref, out, held = refs[span:]
            ordered(ids_ref[0] % span, part_refs, held)
            above = against(held, high_ref, low_ref, span)
            out[...] = solved_ref[...] / pivot_ref[...] - above

        return call(
            body,
            [(wide, F32)],
            (*parts, *blocks["B", level - 1], solved[level - 1], pivots[level - 1]),
            (ids,),
            [pltpu.VMEM((span, *wide), F32)],
        )

    def transposed(level, parts):
        span = 2**level

        def body(ids_ref, *refs):
            part_refs = refs[:span]
            high_ref, low_ref, out, held = refs[span:]
            ordered(ids_ref[0] % span, part_refs, held)
            out[...] = part_refs[0][...] + against(held, high_ref, low_ref, span)

        return call(
            body,
            [(wide, F32)],
            (*parts, *blocks["A", level]),
            (ids,),
            [pltpu.VMEM((span, *wide), F32)],
        )

    everything = {top: leaf_swaps(current * leaves)}
    for level in range(top, 1, -1):
        wanted = leaf_swaps(descend(level, everything[level]) * 2 ** (level - 1))
        everything[level - 1] = leaf_swaps(transposed(level - 1, wanted) * 2 ** (level - 1))

    packed = tiles * TILE + TILE

    def finish(ids_ref, known_ref, *refs):
        refs = list(refs)
        parts = {level: [refs.pop(0) for _ in range(2**level)] for level in range(1, levels)}
        link_high, link_low, solved_ref, pivot_ref, high_ref, low_ref = refs[:6]
        outs, path, held = refs[6:-2], refs[-2], refs[-1]
        group, me = ids_ref[0], ids_ref[1]
        ordered(group % 2, parts[1], held)
        wanted = solved_ref[...] / pivot_ref[...] - against(held, link_high, link_low, 2)
        lowest = wanted + times(wanted, high_ref[0], low_ref[0], 0)
        owned = [lowest]
        for half in range(halves):
            path[half] = lowest[:, half * TILE : (half + 1) * TILE]
        for level in range(1, levels):
            span = 2**level
            owned.append(parts[level][0][...])
            for offset, ref in enumerate(parts[level]):
                first = (span - 1 + (group % span ^ offset)) * halves
                for half in range(halves):
                    path[first + half] = ref[:, half * TILE : (half + 1) * TILE]
        lane = lax.broadcasted_iota(jnp.int32, (share, TILE), 1)
        for offset, out in enumerate(outs):
            target = me ^ offset
            for tile in range(tiles):
                out[:, tile * TILE : (tile + 1) * TILE] = path[known_ref[target * tiles + tile]]
            pieces = jnp.zeros((share, TILE), F32)
            for level in range(levels):
                shift = (base + level * piece - target * piece) % base
                turned = pltpu.roll(owned[level], shift, 1)[:, :TILE]
                mine = (lane >= level * piece) & (lane < (level + 1) * piece)
                pieces = jnp.where(mine, turned, pieces)
            out[:, tiles * TILE :] = pieces

    replies = call(
        finish,
        [((share, packed), F32)] * ranks,
        (
            *[part for level in range(1, levels) for part in everything[level]],
            *blocks["B", 0],
            solved[0],
            pivots[0],
            *blocks["A", 0],
        ),
        (ids, known),
        [pltpu.VMEM((path_tiles, share, TILE), F32), pltpu.VMEM((2, *wide), F32)],
    )
    replies = [replies[0]] + [swap(v, "row", ranks, j) for j, v in enumerate(replies) if j]
    if share % 8:
        stacked = jnp.stack(replies)[rank ^ jnp.arange(ranks)]
        replies = [stacked.reshape(columns, packed)]

    def local_backward(ids_ref, *refs):
        refs = list(refs)
        reply_refs = [refs.pop(0) for _ in replies]
        solved_ref, pivot_ref, inverse_ref, coupling_ref, out, window_ref, back = refs
        me = ids_ref[1]
        if len(reply_refs) == 1:
            back[...] = reply_refs[0][...]
        else:
            for offset, ref in enumerate(reply_refs):
                start = pl.multiple_of((me ^ offset) * share, 8)
                back[pl.ds(start, share), :] = ref[...]
        remainder = solved_ref[...] / pivot_ref[...] - jnp.dot(
            back[:, : tiles * TILE], coupling_ref[...], precision=EXACT
        )
        answer = remainder + jnp.dot(
            remainder, strict_lower(inverse_ref[...]), precision=EXACT
        )
        out[...] = answer.T
        final = back[:, tiles * TILE :].T
        for level in range(levels):
            window_ref[level] = final[level * piece : (level + 1) * piece]

    answer, window = call(
        local_backward,
        [((local, columns), F32), ((levels, piece, columns), F32)],
        (*replies, solved_loc, loc_pivots[0], loc_inverse[0, 0], loc_coupling[0, 0]),
        (ids,),
        [pltpu.VMEM((columns, packed), F32)],
    )
    return answer[None, None], window


def solution(mesh):
    return jax.shard_map(
        shards,
        mesh=mesh,
        in_specs=(
            P("leaf", "row", None, None),
            P("leaf", "row", None, None),
            P("leaf", "row", None, None),
            P("leaf", "row", None),
            P("leaf", "row", None),
            P(None, ("leaf", "row"), None),
            P(None, ("leaf", "row")),
            P("row", None, "leaf"),
            P("row", None, "leaf"),
        ),
        out_specs=(P("leaf", "row", None, None), P(None, ("leaf", "row"), None)),
        check_vma=False,
    )
```

```python
import math

import jax
import jax.numpy as jnp
from jax import lax
from jax.experimental import pallas as pl
from jax.experimental.pallas import tpu as pltpu
from jax.sharding import PartitionSpec as P

TILE = 128
EXACT = lax.Precision.HIGHEST
F32 = jnp.float32
BF16 = jnp.bfloat16


def swap(value, axis, count, offset):
    return lax.ppermute(value, axis, [(i, i ^ offset) for i in range(count)])


def gather_parts(block, count):
    parts = {0: block}
    step = count // 2
    while step:
        for offset in list(parts):
            parts[offset ^ step] = swap(parts[offset], "row", count, step)
        step //= 2
    return [parts[offset] for offset in range(count)]


def call(body, outs, arrays, scalars=(), scratch=(), work=0):
    moved = sum(a.size * a.dtype.itemsize for a in arrays)
    moved += sum(math.prod(shape) * jnp.dtype(kind).itemsize for shape, kind in outs)
    return pl.pallas_call(
        body,
        out_shape=[jax.ShapeDtypeStruct(*o) for o in outs],
        in_specs=[pl.BlockSpec(memory_space=pltpu.SMEM)] * len(scalars)
        + [pl.BlockSpec(memory_space=pltpu.VMEM)] * len(arrays),
        out_specs=[pl.BlockSpec(memory_space=pltpu.VMEM)] * len(outs),
        scratch_shapes=list(scratch),
        compiler_params=pltpu.CompilerParams(vmem_limit_bytes=40 << 20),
        cost_estimate=pl.CostEstimate(flops=work, bytes_accessed=moved, transcendentals=0),
    )(*scalars, *arrays)


def split(value):
    high = value.astype(BF16).astype(F32)
    return high, value - high


def times(value, high, low, right_dim):
    rows = value.shape[0]
    dims = (((1,), (right_dim,)), ((), ()))

    def product(part):
        return lax.dot_general(part, high, dims, preferred_element_type=F32) + lax.dot_general(
            part, low, dims, preferred_element_type=F32
        )

    first, second = split(value)
    if rows % 8:
        return product(first.astype(BF16)) + product(second.astype(BF16))
    both = product(jnp.concatenate([first, second], 0).astype(BF16))
    return both[:rows] + both[rows:]


def strict_lower(block):
    row_ids = lax.broadcasted_iota(jnp.int32, block.shape, 0)
    col_ids = lax.broadcasted_iota(jnp.int32, block.shape, 1)
    return jnp.where(col_ids < row_ids, block, 0.0)


def shards(
    loc_rhs,
    loc_inverse,
    loc_coupling,
    loc_pivots,
    pattern,
    win_rhs,
    win_pivots,
    win_inverse,
    win_coupling,
):
    leaves = lax.axis_size("leaf")
    ranks = lax.axis_size("row")
    leaf = lax.axis_index("leaf")
    rank = lax.axis_index("row")
    levels, piece, columns = win_rhs.shape
    base = piece * ranks
    share = columns // ranks
    halves = base // TILE
    path_tiles = (2 * leaves - 1) * halves
    tiles = pattern.shape[2]
    local = loc_rhs.shape[2]
    top = levels - 1
    ids = jnp.stack([leaf, rank]).astype(jnp.int32)
    wide = (share, base)

    def leaf_swaps(values):
        return [values[0]] + [swap(v, "leaf", leaves, j) for j, v in enumerate(values) if j]

    def inverse_rows(level):
        return (2**level - 1) * piece, (2 ** (level + 1) - 1) * piece

    def coupling_rows(level):
        return (2 ** (level + 1) - 2) * piece, (2 ** (level + 2) - 2) * piece

    def gathered(names):
        rows = []
        for kind, level in names:
            source = win_inverse if kind == "A" else win_coupling
            low, high = inverse_rows(level) if kind == "A" else coupling_rows(level)
            rows.append(source[0, low:high])
        return gather_parts(jnp.concatenate(rows, 0), ranks)

    def assemble(parts, names):
        spans = [2**level if kind == "A" else 2 ** (level + 1) for kind, level in names]

        def body(ids_ref, *refs):
            parts_refs, outs = refs[:ranks], refs[ranks:-1]
            natural = refs[-1]
            me, group = ids_ref[1], ids_ref[0]
            for offset, ref in enumerate(parts_refs):
                start = pl.multiple_of((me ^ offset) * piece, 8)
                for slot in range(sum(spans)):
                    natural[slot, pl.ds(start, piece), :] = ref[
                        slot * piece : (slot + 1) * piece, :
                    ]
            first = 0
            for index, ((kind, level), span) in enumerate(zip(names, spans)):
                for slot in range(span):
                    block = natural[first + slot]
                    if kind == "A":
                        row_ids = lax.broadcasted_iota(jnp.int32, block.shape, 0) + slot * base
                        col_ids = lax.broadcasted_iota(jnp.int32, block.shape, 1)
                        col_ids = col_ids + group % span * base
                        block = jnp.where(col_ids < row_ids, block, 0.0)
                    high, low = split(block)
                    outs[2 * index][slot] = high.astype(BF16)
                    outs[2 * index + 1][slot] = low.astype(BF16)
                first += span

        outs = [((span, base, base), BF16) for span in spans for _ in range(2)]
        made = call(
            body, outs, parts, (ids,), [pltpu.VMEM((sum(spans), base, base), F32)]
        )
        return {name: made[2 * i : 2 * i + 2] for i, name in enumerate(names)}

    lower_names = [("A", level) for level in range(top)]
    lower_names += [("B", level) for level in range(top - 1)]
    upper_names = [("B", top - 1), ("A", top)]
    lower_parts = gathered(lower_names)
    upper_parts = gathered(upper_names)

    narrow = TILE - levels * piece
    aux = jnp.concatenate([win_pivots.reshape(-1), pattern[0, 0].astype(F32)])
    aux = jnp.pad(aux, (0, share * narrow - aux.size)).reshape(share, narrow)
    aux = jnp.tile(jnp.pad(aux, ((0, 0), (levels * piece, 0))), (ranks, 1))
    packed = tiles * TILE + TILE

    def local_forward(rhs_ref, inverse_ref, coupling_ref, window_ref, aux_ref, *outs):
        solved_ref, terms_ref, held = outs
        rhs = rhs_ref[...]
        solved = rhs + jnp.dot(strict_lower(inverse_ref[...]), rhs, precision=EXACT)
        solved_ref[...] = solved.T
        terms_ref[:, : tiles * TILE] = jnp.dot(coupling_ref[...], solved, precision=EXACT).T
        held[...] = jnp.zeros_like(held)
        for level in range(levels):
            held[level * piece : (level + 1) * piece, :] = window_ref[level]
        terms_ref[:, tiles * TILE :] = held[...].T + aux_ref[...]

    solved_loc, terms = call(
        local_forward,
        [((columns, local), F32), ((columns, packed), F32)],
        (loc_rhs[0, 0], loc_inverse[0, 0], loc_coupling[0, 0], win_rhs, aux),
        scratch=[pltpu.VMEM((TILE, columns), F32)],
        work=24 * local * local * columns,
    )
    terms = lax.all_to_all(terms.reshape(ranks, share, packed), "row", 0, 0, tiled=True)
    aux = terms[:, :, tiles * TILE + levels * piece :].reshape(ranks, -1)
    known = aux[:, levels * piece : levels * piece + tiles].astype(jnp.int32).reshape(-1)
    pivots = aux[:, : levels * piece].reshape(ranks, levels, piece)
    pivots = pivots.transpose(1, 0, 2).reshape(levels, 1, base)
    top_pivots = leaf_swaps([pivots[top]] * leaves)

    lower = assemble(lower_parts, lower_names)
    upper = assemble(upper_parts, upper_names)
    blocks = {**lower, **upper}

    def scatter(ids_ref, known_ref, terms_ref, *refs):
        outs, path = refs[:-1], refs[-1]
        lane = lax.broadcasted_iota(jnp.int32, (share, TILE), 1)
        path[...] = jnp.zeros_like(path)
        for source in range(ranks):
            for tile in range(tiles):
                place = known_ref[source * tiles + tile]
                path[place] = path[place] - terms_ref[source, :, tile * TILE : (tile + 1) * TILE]
        for level in range(levels):
            span = 2**level
            for slot in range(span):
                first = (span - 1 + slot) * halves
                outs[level][slot] = jnp.concatenate([path[first + h] for h in range(halves)], 1)
            own = ids_ref[0] % span
            rows = []
            for half in range(halves):
                row = jnp.zeros((share, TILE), F32)
                for source in range(half * TILE // piece, (half + 1) * TILE // piece):
                    place = source * piece % TILE
                    shift = (TILE + place - level * piece) % TILE
                    turned = pltpu.roll(terms_ref[source, :, tiles * TILE :], shift, 1)
                    row = jnp.where((lane >= place) & (lane < place + piece), turned, row)
                rows.append(row)
            outs[level][own] = outs[level][own] + jnp.concatenate(rows, 1)

    rest = call(
        scatter,
        [((2**level, *wide), F32) for level in range(levels)],
        (terms,),
        (ids, known),
        [pltpu.VMEM((path_tiles, share, TILE), F32)],
    )

    def total(refs):
        value = refs[0][...]
        for ref in refs[1:]:
            value = value + ref[...]
        return value

    def diagonal(level, chunks):
        span = 2**level
        high, low = blocks["A", level]

        def body(ids_ref, *refs):
            chunk_refs, (high_ref, low_ref) = refs[:span], refs[span : span + 2]
            outs, parts = refs[span + 2 : -1], refs[-1]
            own = ids_ref[0] % span
            value = total(chunk_refs)
            for slot in range(span):
                parts[slot] = times(value, high_ref[slot], low_ref[slot], 1)
            parts[own] = parts[own] + value
            if level == top:
                outs[0][...] = parts[...]
            else:
                for offset, out in enumerate(outs):
                    out[...] = parts[own ^ offset]

        outs = [((span, *wide), F32)] if level == top else [(wide, F32)] * span
        return call(
            body, outs, (*chunks, high, low), (ids,), [pltpu.VMEM((span, *wide), F32)]
        )

    def link(level, chunks):
        span, above = 2**level, 2 ** (level + 1)
        high, low = blocks["B", level]

        def body(ids_ref, *refs):
            chunk_refs = refs[:span]
            high_ref, low_ref, rest_ref, solved_ref = refs[span : span + 4]
            outs, parts = refs[span + 4 : -1], refs[-1]
            value = total(chunk_refs)
            solved_ref[...] = value
            for slot in range(above):
                parts[slot] = rest_ref[slot] - times(value, high_ref[slot], low_ref[slot], 1)
            own = ids_ref[0] % above
            for offset, out in enumerate(outs):
                out[...] = parts[own ^ offset]

        made = call(
            body,
            [(wide, F32)] * (above + 1),
            (*chunks, high, low, rest[level + 1]),
            (ids,),
            [pltpu.VMEM((above, *wide), F32)],
        )
        return made[0], made[1:]

    chunks = [rest[0][0]]
    solved = []
    for level in range(top):
        chunks = leaf_swaps(diagonal(level, chunks))
        value, chunks = link(level, chunks)
        solved.append(value)
        chunks = leaf_swaps(chunks)
    sums = leaf_swaps(diagonal(top, chunks) * leaves)

    def peak(ids_ref, *refs):
        sum_refs, pivot_refs = refs[:leaves], refs[leaves : 2 * leaves]
        high_ref, low_ref, out, wanted = refs[2 * leaves :]
        own = ids_ref[0] % leaves
        wanted[...] = total(sum_refs)
        for offset, ref in enumerate(pivot_refs):
            wanted[own ^ offset] = wanted[own ^ offset] / ref[...]
        value = wanted[own]
        for slot in range(leaves):
            value = value + times(wanted[slot], high_ref[slot], low_ref[slot], 0)
        out[...] = value

    current = call(
        peak,
        [(wide, F32)],
        (*sums, *top_pivots, *blocks["A", top]),
        (ids,),
        [pltpu.VMEM((leaves, *wide), F32)],
    )

    def ordered(own, refs, held):
        for offset, ref in enumerate(refs):
            held[own ^ offset] = ref[...]

    def against(held, high_ref, low_ref, span):
        value = times(held[0], high_ref[0], low_ref[0], 0)
        for slot in range(1, span):
            value = value + times(held[slot], high_ref[slot], low_ref[slot], 0)
        return value

    def descend(level, parts):
        span = 2**level

        def body(ids_ref, *refs):
            part_refs = refs[:span]
            high_ref, low_ref, solved_ref, pivot_ref, out, held = refs[span:]
            ordered(ids_ref[0] % span, part_refs, held)
            above = against(held, high_ref, low_ref, span)
            out[...] = solved_ref[...] / pivot_ref[...] - above

        return call(
            body,
            [(wide, F32)],
            (*parts, *blocks["B", level - 1], solved[level - 1], pivots[level - 1]),
            (ids,),
            [pltpu.VMEM((span, *wide), F32)],
        )

    def transposed(level, parts):
        span = 2**level

        def body(ids_ref, *refs):
            part_refs = refs[:span]
            high_ref, low_ref, out, held = refs[span:]
            ordered(ids_ref[0] % span, part_refs, held)
            out[...] = part_refs[0][...] + against(held, high_ref, low_ref, span)

        return call(
            body,
            [(wide, F32)],
            (*parts, *blocks["A", level]),
            (ids,),
            [pltpu.VMEM((span, *wide), F32)],
        )

    everything = {top: leaf_swaps(current * leaves)}
    for level in range(top, 1, -1):
        wanted = leaf_swaps(descend(level, everything[level]) * 2 ** (level - 1))
        everything[level - 1] = leaf_swaps(transposed(level - 1, wanted) * 2 ** (level - 1))

    def finish(ids_ref, known_ref, *refs):
        refs = list(refs)
        parts = {level: [refs.pop(0) for _ in range(2**level)] for level in range(1, levels)}
        link_high, link_low, solved_ref, pivot_ref, high_ref, low_ref = refs[:6]
        out, path, held = refs[6:]
        group = ids_ref[0]
        ordered(group % 2, parts[1], held)
        wanted = solved_ref[...] / pivot_ref[...] - against(held, link_high, link_low, 2)
        lowest = wanted + times(wanted, high_ref[0], low_ref[0], 0)
        owned = [lowest]
        for half in range(halves):
            path[half] = lowest[:, half * TILE : (half + 1) * TILE]
        for level in range(1, levels):
            span = 2**level
            owned.append(parts[level][0][...])
            for offset, ref in enumerate(parts[level]):
                first = (span - 1 + (group % span ^ offset)) * halves
                for half in range(halves):
                    path[first + half] = ref[:, half * TILE : (half + 1) * TILE]
        lane = lax.broadcasted_iota(jnp.int32, (share, TILE), 1)
        for target in range(ranks):
            for tile in range(tiles):
                out[target, :, tile * TILE : (tile + 1) * TILE] = path[
                    known_ref[target * tiles + tile]
                ]
            pieces = jnp.zeros((share, TILE), F32)
            for level in range(levels):
                shift = (base + level * piece - target * piece) % base
                turned = pltpu.roll(owned[level], shift, 1)[:, :TILE]
                mine = (lane >= level * piece) & (lane < (level + 1) * piece)
                pieces = jnp.where(mine, turned, pieces)
            out[target, :, tiles * TILE :] = pieces

    replies = call(
        finish,
        [((ranks, share, packed), F32)],
        (
            *[part for level in range(1, levels) for part in everything[level]],
            *blocks["B", 0],
            solved[0],
            pivots[0],
            *blocks["A", 0],
        ),
        (ids, known),
        [pltpu.VMEM((path_tiles, share, TILE), F32), pltpu.VMEM((2, *wide), F32)],
    )
    back = lax.all_to_all(replies[0], "row", 0, 0, tiled=True).reshape(columns, packed)

    def local_backward(back, solved_ref, pivot_ref, inverse_ref, coupling_ref, out, window_ref):
        remainder = solved_ref[...] / pivot_ref[...] - jnp.dot(
            back[:, : tiles * TILE], coupling_ref[...], precision=EXACT
        )
        answer = remainder + jnp.dot(
            remainder, strict_lower(inverse_ref[...]), precision=EXACT
        )
        out[...] = answer.T
        final = back[:, tiles * TILE :].T
        for level in range(levels):
            window_ref[level] = final[level * piece : (level + 1) * piece]

    answer, window = call(
        local_backward,
        [((local, columns), F32), ((levels, piece, columns), F32)],
        (back, solved_loc, loc_pivots[0], loc_inverse[0, 0], loc_coupling[0, 0]),
        work=24 * local * local * columns,
    )
    return answer[None, None], window


def solution(mesh):
    return jax.shard_map(
        shards,
        mesh=mesh,
        in_specs=(
            P("leaf", "row", None, None),
            P("leaf", "row", None, None),
            P("leaf", "row", None, None),
            P("leaf", "row", None),
            P("leaf", "row", None),
            P(None, ("leaf", "row"), None),
            P(None, ("leaf", "row")),
            P("row", None, "leaf"),
            P("row", None, "leaf"),
        ),
        out_specs=(P("leaf", "row", None, None), P(None, ("leaf", "row"), None)),
        check_vma=False,
    )
```

```python
import math

import jax
import jax.numpy as jnp
from jax import lax
from jax.experimental import pallas as pl
from jax.experimental.pallas import tpu as pltpu
from jax.sharding import PartitionSpec as P

TILE = 128
EXACT = lax.Precision.HIGHEST
F32 = jnp.float32
BF16 = jnp.bfloat16


def swap(value, axis, count, offset):
    return lax.ppermute(value, axis, [(i, i ^ offset) for i in range(count)])


def ring_order(count):
    return list(range(0, count, 2)) + list(range(count - 1, 0, -2))


def ring_gather(groups, count):
    order = ring_order(count)
    right = [(order[i], order[(i + 1) % count]) for i in range(count)]
    left = [(target, source) for source, target in right]
    parts = [[(0, block)] for block in groups]
    moving = [[block, block] for block in groups]
    for step in range(1, count // 2 + 1):
        for index in range(len(groups)):
            last = 2 * step == count
            if not last or index % 2 == 0:
                moving[index][0] = lax.ppermute(moving[index][0], "row", right)
                parts[index].append((-step, moving[index][0]))
            if not last or index % 2 == 1:
                moving[index][1] = lax.ppermute(moving[index][1], "row", left)
                parts[index].append((step, moving[index][1]))
    return parts


def call(body, outs, arrays, scalars=(), scratch=(), work=0, remote=0):
    moved = sum(a.size * a.dtype.itemsize for a in arrays)
    moved += sum(math.prod(shape) * jnp.dtype(kind).itemsize for shape, kind in outs)
    return pl.pallas_call(
        body,
        out_shape=[jax.ShapeDtypeStruct(*o) for o in outs],
        in_specs=[pl.BlockSpec(memory_space=pltpu.SMEM)] * len(scalars)
        + [pl.BlockSpec(memory_space=pltpu.VMEM)] * (len(arrays) - remote)
        + [pl.BlockSpec(memory_space=pl.ANY)] * remote,
        out_specs=[pl.BlockSpec(memory_space=pltpu.VMEM)] * len(outs),
        scratch_shapes=list(scratch),
        compiler_params=pltpu.CompilerParams(vmem_limit_bytes=40 << 20),
        cost_estimate=pl.CostEstimate(flops=work, bytes_accessed=moved, transcendentals=0),
    )(*scalars, *arrays)


def split(value):
    high = value.astype(BF16).astype(F32)
    return high, value - high


def times(value, high, low, right_dim):
    rows = value.shape[0]
    dims = (((1,), (right_dim,)), ((), ()))

    def product(part):
        return lax.dot_general(part, high, dims, preferred_element_type=F32) + lax.dot_general(
            part, low, dims, preferred_element_type=F32
        )

    first, second = split(value)
    if rows % 8:
        return product(first.astype(BF16)) + product(second.astype(BF16))
    both = product(jnp.concatenate([first, second], 0).astype(BF16))
    return both[:rows] + both[rows:]


def strict_lower(block):
    row_ids = lax.broadcasted_iota(jnp.int32, block.shape, 0)
    col_ids = lax.broadcasted_iota(jnp.int32, block.shape, 1)
    return jnp.where(col_ids < row_ids, block, 0.0)


def shards(
    loc_rhs,
    loc_inverse,
    loc_coupling,
    loc_pivots,
    pattern,
    win_rhs,
    win_pivots,
    win_inverse,
    win_coupling,
):
    leaves = lax.axis_size("leaf")
    ranks = lax.axis_size("row")
    leaf = lax.axis_index("leaf")
    rank = lax.axis_index("row")
    levels, piece, columns = win_rhs.shape
    base = piece * ranks
    share = columns // ranks
    halves = base // TILE
    path_tiles = (2 * leaves - 1) * halves
    tiles = pattern.shape[2]
    local = loc_rhs.shape[2]
    top = levels - 1
    ids = jnp.stack([leaf, rank]).astype(jnp.int32)
    wide = (share, base)

    def leaf_swaps(values):
        return [values[0]] + [swap(v, "leaf", leaves, j) for j, v in enumerate(values) if j]

    def source_row(me, step):
        place = jnp.where(me % 2 == 0, me // 2, ranks - 1 - me // 2)
        place = (place + step + ranks) % ranks
        return jnp.where(2 * place < ranks, 2 * place, 2 * (ranks - 1 - place) + 1)

    def assemble(parts, names):
        spans = [2**level if kind == "A" else 2 ** (level + 1) for kind, level in names]
        steps = [step for step, _ in parts]
        parts = [part for _, part in parts]

        def body(ids_ref, *refs):
            parts_refs, outs = refs[:ranks], refs[ranks:-2]
            natural, done = refs[-2:]
            group = ids_ref[0]
            copies = []
            for index, ref in enumerate(parts_refs):
                start = pl.multiple_of(source_row(ids_ref[1], steps[index]) * piece, 8)
                copies.append(
                    pltpu.make_async_copy(
                        ref, natural.at[:, pl.ds(start, piece), :], done.at[index]
                    )
                )
            for copy in copies:
                copy.start()
            for copy in copies:
                copy.wait()
            first = 0
            for index, ((kind, level), span) in enumerate(zip(names, spans)):
                for slot in range(span):
                    block = natural[first + slot]
                    if kind == "A":
                        row_ids = lax.broadcasted_iota(jnp.int32, block.shape, 0) + slot * base
                        col_ids = lax.broadcasted_iota(jnp.int32, block.shape, 1)
                        col_ids = col_ids + group % span * base
                        block = jnp.where(col_ids < row_ids, block, 0.0)
                    high, low = split(block)
                    outs[2 * index][slot] = high.astype(BF16)
                    outs[2 * index + 1][slot] = low.astype(BF16)
                first += span

        outs = [((span, base, base), BF16) for span in spans for _ in range(2)]
        made = call(
            body,
            outs,
            parts,
            (ids,),
            [pltpu.VMEM((sum(spans), base, base), F32), pltpu.SemaphoreType.DMA((ranks,))],
            remote=ranks,
        )
        return {name: made[2 * i : 2 * i + 2] for i, name in enumerate(names)}

    lower_names = [("A", level) for level in range(top)]
    lower_names += [("B", level) for level in range(top)]
    upper_names = [("A", top)]
    below = (2**top - 1) * piece
    own_blocks = [
        jnp.concatenate([win_inverse[0, :below], win_coupling[0]], 0).reshape(-1, piece, base),
        win_inverse[0, below:].reshape(-1, piece, base),
    ]
    lower_parts, upper_parts = ring_gather(own_blocks, ranks)

    narrow = TILE - levels * piece
    aux = jnp.concatenate([win_pivots.reshape(-1), pattern[0, 0].astype(F32)])
    aux = jnp.pad(aux, (0, share * narrow - aux.size)).reshape(share, narrow)
    aux = jnp.tile(jnp.pad(aux, ((0, 0), (levels * piece, 0))), (ranks, 1))
    packed = tiles * TILE + TILE

    def local_forward(rhs_ref, inverse_ref, coupling_ref, window_ref, aux_ref, *outs):
        solved_ref, terms_ref, held = outs[1:]
        rhs = rhs_ref[...]
        solved = rhs + jnp.dot(strict_lower(inverse_ref[...]), rhs, precision=EXACT)
        solved_ref[...] = solved.T
        terms_ref[:, : tiles * TILE] = jnp.dot(coupling_ref[...], solved, precision=EXACT).T
        held[...] = jnp.zeros_like(held)
        for level in range(levels):
            held[level * piece : (level + 1) * piece, :] = window_ref[level]
        terms_ref[:, tiles * TILE :] = held[...].T + aux_ref[...]

    solved_loc, terms = call(
        local_forward,
        [((columns, local), F32), ((columns, packed), F32)],
        (loc_rhs[0, 0], loc_inverse[0, 0], loc_coupling[0, 0], win_rhs, aux, lower_parts[1][1]),
        remote=1,
        scratch=[pltpu.VMEM((TILE, columns), F32)],
        work=24 * local * local * columns,
    )
    terms = lax.all_to_all(terms.reshape(ranks, share, packed), "row", 0, 0, tiled=True)
    aux = terms[:, :, tiles * TILE + levels * piece :].reshape(ranks, -1)
    known = aux[:, levels * piece : levels * piece + tiles].astype(jnp.int32).reshape(-1)
    pivots = aux[:, : levels * piece].reshape(ranks, levels, piece)
    pivots = pivots.transpose(1, 0, 2).reshape(levels, 1, base)
    top_pivots = leaf_swaps([pivots[top]] * leaves)

    lower = assemble(lower_parts, lower_names)
    upper = assemble(upper_parts, upper_names)
    blocks = {**lower, **upper}

    def scatter(ids_ref, known_ref, terms_ref, *refs):
        outs, path = refs[:-1], refs[-1]
        lane = lax.broadcasted_iota(jnp.int32, (share, TILE), 1)
        path[...] = jnp.zeros_like(path)
        for source in range(ranks):
            for tile in range(tiles):
                place = known_ref[source * tiles + tile]
                path[place] = path[place] - terms_ref[source, :, tile * TILE : (tile + 1) * TILE]
        for level in range(levels):
            span = 2**level
            for slot in range(span):
                first = (span - 1 + slot) * halves
                outs[level][slot] = jnp.concatenate([path[first + h] for h in range(halves)], 1)
            own = ids_ref[0] % span
            rows = []
            for half in range(halves):
                row = jnp.zeros((share, TILE), F32)
                for source in range(half * TILE // piece, (half + 1) * TILE // piece):
                    place = source * piece % TILE
                    shift = (TILE + place - level * piece) % TILE
                    turned = pltpu.roll(terms_ref[source, :, tiles * TILE :], shift, 1)
                    row = jnp.where((lane >= place) & (lane < place + piece), turned, row)
                rows.append(row)
            outs[level][own] = outs[level][own] + jnp.concatenate(rows, 1)

    rest = call(
        scatter,
        [((2**level, *wide), F32) for level in range(levels)],
        (terms,),
        (ids, known),
        [pltpu.VMEM((path_tiles, share, TILE), F32)],
    )

    def total(refs):
        value = refs[0][...]
        for ref in refs[1:]:
            value = value + ref[...]
        return value

    def diagonal(level, chunks):
        span = 2**level
        high, low = blocks["A", level]

        def body(ids_ref, *refs):
            chunk_refs, (high_ref, low_ref) = refs[:span], refs[span : span + 2]
            outs, parts = refs[span + 2 : -1], refs[-1]
            own = ids_ref[0] % span
            value = total(chunk_refs)
            for slot in range(span):
                parts[slot] = times(value, high_ref[slot], low_ref[slot], 1)
            parts[own] = parts[own] + value
            if level == top:
                outs[0][...] = parts[...]
            else:
                for offset, out in enumerate(outs):
                    out[...] = parts[own ^ offset]

        outs = [((span, *wide), F32)] if level == top else [(wide, F32)] * span
        return call(
            body, outs, (*chunks, high, low), (ids,), [pltpu.VMEM((span, *wide), F32)]
        )

    def link(level, chunks):
        span, above = 2**level, 2 ** (level + 1)
        high, low = blocks["B", level]

        def body(ids_ref, *refs):
            chunk_refs = refs[:span]
            high_ref, low_ref, rest_ref, solved_ref = refs[span : span + 4]
            outs, parts = refs[span + 4 : -1], refs[-1]
            value = total(chunk_refs)
            solved_ref[...] = value
            for slot in range(above):
                parts[slot] = rest_ref[slot] - times(value, high_ref[slot], low_ref[slot], 1)
            own = ids_ref[0] % above
            for offset, out in enumerate(outs):
                out[...] = parts[own ^ offset]

        made = call(
            body,
            [(wide, F32)] * (above + 1),
            (*chunks, high, low, rest[level + 1]),
            (ids,),
            [pltpu.VMEM((above, *wide), F32)],
        )
        return made[0], made[1:]

    chunks = [rest[0][0]]
    solved = []
    for level in range(top):
        chunks = leaf_swaps(diagonal(level, chunks))
        value, chunks = link(level, chunks)
        solved.append(value)
        chunks = leaf_swaps(chunks)
    sums = leaf_swaps(diagonal(top, chunks) * leaves)

    def peak(ids_ref, *refs):
        sum_refs, pivot_refs = refs[:leaves], refs[leaves : 2 * leaves]
        high_ref, low_ref, out, wanted = refs[2 * leaves :]
        own = ids_ref[0] % leaves
        wanted[...] = total(sum_refs)
        for offset, ref in enumerate(pivot_refs):
            wanted[own ^ offset] = wanted[own ^ offset] / ref[...]
        value = wanted[own]
        for slot in range(leaves):
            value = value + times(wanted[slot], high_ref[slot], low_ref[slot], 0)
        out[...] = value

    current = call(
        peak,
        [(wide, F32)],
        (*sums, *top_pivots, *blocks["A", top]),
        (ids,),
        [pltpu.VMEM((leaves, *wide), F32)],
    )

    def ordered(own, refs, held):
        for offset, ref in enumerate(refs):
            held[own ^ offset] = ref[...]

    def against(held, high_ref, low_ref, span):
        value = times(held[0], high_ref[0], low_ref[0], 0)
        for slot in range(1, span):
            value = value + times(held[slot], high_ref[slot], low_ref[slot], 0)
        return value

    def descend(level, parts):
        span = 2**level

        def body(ids_ref, *refs):
            part_refs = refs[:span]
            high_ref, low_ref, solved_ref, pivot_ref, out, held = refs[span:]
            ordered(ids_ref[0] % span, part_refs, held)
            above = against(held, high_ref, low_ref, span)
            out[...] = solved_ref[...] / pivot_ref[...] - above

        return call(
            body,
            [(wide, F32)],
            (*parts, *blocks["B", level - 1], solved[level - 1], pivots[level - 1]),
            (ids,),
            [pltpu.VMEM((span, *wide), F32)],
        )

    def transposed(level, parts):
        span = 2**level

        def body(ids_ref, *refs):
            part_refs = refs[:span]
            high_ref, low_ref, out, held = refs[span:]
            ordered(ids_ref[0] % span, part_refs, held)
            out[...] = part_refs[0][...] + against(held, high_ref, low_ref, span)

        return call(
            body,
            [(wide, F32)],
            (*parts, *blocks["A", level]),
            (ids,),
            [pltpu.VMEM((span, *wide), F32)],
        )

    everything = {top: leaf_swaps(current * leaves)}
    for level in range(top, 1, -1):
        wanted = leaf_swaps(descend(level, everything[level]) * 2 ** (level - 1))
        everything[level - 1] = leaf_swaps(transposed(level - 1, wanted) * 2 ** (level - 1))

    def finish(ids_ref, known_ref, *refs):
        refs = list(refs)
        parts = {level: [refs.pop(0) for _ in range(2**level)] for level in range(1, levels)}
        link_high, link_low, solved_ref, pivot_ref, high_ref, low_ref = refs[:6]
        out, path, held = refs[6:]
        group = ids_ref[0]
        ordered(group % 2, parts[1], held)
        wanted = solved_ref[...] / pivot_ref[...] - against(held, link_high, link_low, 2)
        lowest = wanted + times(wanted, high_ref[0], low_ref[0], 0)
        owned = [lowest]
        for half in range(halves):
            path[half] = lowest[:, half * TILE : (half + 1) * TILE]
        for level in range(1, levels):
            span = 2**level
            owned.append(parts[level][0][...])
            for offset, ref in enumerate(parts[level]):
                first = (span - 1 + (group % span ^ offset)) * halves
                for half in range(halves):
                    path[first + half] = ref[:, half * TILE : (half + 1) * TILE]
        lane = lax.broadcasted_iota(jnp.int32, (share, TILE), 1)
        for target in range(ranks):
            for tile in range(tiles):
                out[target, :, tile * TILE : (tile + 1) * TILE] = path[
                    known_ref[target * tiles + tile]
                ]
            pieces = jnp.zeros((share, TILE), F32)
            for level in range(levels):
                shift = (base + level * piece - target * piece) % base
                turned = pltpu.roll(owned[level], shift, 1)[:, :TILE]
                mine = (lane >= level * piece) & (lane < (level + 1) * piece)
                pieces = jnp.where(mine, turned, pieces)
            out[target, :, tiles * TILE :] = pieces

    replies = call(
        finish,
        [((ranks, share, packed), F32)],
        (
            *[part for level in range(1, levels) for part in everything[level]],
            *blocks["B", 0],
            solved[0],
            pivots[0],
            *blocks["A", 0],
        ),
        (ids, known),
        [pltpu.VMEM((path_tiles, share, TILE), F32), pltpu.VMEM((2, *wide), F32)],
    )
    back = lax.all_to_all(replies[0], "row", 0, 0, tiled=True).reshape(columns, packed)

    def local_backward(back, solved_ref, pivot_ref, inverse_any, coupling_any, *refs):
        out, window_ref, inverse_ref, coupling_ref, done = refs
        first = pltpu.make_async_copy(coupling_any, coupling_ref, done.at[0])
        second = pltpu.make_async_copy(inverse_any, inverse_ref, done.at[1])
        first.start()
        second.start()
        final = back[:, tiles * TILE :].T
        for level in range(levels):
            window_ref[level] = final[level * piece : (level + 1) * piece]
        first.wait()
        remainder = solved_ref[...] / pivot_ref[...] - jnp.dot(
            back[:, : tiles * TILE], coupling_ref[...], precision=EXACT
        )
        second.wait()
        answer = remainder + jnp.dot(
            remainder, strict_lower(inverse_ref[...]), precision=EXACT
        )
        out[...] = answer.T

    answer, window = call(
        local_backward,
        [((local, columns), F32), ((levels, piece, columns), F32)],
        (back, solved_loc, loc_pivots[0], loc_inverse[0, 0], loc_coupling[0, 0]),
        scratch=[
            pltpu.VMEM((local, local), F32),
            pltpu.VMEM((tiles * TILE, local), F32),
            pltpu.SemaphoreType.DMA((2,)),
        ],
        remote=2,
        work=24 * local * local * columns,
    )
    return answer[None, None], window


def solution(mesh):
    return jax.shard_map(
        shards,
        mesh=mesh,
        in_specs=(
            P("leaf", "row", None, None),
            P("leaf", "row", None, None),
            P("leaf", "row", None, None),
            P("leaf", "row", None),
            P("leaf", "row", None),
            P(None, ("leaf", "row"), None),
            P(None, ("leaf", "row")),
            P("row", None, "leaf"),
            P("row", None, "leaf"),
        ),
        out_specs=(P("leaf", "row", None, None), P(None, ("leaf", "row"), None)),
        check_vma=False,
    )
```

```python
import math

import jax
import jax.numpy as jnp
from jax import lax
from jax.experimental import pallas as pl
from jax.experimental.pallas import tpu as pltpu
from jax.sharding import PartitionSpec as P

TILE = 128
EXACT = lax.Precision.HIGHEST
F32 = jnp.float32
BF16 = jnp.bfloat16


def swap(value, axis, count, offset):
    return lax.ppermute(value, axis, [(i, i ^ offset) for i in range(count)])


def ring_order(count):
    return list(range(0, count, 2)) + list(range(count - 1, 0, -2))


def ring_gather(groups, count):
    order = ring_order(count)
    right = [(order[i], order[(i + 1) % count]) for i in range(count)]
    left = [(target, source) for source, target in right]
    parts = [[(0, block)] for block in groups]
    moving = [[block, block] for block in groups]
    for step in range(1, count // 2 + 1):
        for index in range(len(groups)):
            last = 2 * step == count
            if not last or index % 2 == 0:
                moving[index][0] = lax.ppermute(moving[index][0], "row", right)
                parts[index].append((-step, moving[index][0]))
            if not last or index % 2 == 1:
                moving[index][1] = lax.ppermute(moving[index][1], "row", left)
                parts[index].append((step, moving[index][1]))
    return parts


def call(body, outs, arrays, scalars=(), scratch=(), work=0, remote=0, room=40):
    moved = sum(a.size * a.dtype.itemsize for a in arrays)
    moved += sum(math.prod(shape) * jnp.dtype(kind).itemsize for shape, kind in outs)
    return pl.pallas_call(
        body,
        out_shape=[jax.ShapeDtypeStruct(*o) for o in outs],
        in_specs=[pl.BlockSpec(memory_space=pltpu.SMEM)] * len(scalars)
        + [pl.BlockSpec(memory_space=pltpu.VMEM)] * (len(arrays) - remote)
        + [pl.BlockSpec(memory_space=pltpu.HBM)] * remote,
        out_specs=[pl.BlockSpec(memory_space=pltpu.VMEM)] * len(outs),
        scratch_shapes=list(scratch),
        compiler_params=pltpu.CompilerParams(vmem_limit_bytes=room << 20),
        cost_estimate=pl.CostEstimate(flops=work, bytes_accessed=moved, transcendentals=0),
    )(*scalars, *arrays)


def split(value):
    high = value.astype(BF16).astype(F32)
    return high, value - high


def times(value, high, low, right_dim):
    rows = value.shape[0]
    dims = (((1,), (right_dim,)), ((), ()))

    def product(part):
        return lax.dot_general(part, high, dims, preferred_element_type=F32) + lax.dot_general(
            part, low, dims, preferred_element_type=F32
        )

    first, second = split(value)
    if rows % 8:
        return product(first.astype(BF16)) + product(second.astype(BF16))
    both = product(jnp.concatenate([first, second], 0).astype(BF16))
    return both[:rows] + both[rows:]


def strict_lower(block):
    row_ids = lax.broadcasted_iota(jnp.int32, block.shape, 0)
    col_ids = lax.broadcasted_iota(jnp.int32, block.shape, 1)
    return jnp.where(col_ids < row_ids, block, 0.0)


def shards(
    loc_rhs,
    loc_inverse,
    loc_coupling,
    loc_pivots,
    pattern,
    win_rhs,
    win_pivots,
    win_inverse,
    win_coupling,
):
    leaves = lax.axis_size("leaf")
    ranks = lax.axis_size("row")
    leaf = lax.axis_index("leaf")
    rank = lax.axis_index("row")
    levels, piece, columns = win_rhs.shape
    base = piece * ranks
    share = columns // ranks
    halves = base // TILE
    path_tiles = (2 * leaves - 1) * halves
    tiles = pattern.shape[2]
    local = loc_rhs.shape[2]
    top = levels - 1
    ids = jnp.stack([leaf, rank]).astype(jnp.int32)
    wide = (share, base)

    def leaf_swaps(values):
        return [values[0]] + [swap(v, "leaf", leaves, j) for j, v in enumerate(values) if j]

    def source_row(me, step):
        place = jnp.where(me % 2 == 0, me // 2, ranks - 1 - me // 2)
        place = (place + step + ranks) % ranks
        return jnp.where(2 * place < ranks, 2 * place, 2 * (ranks - 1 - place) + 1)

    def assemble(parts, names):
        spans = [2**level if kind == "A" else 2 ** (level + 1) for kind, level in names]
        steps = [step for step, _ in parts]
        parts = [part for _, part in parts]

        def body(ids_ref, *refs):
            parts_refs, outs = refs[:ranks], refs[ranks:-2]
            natural, done = refs[-2:]
            group = ids_ref[0]
            copies = []
            for index, ref in enumerate(parts_refs):
                start = pl.multiple_of(source_row(ids_ref[1], steps[index]) * piece, 8)
                copies.append(
                    pltpu.make_async_copy(
                        ref, natural.at[:, pl.ds(start, piece), :], done.at[index]
                    )
                )
            for copy in copies:
                copy.start()
            for copy in copies:
                copy.wait()
            first = 0
            for index, ((kind, level), span) in enumerate(zip(names, spans)):
                for slot in range(span):
                    block = natural[first + slot]
                    if kind == "A":
                        row_ids = lax.broadcasted_iota(jnp.int32, block.shape, 0) + slot * base
                        col_ids = lax.broadcasted_iota(jnp.int32, block.shape, 1)
                        col_ids = col_ids + group % span * base
                        block = jnp.where(col_ids < row_ids, block, 0.0)
                    high, low = split(block)
                    outs[2 * index][slot] = high.astype(BF16)
                    outs[2 * index + 1][slot] = low.astype(BF16)
                first += span

        outs = [((span, base, base), BF16) for span in spans for _ in range(2)]
        made = call(
            body,
            outs,
            parts,
            (ids,),
            [pltpu.VMEM((sum(spans), base, base), F32), pltpu.SemaphoreType.DMA((ranks,))],
            remote=ranks,
        )
        return {name: made[2 * i : 2 * i + 2] for i, name in enumerate(names)}

    lower_names = [("A", level) for level in range(top)]
    lower_names += [("B", level) for level in range(top)]
    upper_names = [("A", top)]
    below = (2**top - 1) * piece
    own_blocks = [
        jnp.concatenate([win_inverse[0, :below], win_coupling[0]], 0).reshape(-1, piece, base),
        win_inverse[0, below:].reshape(-1, piece, base),
    ]
    lower_parts, upper_parts = ring_gather(own_blocks, ranks)

    narrow = TILE - levels * piece
    aux = jnp.concatenate([win_pivots.reshape(-1), pattern[0, 0].astype(F32)])
    aux = jnp.pad(aux, (0, share * narrow - aux.size)).reshape(share, narrow)
    aux = jnp.tile(jnp.pad(aux, ((0, 0), (levels * piece, 0))), (ranks, 1))
    packed = tiles * TILE + TILE

    firsts = [part for parts in (lower_parts, upper_parts) for step, part in parts if step in (1, -1)]

    def local_forward(rhs_ref, window_ref, aux_ref, inverse_any, coupling_any, *refs):
        solved_ref, terms_ref, held, inverse_ref, coupling_ref, done = refs[len(firsts) :]
        first = pltpu.make_async_copy(inverse_any, inverse_ref, done.at[0])
        second = pltpu.make_async_copy(coupling_any, coupling_ref, done.at[1])
        first.start()
        second.start()
        rhs = rhs_ref[...]
        held[...] = jnp.zeros_like(held)
        for level in range(levels):
            held[level * piece : (level + 1) * piece, :] = window_ref[level]
        terms_ref[:, tiles * TILE :] = held[...].T + aux_ref[...]
        first.wait()
        solved = rhs + jnp.dot(strict_lower(inverse_ref[...]), rhs, precision=EXACT)
        solved_ref[...] = solved.T
        second.wait()
        terms_ref[:, : tiles * TILE] = jnp.dot(coupling_ref[...], solved, precision=EXACT).T

    solved_loc, terms = call(
        local_forward,
        [((columns, local), F32), ((columns, packed), F32)],
        (loc_rhs[0, 0], win_rhs, aux, loc_inverse[0, 0], loc_coupling[0, 0], *firsts),
        remote=2 + len(firsts),
        scratch=[
            pltpu.VMEM((TILE, columns), F32),
            pltpu.VMEM((local, local), F32),
            pltpu.VMEM((tiles * TILE, local), F32),
            pltpu.SemaphoreType.DMA((2,)),
        ],
        work=24 * local * local * columns,
        room=60,
    )
    terms = lax.all_to_all(terms.reshape(ranks, share, packed), "row", 0, 0, tiled=True)
    aux = terms[:, :, tiles * TILE + levels * piece :].reshape(ranks, -1)
    known = aux[:, levels * piece : levels * piece + tiles].astype(jnp.int32).reshape(-1)
    pivots = aux[:, : levels * piece].reshape(ranks, levels, piece)
    pivots = pivots.transpose(1, 0, 2).reshape(levels, 1, base)
    all_pivots = leaf_swaps([pivots] * leaves)

    lower = assemble(lower_parts, lower_names)
    upper = assemble(upper_parts, upper_names)
    blocks = {**lower, **upper}

    def scatter(ids_ref, known_ref, terms_ref, *refs):
        outs, path = refs[:-1], refs[-1]
        lane = lax.broadcasted_iota(jnp.int32, (share, TILE), 1)
        path[...] = jnp.zeros_like(path)
        for source in range(ranks):
            for tile in range(tiles):
                place = known_ref[source * tiles + tile]
                path[place] = path[place] - terms_ref[source, :, tile * TILE : (tile + 1) * TILE]
        for level in range(levels):
            span = 2**level
            filled = outs[level]
            for slot in range(span):
                first = (span - 1 + slot) * halves
                for half in range(halves):
                    filled[slot, :, half * TILE : (half + 1) * TILE] = path[first + half]
            own = ids_ref[0] % span
            rows = []
            for half in range(halves):
                row = jnp.zeros((share, TILE), F32)
                for source in range(half * TILE // piece, (half + 1) * TILE // piece):
                    place = source * piece % TILE
                    shift = (TILE + place - level * piece) % TILE
                    turned = pltpu.roll(terms_ref[source, :, tiles * TILE :], shift, 1)
                    row = jnp.where((lane >= place) & (lane < place + piece), turned, row)
                rows.append(row)
            filled[own] = filled[own] + jnp.concatenate(rows, 1)

    rest = call(
        scatter,
        [((2**level, *wide), F32) for level in range(levels)],
        (terms,),
        (ids, known),
        [pltpu.VMEM((path_tiles, share, TILE), F32)],
    )

    def total(refs):
        value = refs[0][0] if len(refs[0].shape) > len(wide) and len(refs) == 1 else refs[0][...]
        for ref in refs[1:]:
            value = value + ref[...]
        return value

    def diagonal(level, chunks, ahead=()):
        span = 2**level
        high, low = blocks["A", level]

        def body(ids_ref, *refs):
            chunk_refs, (high_ref, low_ref) = refs[:span], refs[span : span + 2]
            outs, parts = refs[span + 2 + len(ahead) : -1], refs[-1]
            own = ids_ref[0] % span
            value = total(chunk_refs)
            for slot in range(span):
                parts[slot] = times(value, high_ref[slot], low_ref[slot], 1)
            parts[own] = parts[own] + value
            if level == top:
                outs[0][...] = parts[...]
            else:
                for offset, out in enumerate(outs):
                    out[...] = parts[own ^ offset]

        outs = [((span, *wide), F32)] if level == top else [(wide, F32)] * span
        return call(
            body,
            outs,
            (*chunks, high, low, *ahead),
            (ids,),
            [pltpu.VMEM((span, *wide), F32)],
        )

    def link(level, chunks):
        span, above = 2**level, 2 ** (level + 1)
        high, low = blocks["B", level]

        def body(ids_ref, *refs):
            chunk_refs = refs[:span]
            high_ref, low_ref, rest_ref, solved_ref = refs[span : span + 4]
            outs, parts = refs[span + 4 : -1], refs[-1]
            value = total(chunk_refs)
            solved_ref[...] = value
            for slot in range(above):
                parts[slot] = rest_ref[slot] - times(value, high_ref[slot], low_ref[slot], 1)
            own = ids_ref[0] % above
            for offset, out in enumerate(outs):
                out[...] = parts[own ^ offset]

        made = call(
            body,
            [(wide, F32)] * (above + 1),
            (*chunks, high, low, rest[level + 1]),
            (ids,),
            [pltpu.VMEM((above, *wide), F32)],
        )
        return made[0], made[1:]

    chunks = [rest[0]]
    solved = []
    for level in range(top):
        chunks = leaf_swaps(diagonal(level, chunks, () if level else all_pivots))
        value, chunks = link(level, chunks)
        solved.append(value)
        chunks = leaf_swaps(chunks)
    sums = leaf_swaps(diagonal(top, chunks) * leaves)

    def peak(ids_ref, *refs):
        sum_refs, pivot_refs = refs[:leaves], refs[leaves : 2 * leaves]
        high_ref, low_ref, out, wanted = refs[2 * leaves :]
        own = ids_ref[0] % leaves
        wanted[...] = total(sum_refs)
        for offset, ref in enumerate(pivot_refs):
            wanted[own ^ offset] = wanted[own ^ offset] / ref[top]
        value = wanted[own]
        for slot in range(leaves):
            value = value + times(wanted[slot], high_ref[slot], low_ref[slot], 0)
        out[...] = value

    current = call(
        peak,
        [(wide, F32)],
        (*sums, *all_pivots, *blocks["A", top]),
        (ids,),
        [pltpu.VMEM((leaves, *wide), F32)],
    )

    def ordered(own, refs, held):
        for offset, ref in enumerate(refs):
            held[own ^ offset] = ref[...]

    def against(held, high_ref, low_ref, span):
        value = times(held[0], high_ref[0], low_ref[0], 0)
        for slot in range(1, span):
            value = value + times(held[slot], high_ref[slot], low_ref[slot], 0)
        return value

    def descend(level, parts):
        span = 2**level

        def body(ids_ref, *refs):
            part_refs = refs[:span]
            high_ref, low_ref, solved_ref, pivot_ref, out, held = refs[span:]
            ordered(ids_ref[0] % span, part_refs, held)
            above = against(held, high_ref, low_ref, span)
            out[...] = solved_ref[...] / pivot_ref[level - 1] - above

        return call(
            body,
            [(wide, F32)],
            (*parts, *blocks["B", level - 1], solved[level - 1], pivots),
            (ids,),
            [pltpu.VMEM((span, *wide), F32)],
        )

    def transposed(level, parts):
        span = 2**level

        def body(ids_ref, *refs):
            part_refs = refs[:span]
            high_ref, low_ref, out, held = refs[span:]
            ordered(ids_ref[0] % span, part_refs, held)
            out[...] = part_refs[0][...] + against(held, high_ref, low_ref, span)

        return call(
            body,
            [(wide, F32)],
            (*parts, *blocks["A", level]),
            (ids,),
            [pltpu.VMEM((span, *wide), F32)],
        )

    everything = {top: leaf_swaps(current * leaves)}
    for level in range(top, 1, -1):
        wanted = leaf_swaps(descend(level, everything[level]) * 2 ** (level - 1))
        everything[level - 1] = leaf_swaps(transposed(level - 1, wanted) * 2 ** (level - 1))

    def finish(ids_ref, known_ref, *refs):
        refs = list(refs)
        parts = {level: [refs.pop(0) for _ in range(2**level)] for level in range(1, levels)}
        link_high, link_low, solved_ref, pivot_ref, high_ref, low_ref = refs[:6]
        out, path, held = refs[6:]
        group = ids_ref[0]
        ordered(group % 2, parts[1], held)
        wanted = solved_ref[...] / pivot_ref[0] - against(held, link_high, link_low, 2)
        lowest = wanted + times(wanted, high_ref[0], low_ref[0], 0)
        owned = [lowest]
        for half in range(halves):
            path[half] = lowest[:, half * TILE : (half + 1) * TILE]
        for level in range(1, levels):
            span = 2**level
            owned.append(parts[level][0][...])
            for offset, ref in enumerate(parts[level]):
                first = (span - 1 + (group % span ^ offset)) * halves
                for half in range(halves):
                    path[first + half] = ref[:, half * TILE : (half + 1) * TILE]
        lane = lax.broadcasted_iota(jnp.int32, (share, TILE), 1)
        for target in range(ranks):
            for tile in range(tiles):
                out[target, :, tile * TILE : (tile + 1) * TILE] = path[
                    known_ref[target * tiles + tile]
                ]
            pieces = jnp.zeros((share, TILE), F32)
            for level in range(levels):
                shift = (base + level * piece - target * piece) % base
                turned = pltpu.roll(owned[level], shift, 1)[:, :TILE]
                mine = (lane >= level * piece) & (lane < (level + 1) * piece)
                pieces = jnp.where(mine, turned, pieces)
            out[target, :, tiles * TILE :] = pieces

    replies = call(
        finish,
        [((ranks, share, packed), F32)],
        (
            *[part for level in range(1, levels) for part in everything[level]],
            *blocks["B", 0],
            solved[0],
            pivots,
            *blocks["A", 0],
        ),
        (ids, known),
        [pltpu.VMEM((path_tiles, share, TILE), F32), pltpu.VMEM((2, *wide), F32)],
    )
    back = lax.all_to_all(replies[0], "row", 0, 0, tiled=True).reshape(columns, packed)

    def local_backward(back, solved_ref, pivot_ref, inverse_any, coupling_any, *refs):
        out, window_ref, inverse_ref, coupling_ref, done = refs
        first = pltpu.make_async_copy(coupling_any, coupling_ref, done.at[0])
        second = pltpu.make_async_copy(inverse_any, inverse_ref, done.at[1])
        first.start()
        second.start()
        final = back[:, tiles * TILE :].T
        for level in range(levels):
            window_ref[level] = final[level * piece : (level + 1) * piece]
        first.wait()
        remainder = solved_ref[...] / pivot_ref[...] - jnp.dot(
            back[:, : tiles * TILE], coupling_ref[...], precision=EXACT
        )
        second.wait()
        answer = remainder + jnp.dot(
            remainder, strict_lower(inverse_ref[...]), precision=EXACT
        )
        out[...] = answer.T

    answer, window = call(
        local_backward,
        [((local, columns), F32), ((levels, piece, columns), F32)],
        (back, solved_loc, loc_pivots[0], loc_inverse[0, 0], loc_coupling[0, 0]),
        scratch=[
            pltpu.VMEM((local, local), F32),
            pltpu.VMEM((tiles * TILE, local), F32),
            pltpu.SemaphoreType.DMA((2,)),
        ],
        remote=2,
        work=24 * local * local * columns,
        room=60,
    )
    return answer[None, None], window


def solution(mesh):
    return jax.shard_map(
        shards,
        mesh=mesh,
        in_specs=(
            P("leaf", "row", None, None),
            P("leaf", "row", None, None),
            P("leaf", "row", None, None),
            P("leaf", "row", None),
            P("leaf", "row", None),
            P(None, ("leaf", "row"), None),
            P(None, ("leaf", "row")),
            P("row", None, "leaf"),
            P("row", None, "leaf"),
        ),
        out_specs=(P("leaf", "row", None, None), P(None, ("leaf", "row"), None)),
        check_vma=False,
    )
```

```python
import math

import jax
import jax.numpy as jnp
from jax import lax
from jax.experimental import pallas as pl
from jax.experimental.pallas import tpu as pltpu
from jax.sharding import PartitionSpec as P

TILE = 128
EXACT = lax.Precision.HIGHEST
F32 = jnp.float32
BF16 = jnp.bfloat16


def swap(value, axis, count, offset):
    return lax.ppermute(value, axis, [(i, i ^ offset) for i in range(count)])


def ring_order(count):
    return list(range(0, count, 2)) + list(range(count - 1, 0, -2))


def ring_gather(groups, count):
    order = ring_order(count)
    right = [(order[i], order[(i + 1) % count]) for i in range(count)]
    left = [(target, source) for source, target in right]
    parts = [[(0, block)] for block in groups]
    moving = [[block, block] for block in groups]
    for step in range(1, count // 2 + 1):
        for index in range(len(groups)):
            last = 2 * step == count
            if not last or index % 2 == 0:
                moving[index][0] = lax.ppermute(moving[index][0], "row", right)
                parts[index].append((-step, moving[index][0]))
            if not last or index % 2 == 1:
                moving[index][1] = lax.ppermute(moving[index][1], "row", left)
                parts[index].append((step, moving[index][1]))
    return parts


def call(body, outs, arrays, scalars=(), scratch=(), work=0, remote=0, room=16):
    moved = sum(a.size * a.dtype.itemsize for a in arrays)
    moved += sum(math.prod(shape) * jnp.dtype(kind).itemsize for shape, kind in outs)
    return pl.pallas_call(
        body,
        out_shape=[jax.ShapeDtypeStruct(*o) for o in outs],
        in_specs=[pl.BlockSpec(memory_space=pltpu.SMEM)] * len(scalars)
        + [pl.BlockSpec(memory_space=pltpu.VMEM)] * (len(arrays) - remote)
        + [pl.BlockSpec(memory_space=pltpu.HBM)] * remote,
        out_specs=[pl.BlockSpec(memory_space=pltpu.VMEM)] * len(outs),
        scratch_shapes=list(scratch),
        compiler_params=pltpu.CompilerParams(vmem_limit_bytes=room << 20),
        cost_estimate=pl.CostEstimate(flops=work, bytes_accessed=moved, transcendentals=0),
    )(*scalars, *arrays)


def split(value):
    high = value.astype(BF16).astype(F32)
    return high, value - high


def times(value, high, low, right_dim):
    rows = value.shape[0]
    dims = (((1,), (right_dim,)), ((), ()))

    def product(part):
        return lax.dot_general(part, high, dims, preferred_element_type=F32) + lax.dot_general(
            part, low, dims, preferred_element_type=F32
        )

    first, second = split(value)
    if rows % 8:
        return product(first.astype(BF16)) + product(second.astype(BF16))
    both = product(jnp.concatenate([first, second], 0).astype(BF16))
    return both[:rows] + both[rows:]


def strict_lower(block):
    row_ids = lax.broadcasted_iota(jnp.int32, block.shape, 0)
    col_ids = lax.broadcasted_iota(jnp.int32, block.shape, 1)
    return jnp.where(col_ids < row_ids, block, 0.0)


def shards(
    loc_rhs,
    loc_inverse,
    loc_coupling,
    loc_pivots,
    pattern,
    win_rhs,
    win_pivots,
    win_inverse,
    win_coupling,
):
    leaves = lax.axis_size("leaf")
    ranks = lax.axis_size("row")
    leaf = lax.axis_index("leaf")
    rank = lax.axis_index("row")
    levels, piece, columns = win_rhs.shape
    base = piece * ranks
    share = columns // ranks
    halves = base // TILE
    path_tiles = (2 * leaves - 1) * halves
    tiles = pattern.shape[2]
    local = loc_rhs.shape[2]
    top = levels - 1
    ids = jnp.stack([leaf, rank]).astype(jnp.int32)
    wide = (share, base)

    def leaf_swaps(values):
        return [values[0]] + [swap(v, "leaf", leaves, j) for j, v in enumerate(values) if j]

    def source_row(me, step):
        place = jnp.where(me % 2 == 0, me // 2, ranks - 1 - me // 2)
        place = (place + step + ranks) % ranks
        return jnp.where(2 * place < ranks, 2 * place, 2 * (ranks - 1 - place) + 1)

    def assemble(parts, names):
        spans = [2**level if kind == "A" else 2 ** (level + 1) for kind, level in names]
        steps = [step for step, _ in parts]
        parts = [part for _, part in parts]

        def body(ids_ref, *refs):
            parts_refs, outs = refs[:ranks], refs[ranks:-2]
            natural, done = refs[-2:]
            group = ids_ref[0]
            copies = []
            for index, ref in enumerate(parts_refs):
                start = pl.multiple_of(source_row(ids_ref[1], steps[index]) * piece, 8)
                copies.append(
                    pltpu.make_async_copy(
                        ref, natural.at[:, pl.ds(start, piece), :], done.at[index]
                    )
                )
            for copy in copies:
                copy.start()
            for copy in copies:
                copy.wait()
            first = 0
            for index, ((kind, level), span) in enumerate(zip(names, spans)):
                for slot in range(span):
                    block = natural[first + slot]
                    if kind == "A":
                        row_ids = lax.broadcasted_iota(jnp.int32, block.shape, 0) + slot * base
                        col_ids = lax.broadcasted_iota(jnp.int32, block.shape, 1)
                        col_ids = col_ids + group % span * base
                        block = jnp.where(col_ids < row_ids, block, 0.0)
                    high, low = split(block)
                    outs[2 * index][slot] = high.astype(BF16)
                    outs[2 * index + 1][slot] = low.astype(BF16)
                first += span

        outs = [((span, base, base), BF16) for span in spans for _ in range(2)]
        made = call(
            body,
            outs,
            parts,
            (ids,),
            [pltpu.VMEM((sum(spans), base, base), F32), pltpu.SemaphoreType.DMA((ranks,))],
            remote=ranks,
            room=24,
        )
        return {name: made[2 * i : 2 * i + 2] for i, name in enumerate(names)}

    lower_names = [("A", level) for level in range(top)]
    lower_names += [("B", level) for level in range(top)]
    upper_names = [("A", top)]
    below = (2**top - 1) * piece
    own_blocks = [
        jnp.concatenate([win_inverse[0, :below], win_coupling[0]], 0).reshape(-1, piece, base),
        win_inverse[0, below:].reshape(-1, piece, base),
    ]
    lower_parts, upper_parts = ring_gather(own_blocks, ranks)

    start = levels * piece
    beside = start + piece + tiles <= TILE
    number_row, number_lane = (0, start + piece) if beside else (levels, start)
    aux = jnp.zeros((share, TILE), F32)
    aux = lax.dynamic_update_slice(aux, win_pivots, (0, start))
    aux = lax.dynamic_update_slice(aux, pattern[0].astype(F32), (number_row, number_lane))
    aux = jnp.tile(aux, (ranks, 1))
    packed = tiles * TILE + TILE

    firsts = [part for parts in (lower_parts, upper_parts) for step, part in parts if step in (1, -1)]

    def local_forward(rhs_ref, window_ref, aux_ref, inverse_any, coupling_any, *refs):
        refs = refs[len(firsts) :]
        solved_ref, terms_ref, split_refs = refs[0], refs[1], refs[2:6]
        held, inverse_ref, coupling_ref, done = refs[6:]
        first = pltpu.make_async_copy(inverse_any, inverse_ref, done.at[0])
        second = pltpu.make_async_copy(coupling_any, coupling_ref, done.at[1])
        first.start()
        second.start()
        rhs = rhs_ref[...]
        held[...] = jnp.zeros_like(held)
        for level in range(levels):
            held[level * piece : (level + 1) * piece, :] = window_ref[level]
        terms_ref[:, tiles * TILE :] = held[...].T + aux_ref[...]
        first.wait()
        strict = strict_lower(inverse_ref[...])
        solved = rhs + jnp.dot(strict, rhs, precision=EXACT)
        solved_ref[...] = solved.T
        second.wait()
        terms_ref[:, : tiles * TILE] = jnp.dot(coupling_ref[...], solved, precision=EXACT).T
        for part_ref, part in zip(split_refs, split(coupling_ref[...]) + split(strict)):
            part_ref[...] = part.astype(BF16)

    square = [((tiles * TILE, local), BF16)] * 2 + [((local, local), BF16)] * 2
    solved_loc, terms, *local_parts = call(
        local_forward,
        [((columns, local), F32), ((columns, packed), F32)] + square,
        (loc_rhs[0, 0], win_rhs, aux, loc_inverse[0, 0], loc_coupling[0, 0], *firsts),
        remote=2 + len(firsts),
        scratch=[
            pltpu.VMEM((TILE, columns), F32),
            pltpu.VMEM((local, local), F32),
            pltpu.VMEM((tiles * TILE, local), F32),
            pltpu.SemaphoreType.DMA((2,)),
        ],
        work=24 * local * local * columns,
        room=24,
    )
    terms = lax.all_to_all(terms.reshape(ranks, share, packed), "row", 0, 0, tiled=True)
    number_lane += tiles * TILE
    known = terms[:, number_row, number_lane : number_lane + tiles].astype(jnp.int32)

    lower = assemble(lower_parts, lower_names)
    upper = assemble(upper_parts, upper_names)
    blocks = {**lower, **upper}

    def scatter(ids_ref, known_ref, terms_ref, *refs):
        outs, pivots_ref, path = refs[:-2], refs[-2], refs[-1]
        lane = lax.broadcasted_iota(jnp.int32, (share, TILE), 1)
        path[...] = jnp.zeros_like(path)
        for source in range(ranks):
            for tile in range(tiles):
                place = known_ref[source, tile]
                path[place] = path[place] - terms_ref[source, :, tile * TILE : (tile + 1) * TILE]

        def spread(first):
            rows = []
            for half in range(halves):
                row = jnp.zeros((share, TILE), F32)
                for source in range(half * TILE // piece, (half + 1) * TILE // piece):
                    place = source * piece % TILE
                    shift = (TILE + place - first) % TILE
                    turned = pltpu.roll(terms_ref[source, :, tiles * TILE :], shift, 1)
                    row = jnp.where((lane >= place) & (lane < place + piece), turned, row)
                rows.append(row)
            return jnp.concatenate(rows, 1)

        pivots_ref[...] = spread(levels * piece)
        for level in range(levels):
            span = 2**level
            filled = outs[level]
            for slot in range(span):
                first = (span - 1 + slot) * halves
                for half in range(halves):
                    filled[slot, :, half * TILE : (half + 1) * TILE] = path[first + half]
            own = ids_ref[0] % span
            filled[own] = filled[own] + spread(level * piece)

    *rest, pivots = call(
        scatter,
        [((2**level, *wide), F32) for level in range(levels)] + [(wide, F32)],
        (terms,),
        (ids, known),
        [pltpu.VMEM((path_tiles, share, TILE), F32)],
    )

    all_pivots = leaf_swaps([pivots] * leaves)

    def total(refs):
        value = refs[0][0] if len(refs[0].shape) > len(wide) and len(refs) == 1 else refs[0][...]
        for ref in refs[1:]:
            value = value + ref[...]
        return value

    def diagonal(level, chunks, ahead=()):
        span = 2**level
        high, low = blocks["A", level]

        def body(ids_ref, *refs):
            chunk_refs, (high_ref, low_ref) = refs[:span], refs[span : span + 2]
            outs, parts = refs[span + 2 + len(ahead) : -1], refs[-1]
            own = ids_ref[0] % span
            value = total(chunk_refs)
            for slot in range(span):
                parts[slot] = times(value, high_ref[slot], low_ref[slot], 1)
            parts[own] = parts[own] + value
            if level == top:
                outs[0][...] = parts[...]
            else:
                for offset, out in enumerate(outs):
                    out[...] = parts[own ^ offset]

        outs = [((span, *wide), F32)] if level == top else [(wide, F32)] * span
        return call(
            body,
            outs,
            (*chunks, high, low, *ahead),
            (ids,),
            [pltpu.VMEM((span, *wide), F32)],
        )

    def link(level, chunks):
        span, above = 2**level, 2 ** (level + 1)
        high, low = blocks["B", level]

        def body(ids_ref, *refs):
            chunk_refs = refs[:span]
            high_ref, low_ref, rest_ref, solved_ref = refs[span : span + 4]
            outs, parts = refs[span + 4 : -1], refs[-1]
            value = total(chunk_refs)
            solved_ref[...] = value
            for slot in range(above):
                parts[slot] = rest_ref[slot] - times(value, high_ref[slot], low_ref[slot], 1)
            own = ids_ref[0] % above
            for offset, out in enumerate(outs):
                out[...] = parts[own ^ offset]

        made = call(
            body,
            [(wide, F32)] * (above + 1),
            (*chunks, high, low, rest[level + 1]),
            (ids,),
            [pltpu.VMEM((above, *wide), F32)],
        )
        return made[0], made[1:]

    chunks = [rest[0]]
    solved = []
    for level in range(top):
        chunks = leaf_swaps(diagonal(level, chunks, all_pivots if level == 1 else ()))
        value, chunks = link(level, chunks)
        solved.append(value)
        chunks = leaf_swaps(chunks)
    sums = leaf_swaps(diagonal(top, chunks) * leaves)

    def peak(ids_ref, *refs):
        sum_refs, pivot_refs = refs[:leaves], refs[leaves : 2 * leaves]
        high_ref, low_ref, out, wanted = refs[2 * leaves :]
        own = ids_ref[0] % leaves
        wanted[...] = total(sum_refs)
        for offset, ref in enumerate(pivot_refs):
            wanted[own ^ offset] = wanted[own ^ offset] / ref[top : top + 1, :]
        value = wanted[own]
        for slot in range(leaves):
            value = value + times(wanted[slot], high_ref[slot], low_ref[slot], 0)
        out[...] = value

    current = call(
        peak,
        [(wide, F32)],
        (*sums, *all_pivots, *blocks["A", top]),
        (ids,),
        [pltpu.VMEM((leaves, *wide), F32)],
    )

    def ordered(own, refs, held):
        for offset, ref in enumerate(refs):
            held[own ^ offset] = ref[...]

    def against(held, high_ref, low_ref, span):
        value = times(held[0], high_ref[0], low_ref[0], 0)
        for slot in range(1, span):
            value = value + times(held[slot], high_ref[slot], low_ref[slot], 0)
        return value

    def descend(level, parts):
        span = 2**level

        def body(ids_ref, *refs):
            part_refs = refs[:span]
            high_ref, low_ref, solved_ref, pivot_ref, out, held = refs[span:]
            ordered(ids_ref[0] % span, part_refs, held)
            above = against(held, high_ref, low_ref, span)
            out[...] = solved_ref[...] / pivot_ref[level - 1 : level, :] - above

        return call(
            body,
            [(wide, F32)],
            (*parts, *blocks["B", level - 1], solved[level - 1], pivots),
            (ids,),
            [pltpu.VMEM((span, *wide), F32)],
        )

    def transposed(level, parts):
        span = 2**level

        def body(ids_ref, *refs):
            part_refs = refs[:span]
            high_ref, low_ref, out, held = refs[span:]
            ordered(ids_ref[0] % span, part_refs, held)
            out[...] = part_refs[0][...] + against(held, high_ref, low_ref, span)

        return call(
            body,
            [(wide, F32)],
            (*parts, *blocks["A", level]),
            (ids,),
            [pltpu.VMEM((span, *wide), F32)],
        )

    everything = {top: leaf_swaps(current * leaves)}
    for level in range(top, 1, -1):
        wanted = leaf_swaps(descend(level, everything[level]) * 2 ** (level - 1))
        everything[level - 1] = leaf_swaps(transposed(level - 1, wanted) * 2 ** (level - 1))

    def finish(ids_ref, known_ref, *refs):
        refs = list(refs)
        parts = {level: [refs.pop(0) for _ in range(2**level)] for level in range(1, levels)}
        link_high, link_low, solved_ref, pivot_ref, high_ref, low_ref = refs[:6]
        out, path, held = refs[6:]
        group = ids_ref[0]
        ordered(group % 2, parts[1], held)
        wanted = solved_ref[...] / pivot_ref[0:1, :] - against(held, link_high, link_low, 2)
        lowest = wanted + times(wanted, high_ref[0], low_ref[0], 0)
        owned = [lowest]
        for half in range(halves):
            path[half] = lowest[:, half * TILE : (half + 1) * TILE]
        for level in range(1, levels):
            span = 2**level
            owned.append(parts[level][0][...])
            for offset, ref in enumerate(parts[level]):
                first = (span - 1 + (group % span ^ offset)) * halves
                for half in range(halves):
                    path[first + half] = ref[:, half * TILE : (half + 1) * TILE]
        lane = lax.broadcasted_iota(jnp.int32, (share, TILE), 1)
        for target in range(ranks):
            for tile in range(tiles):
                out[target, :, tile * TILE : (tile + 1) * TILE] = path[known_ref[target, tile]]
            pieces = jnp.zeros((share, TILE), F32)
            for level in range(levels):
                shift = (base + level * piece - target * piece) % base
                turned = pltpu.roll(owned[level], shift, 1)[:, :TILE]
                mine = (lane >= level * piece) & (lane < (level + 1) * piece)
                pieces = jnp.where(mine, turned, pieces)
            out[target, :, tiles * TILE :] = pieces

    replies = call(
        finish,
        [((ranks, share, packed), F32)],
        (
            *[part for level in range(1, levels) for part in everything[level]],
            *blocks["B", 0],
            solved[0],
            pivots,
            *blocks["A", 0],
        ),
        (ids, known),
        [pltpu.VMEM((path_tiles, share, TILE), F32), pltpu.VMEM((2, *wide), F32)],
    )
    back = lax.all_to_all(replies[0], "row", 0, 0, tiled=True).reshape(columns, packed)

    def local_backward(back, solved_ref, pivot_ref, *refs):
        sources, (out, window_ref), held, done = refs[:4], refs[4:6], refs[6:10], refs[10]
        copies = [
            pltpu.make_async_copy(source, target, done.at[index])
            for index, (source, target) in enumerate(zip(sources, held))
        ]
        for copy in copies:
            copy.start()
        final = back[:, tiles * TILE :].T
        for level in range(levels):
            window_ref[level] = final[level * piece : (level + 1) * piece]
        scaled = solved_ref[...] / pivot_ref[...]
        copies[0].wait()
        copies[1].wait()
        remainder = scaled - times(back[:, : tiles * TILE], held[0][...], held[1][...], 0)
        copies[2].wait()
        copies[3].wait()
        answer = remainder + times(remainder, held[2][...], held[3][...], 0)
        out[...] = answer.T

    answer, window = call(
        local_backward,
        [((local, columns), F32), ((levels, piece, columns), F32)],
        (back, solved_loc, loc_pivots[0], *local_parts),
        scratch=[pltpu.VMEM(*part) for part in square] + [pltpu.SemaphoreType.DMA((4,))],
        remote=4,
        work=24 * local * local * columns,
        room=24,
    )
    return answer[None, None], window


def solution(mesh):
    return jax.shard_map(
        shards,
        mesh=mesh,
        in_specs=(
            P("leaf", "row", None, None),
            P("leaf", "row", None, None),
            P("leaf", "row", None, None),
            P("leaf", "row", None),
            P("leaf", "row", None),
            P(None, ("leaf", "row"), None),
            P(None, ("leaf", "row")),
            P("row", None, "leaf"),
            P("row", None, "leaf"),
        ),
        out_specs=(P("leaf", "row", None, None), P(None, ("leaf", "row"), None)),
        check_vma=False,
    )
```

```python
import math

import jax
import jax.numpy as jnp
from jax import lax
from jax.experimental import pallas as pl
from jax.experimental.pallas import tpu as pltpu
from jax.sharding import PartitionSpec as P

TILE = 128
EXACT = lax.Precision.HIGHEST
F32 = jnp.float32
BF16 = jnp.bfloat16


def swap(value, axis, count, offset):
    return lax.ppermute(value, axis, [(i, i ^ offset) for i in range(count)])


def ring_order(count):
    return list(range(0, count, 2)) + list(range(count - 1, 0, -2))


def ring_gather(block, count):
    order = ring_order(count)
    right = [(order[i], order[(i + 1) % count]) for i in range(count)]
    left = [(target, source) for source, target in right]
    parts = [(0, 0, block)]
    forward = backward = block
    middle = block.shape[0] // 2
    for step in range(1, count // 2 + 1):
        first = 0
        if 2 * step == count:
            forward, backward, first = forward[:middle], backward[middle:], middle
        forward = lax.ppermute(forward, "row", right)
        backward = lax.ppermute(backward, "row", left)
        parts += [(-step, 0, forward), (step, first, backward)]
    return parts


def call(body, outs, arrays, scalars=(), scratch=(), work=0, remote=0, room=16):
    moved = sum(a.size * a.dtype.itemsize for a in arrays)
    moved += sum(math.prod(shape) * jnp.dtype(kind).itemsize for shape, kind in outs)
    return pl.pallas_call(
        body,
        out_shape=[jax.ShapeDtypeStruct(*o) for o in outs],
        in_specs=[pl.BlockSpec(memory_space=pltpu.SMEM)] * len(scalars)
        + [pl.BlockSpec(memory_space=pltpu.VMEM)] * (len(arrays) - remote)
        + [pl.BlockSpec(memory_space=pltpu.HBM)] * remote,
        out_specs=[pl.BlockSpec(memory_space=pltpu.VMEM)] * len(outs),
        scratch_shapes=list(scratch),
        compiler_params=pltpu.CompilerParams(vmem_limit_bytes=room << 20),
        cost_estimate=pl.CostEstimate(flops=work, bytes_accessed=moved, transcendentals=0),
    )(*scalars, *arrays)


def split(value):
    high = value.astype(BF16).astype(F32)
    return high, value - high


def times(value, high, low, right_dim):
    rows = value.shape[0]
    dims = (((1,), (right_dim,)), ((), ()))

    def product(part):
        return lax.dot_general(part, high, dims, preferred_element_type=F32) + lax.dot_general(
            part, low, dims, preferred_element_type=F32
        )

    first, second = split(value)
    if rows % 8:
        return product(first.astype(BF16)) + product(second.astype(BF16))
    both = product(jnp.concatenate([first, second], 0).astype(BF16))
    return both[:rows] + both[rows:]


def strict_lower(block):
    row_ids = lax.broadcasted_iota(jnp.int32, block.shape, 0)
    col_ids = lax.broadcasted_iota(jnp.int32, block.shape, 1)
    return jnp.where(col_ids < row_ids, block, 0.0)


def shards(
    loc_rhs,
    loc_inverse,
    loc_coupling,
    loc_pivots,
    pattern,
    win_rhs,
    win_pivots,
    win_inverse,
    win_coupling,
):
    leaves = lax.axis_size("leaf")
    ranks = lax.axis_size("row")
    leaf = lax.axis_index("leaf")
    rank = lax.axis_index("row")
    levels, piece, columns = win_rhs.shape
    base = piece * ranks
    share = columns // ranks
    halves = base // TILE
    path_tiles = (2 * leaves - 1) * halves
    tiles = pattern.shape[2]
    local = loc_rhs.shape[2]
    top = levels - 1
    ids = jnp.stack([leaf, rank]).astype(jnp.int32)
    wide = (share, base)

    def leaf_swaps(values):
        return [values[0]] + [swap(v, "leaf", leaves, j) for j, v in enumerate(values) if j]

    def source_row(me, step):
        place = jnp.where(me % 2 == 0, me // 2, ranks - 1 - me // 2)
        place = (place + step + ranks) % ranks
        return jnp.where(2 * place < ranks, 2 * place, 2 * (ranks - 1 - place) + 1)

    def width(name):
        return 2 ** name[1] if name[0] == "A" else 2 ** (name[1] + 1)

    all_names = [("A", level) for level in range(levels)] + [("B", level) for level in range(top)]

    def runs(names):
        found, slot, place = [], 0, 0
        for name in all_names:
            if name in names:
                if found and found[-1][1] == slot:
                    found[-1][1] += width(name)
                else:
                    found.append([slot, slot + width(name), place])
                place += width(name)
            slot += width(name)
        return found

    def assemble(names):
        names = [name for name in all_names if name in names]
        spans = [width(name) for name in names]
        moves = []
        for index, (step, before, part) in enumerate(parts):
            for first, end, place in runs(names):
                low, high = max(first, before), min(end, before + part.shape[0])
                if low < high:
                    moves.append((index, step, low - before, high - before, place + low - first))

        def body(ids_ref, *refs):
            parts_refs, outs = refs[: len(parts)], refs[len(parts) : -2]
            natural, done = refs[-2:]
            group = ids_ref[0]
            copies = []
            for number, (index, step, low, high, place) in enumerate(moves):
                start = pl.multiple_of(source_row(ids_ref[1], step) * piece, 8)
                copies.append(
                    pltpu.make_async_copy(
                        parts_refs[index].at[low:high],
                        natural.at[place : place + high - low, pl.ds(start, piece), :],
                        done.at[number],
                    )
                )
            for copy in copies:
                copy.start()
            for copy in copies:
                copy.wait()
            first = 0
            for index, ((kind, level), span) in enumerate(zip(names, spans)):
                for slot in range(span):
                    block = natural[first + slot]
                    if kind == "A":
                        row_ids = lax.broadcasted_iota(jnp.int32, block.shape, 0) + slot * base
                        col_ids = lax.broadcasted_iota(jnp.int32, block.shape, 1)
                        col_ids = col_ids + group % span * base
                        block = jnp.where(col_ids < row_ids, block, 0.0)
                    high, low = split(block)
                    outs[2 * index][slot] = high.astype(BF16)
                    outs[2 * index + 1][slot] = low.astype(BF16)
                first += span

        outs = [((span, base, base), BF16) for span in spans for _ in range(2)]
        made = call(
            body,
            outs,
            [part for _, _, part in parts],
            (ids,),
            [pltpu.VMEM((sum(spans), base, base), F32), pltpu.SemaphoreType.DMA((len(moves),))],
            remote=len(parts),
            room=24,
        )
        return {name: made[2 * i : 2 * i + 2] for i, name in enumerate(names)}

    parts = ring_gather(
        jnp.concatenate([win_inverse[0], win_coupling[0]], 0).reshape(-1, piece, base), ranks
    )

    start = levels * piece
    beside = start + piece + tiles <= TILE
    number_row, number_lane = (0, start + piece) if beside else (levels, start)
    aux = jnp.zeros((share, TILE), F32)
    aux = lax.dynamic_update_slice(aux, win_pivots, (0, start))
    aux = lax.dynamic_update_slice(aux, pattern[0].astype(F32), (number_row, number_lane))
    aux = jnp.tile(aux, (ranks, 1))
    packed = tiles * TILE + TILE

    firsts = [part for step, _, part in parts if step in (1, -1)]

    def local_forward(rhs_ref, window_ref, aux_ref, inverse_any, coupling_any, *refs):
        refs = refs[len(firsts) :]
        solved_ref, terms_ref, held, inverse_ref, coupling_ref, done = refs
        first = pltpu.make_async_copy(inverse_any, inverse_ref, done.at[0])
        second = pltpu.make_async_copy(coupling_any, coupling_ref, done.at[1])
        first.start()
        second.start()
        rhs = rhs_ref[...]
        held[...] = jnp.zeros_like(held)
        for level in range(levels):
            held[level * piece : (level + 1) * piece, :] = window_ref[level]
        terms_ref[:, tiles * TILE :] = held[...].T + aux_ref[...]
        first.wait()
        strict = strict_lower(inverse_ref[...])
        solved = rhs + jnp.dot(strict, rhs, precision=EXACT)
        solved_ref[...] = solved.T
        second.wait()
        terms_ref[:, : tiles * TILE] = jnp.dot(coupling_ref[...], solved, precision=EXACT).T

    solved_loc, terms = call(
        local_forward,
        [((columns, local), F32), ((columns, packed), F32)],
        (loc_rhs[0, 0], win_rhs, aux, loc_inverse[0, 0], loc_coupling[0, 0], *firsts),
        remote=2 + len(firsts),
        scratch=[
            pltpu.VMEM((TILE, columns), F32),
            pltpu.VMEM((local, local), F32),
            pltpu.VMEM((tiles * TILE, local), F32),
            pltpu.SemaphoreType.DMA((2,)),
        ],
        work=24 * local * local * columns,
        room=24,
    )
    terms = lax.all_to_all(terms.reshape(ranks, share, packed), "row", 0, 0, tiled=True)
    number_lane += tiles * TILE
    known = terms[:, number_row, number_lane : number_lane + tiles].astype(jnp.int32)

    lower = assemble([name for name in all_names if name != ("A", top)])
    upper = assemble([("A", top)])
    blocks = {**lower, **upper}

    def scatter(ids_ref, known_ref, terms_ref, *refs):
        outs, pivots_ref, path = refs[:-2], refs[-2], refs[-1]
        lane = lax.broadcasted_iota(jnp.int32, (share, TILE), 1)
        path[...] = jnp.zeros_like(path)
        for source in range(ranks):
            for tile in range(tiles):
                place = known_ref[source, tile]
                path[place] = path[place] - terms_ref[source, :, tile * TILE : (tile + 1) * TILE]

        def spread(first):
            rows = []
            for half in range(halves):
                row = jnp.zeros((share, TILE), F32)
                for source in range(half * TILE // piece, (half + 1) * TILE // piece):
                    place = source * piece % TILE
                    shift = (TILE + place - first) % TILE
                    turned = pltpu.roll(terms_ref[source, :, tiles * TILE :], shift, 1)
                    row = jnp.where((lane >= place) & (lane < place + piece), turned, row)
                rows.append(row)
            return jnp.concatenate(rows, 1)

        pivots_ref[...] = spread(levels * piece)
        for level in range(levels):
            span = 2**level
            filled = outs[level]
            for slot in range(span):
                first = (span - 1 + slot) * halves
                for half in range(halves):
                    filled[slot, :, half * TILE : (half + 1) * TILE] = path[first + half]
            own = ids_ref[0] % span
            filled[own] = filled[own] + spread(level * piece)

    *rest, pivots = call(
        scatter,
        [((2**level, *wide), F32) for level in range(levels)] + [(wide, F32)],
        (terms,),
        (ids, known),
        [pltpu.VMEM((path_tiles, share, TILE), F32)],
    )

    all_pivots = leaf_swaps([pivots] * leaves)

    def total(refs):
        value = refs[0][0] if len(refs[0].shape) > len(wide) and len(refs) == 1 else refs[0][...]
        for ref in refs[1:]:
            value = value + ref[...]
        return value

    def diagonal(level, chunks, ahead=()):
        span = 2**level
        high, low = blocks["A", level]

        def body(ids_ref, *refs):
            chunk_refs, (high_ref, low_ref) = refs[:span], refs[span : span + 2]
            outs, parts = refs[span + 2 + len(ahead) : -1], refs[-1]
            own = ids_ref[0] % span
            value = total(chunk_refs)
            for slot in range(span):
                parts[slot] = times(value, high_ref[slot], low_ref[slot], 1)
            parts[own] = parts[own] + value
            if level == top:
                outs[0][...] = parts[...]
            else:
                for offset, out in enumerate(outs):
                    out[...] = parts[own ^ offset]

        outs = [((span, *wide), F32)] if level == top else [(wide, F32)] * span
        return call(
            body,
            outs,
            (*chunks, high, low, *ahead),
            (ids,),
            [pltpu.VMEM((span, *wide), F32)],
        )

    def link(level, chunks):
        span, above = 2**level, 2 ** (level + 1)
        high, low = blocks["B", level]

        def body(ids_ref, *refs):
            chunk_refs = refs[:span]
            high_ref, low_ref, rest_ref, solved_ref = refs[span : span + 4]
            outs, parts = refs[span + 4 : -1], refs[-1]
            value = total(chunk_refs)
            solved_ref[...] = value
            for slot in range(above):
                parts[slot] = rest_ref[slot] - times(value, high_ref[slot], low_ref[slot], 1)
            own = ids_ref[0] % above
            for offset, out in enumerate(outs):
                out[...] = parts[own ^ offset]

        made = call(
            body,
            [(wide, F32)] * (above + 1),
            (*chunks, high, low, rest[level + 1]),
            (ids,),
            [pltpu.VMEM((above, *wide), F32)],
        )
        return made[0], made[1:]

    chunks = [rest[0]]
    solved = []
    for level in range(top):
        chunks = leaf_swaps(diagonal(level, chunks, all_pivots if level == 1 else ()))
        value, chunks = link(level, chunks)
        solved.append(value)
        chunks = leaf_swaps(chunks)
    sums = leaf_swaps(diagonal(top, chunks) * leaves)

    def peak(ids_ref, *refs):
        sum_refs, pivot_refs = refs[:leaves], refs[leaves : 2 * leaves]
        high_ref, low_ref, out, wanted = refs[2 * leaves :]
        own = ids_ref[0] % leaves
        wanted[...] = total(sum_refs)
        for offset, ref in enumerate(pivot_refs):
            wanted[own ^ offset] = wanted[own ^ offset] / ref[top : top + 1, :]
        value = wanted[own]
        for slot in range(leaves):
            value = value + times(wanted[slot], high_ref[slot], low_ref[slot], 0)
        out[...] = value

    current = call(
        peak,
        [(wide, F32)],
        (*sums, *all_pivots, *blocks["A", top]),
        (ids,),
        [pltpu.VMEM((leaves, *wide), F32)],
    )

    def ordered(own, refs, held):
        for offset, ref in enumerate(refs):
            held[own ^ offset] = ref[...]

    def against(held, high_ref, low_ref, span):
        value = times(held[0], high_ref[0], low_ref[0], 0)
        for slot in range(1, span):
            value = value + times(held[slot], high_ref[slot], low_ref[slot], 0)
        return value

    def descend(level, parts):
        span = 2**level

        def body(ids_ref, *refs):
            part_refs = refs[:span]
            high_ref, low_ref, solved_ref, pivot_ref, out, held = refs[span:]
            ordered(ids_ref[0] % span, part_refs, held)
            above = against(held, high_ref, low_ref, span)
            out[...] = solved_ref[...] / pivot_ref[level - 1 : level, :] - above

        return call(
            body,
            [(wide, F32)],
            (*parts, *blocks["B", level - 1], solved[level - 1], pivots),
            (ids,),
            [pltpu.VMEM((span, *wide), F32)],
        )

    def transposed(level, parts):
        span = 2**level

        def body(ids_ref, *refs):
            part_refs = refs[:span]
            high_ref, low_ref, out, held = refs[span:]
            ordered(ids_ref[0] % span, part_refs, held)
            out[...] = part_refs[0][...] + against(held, high_ref, low_ref, span)

        return call(
            body,
            [(wide, F32)],
            (*parts, *blocks["A", level]),
            (ids,),
            [pltpu.VMEM((span, *wide), F32)],
        )

    everything = {top: leaf_swaps(current * leaves)}
    for level in range(top, 1, -1):
        wanted = leaf_swaps(descend(level, everything[level]) * 2 ** (level - 1))
        everything[level - 1] = leaf_swaps(transposed(level - 1, wanted) * 2 ** (level - 1))

    def finish(ids_ref, known_ref, *refs):
        refs = list(refs)
        parts = {level: [refs.pop(0) for _ in range(2**level)] for level in range(1, levels)}
        link_high, link_low, solved_ref, pivot_ref, high_ref, low_ref = refs[:6]
        out, path, held = refs[6:]
        group = ids_ref[0]
        ordered(group % 2, parts[1], held)
        wanted = solved_ref[...] / pivot_ref[0:1, :] - against(held, link_high, link_low, 2)
        lowest = wanted + times(wanted, high_ref[0], low_ref[0], 0)
        owned = [lowest]
        for half in range(halves):
            path[half] = lowest[:, half * TILE : (half + 1) * TILE]
        for level in range(1, levels):
            span = 2**level
            owned.append(parts[level][0][...])
            for offset, ref in enumerate(parts[level]):
                first = (span - 1 + (group % span ^ offset)) * halves
                for half in range(halves):
                    path[first + half] = ref[:, half * TILE : (half + 1) * TILE]
        lane = lax.broadcasted_iota(jnp.int32, (share, TILE), 1)
        for target in range(ranks):
            for tile in range(tiles):
                out[target, :, tile * TILE : (tile + 1) * TILE] = path[known_ref[target, tile]]
            pieces = jnp.zeros((share, TILE), F32)
            for level in range(levels):
                shift = (base + level * piece - target * piece) % base
                turned = pltpu.roll(owned[level], shift, 1)[:, :TILE]
                mine = (lane >= level * piece) & (lane < (level + 1) * piece)
                pieces = jnp.where(mine, turned, pieces)
            out[target, :, tiles * TILE :] = pieces

    replies = call(
        finish,
        [((ranks, share, packed), F32)],
        (
            *[part for level in range(1, levels) for part in everything[level]],
            *blocks["B", 0],
            solved[0],
            pivots,
            *blocks["A", 0],
        ),
        (ids, known),
        [pltpu.VMEM((path_tiles, share, TILE), F32), pltpu.VMEM((2, *wide), F32)],
    )
    back = lax.all_to_all(replies[0], "row", 0, 0, tiled=True).reshape(columns, packed)

    def local_backward(back, solved_ref, pivot_ref, inverse_any, coupling_any, *refs):
        out, window_ref, inverse_ref, coupling_ref, done = refs
        first = pltpu.make_async_copy(coupling_any, coupling_ref, done.at[0])
        second = pltpu.make_async_copy(inverse_any, inverse_ref, done.at[1])
        first.start()
        second.start()
        final = back[:, tiles * TILE :].T
        for level in range(levels):
            window_ref[level] = final[level * piece : (level + 1) * piece]
        scaled = solved_ref[...] / pivot_ref[...]
        first.wait()
        high, low = split(coupling_ref[...])
        remainder = scaled - times(back[:, : tiles * TILE], high.astype(BF16), low.astype(BF16), 0)
        second.wait()
        high, low = split(strict_lower(inverse_ref[...]))
        answer = remainder + times(remainder, high.astype(BF16), low.astype(BF16), 0)
        out[...] = answer.T

    answer, window = call(
        local_backward,
        [((local, columns), F32), ((levels, piece, columns), F32)],
        (back, solved_loc, loc_pivots[0], loc_inverse[0, 0], loc_coupling[0, 0]),
        scratch=[
            pltpu.VMEM((local, local), F32),
            pltpu.VMEM((tiles * TILE, local), F32),
            pltpu.SemaphoreType.DMA((2,)),
        ],
        remote=2,
        work=24 * local * local * columns,
        room=24,
    )
    return answer[None, None], window


def solution(mesh):
    return jax.shard_map(
        shards,
        mesh=mesh,
        in_specs=(
            P("leaf", "row", None, None),
            P("leaf", "row", None, None),
            P("leaf", "row", None, None),
            P("leaf", "row", None),
            P("leaf", "row", None),
            P(None, ("leaf", "row"), None),
            P(None, ("leaf", "row")),
            P("row", None, "leaf"),
            P("row", None, "leaf"),
        ),
        out_specs=(P("leaf", "row", None, None), P(None, ("leaf", "row"), None)),
        check_vma=False,
    )
```

```python
import math

import jax
import jax.numpy as jnp
from jax import lax
from jax.experimental import pallas as pl
from jax.experimental.pallas import tpu as pltpu
from jax.sharding import PartitionSpec as P

TILE = 128
F32 = jnp.float32
BF16 = jnp.bfloat16


def swap(value, axis, count, offset):
    return lax.ppermute(value, axis, [(i, i ^ offset) for i in range(count)])


def ring_order(count):
    return list(range(0, count, 2)) + list(range(count - 1, 0, -2))


def ring_gather(block, count, ahead):
    order = ring_order(count)
    right = [(order[i], order[(i + 1) % count]) for i in range(count)]
    left = [(target, source) for source, target in right]
    parts = [(0, 0, block)]
    forward = backward = block
    middle = block.shape[0] // 2
    for step in range(1, count // 2 + 1):
        first = 0
        if 2 * step == count:
            forward, backward, first = forward[:middle], backward[middle:], middle
        forward = lax.ppermute(forward, "row", right)
        backward = lax.ppermute(backward, "row", left)
        if step == 1:
            forward, backward, _ = lax.optimization_barrier((forward, backward, ahead))
        parts += [(-step, 0, forward), (step, first, backward)]
    return parts


def call(body, outs, arrays, scalars=(), scratch=(), work=0, remote=0, room=16):
    moved = sum(a.size * a.dtype.itemsize for a in arrays)
    moved += sum(math.prod(shape) * jnp.dtype(kind).itemsize for shape, kind in outs)
    return pl.pallas_call(
        body,
        out_shape=[jax.ShapeDtypeStruct(*o) for o in outs],
        in_specs=[pl.BlockSpec(memory_space=pltpu.SMEM)] * len(scalars)
        + [pl.BlockSpec(memory_space=pltpu.VMEM)] * (len(arrays) - remote)
        + [pl.BlockSpec(memory_space=pltpu.HBM)] * remote,
        out_specs=[pl.BlockSpec(memory_space=pltpu.VMEM)] * len(outs),
        scratch_shapes=list(scratch),
        compiler_params=pltpu.CompilerParams(vmem_limit_bytes=room << 20),
        cost_estimate=pl.CostEstimate(flops=work, bytes_accessed=moved, transcendentals=0),
    )(*scalars, *arrays)


def split(value):
    high = value.astype(BF16).astype(F32)
    return high, value - high


def times(value, high, low, right_dim):
    rows = value.shape[0]
    dims = (((1,), (right_dim,)), ((), ()))

    def product(part):
        return lax.dot_general(part, high, dims, preferred_element_type=F32) + lax.dot_general(
            part, low, dims, preferred_element_type=F32
        )

    first, second = split(value)
    if rows % 8:
        return product(first.astype(BF16)) + product(second.astype(BF16))
    both = product(jnp.concatenate([first, second], 0).astype(BF16))
    return both[:rows] + both[rows:]


def times_left(block, value):
    columns = value.shape[1]
    both = jnp.concatenate(split(value), 1).astype(BF16)
    product = sum(
        jnp.dot(part.astype(BF16), both, preferred_element_type=F32) for part in split(block)
    )
    return product[:, :columns] + product[:, columns:]


def strict_lower(block):
    row_ids = lax.broadcasted_iota(jnp.int32, block.shape, 0)
    col_ids = lax.broadcasted_iota(jnp.int32, block.shape, 1)
    return jnp.where(col_ids < row_ids, block, 0.0)


def shards(
    loc_rhs,
    loc_inverse,
    loc_coupling,
    loc_pivots,
    pattern,
    win_rhs,
    win_pivots,
    win_inverse,
    win_coupling,
):
    leaves = lax.axis_size("leaf")
    ranks = lax.axis_size("row")
    leaf = lax.axis_index("leaf")
    rank = lax.axis_index("row")
    levels, piece, columns = win_rhs.shape
    base = piece * ranks
    share = columns // ranks
    halves = base // TILE
    path_tiles = (2 * leaves - 1) * halves
    tiles = pattern.shape[2]
    local = loc_rhs.shape[2]
    top = levels - 1
    ids = jnp.stack([leaf, rank]).astype(jnp.int32)
    wide = (share, base)

    def leaf_swaps(values):
        return [values[0]] + [swap(v, "leaf", leaves, j) for j, v in enumerate(values) if j]

    def source_row(me, step):
        place = jnp.where(me % 2 == 0, me // 2, ranks - 1 - me // 2)
        place = (place + step + ranks) % ranks
        return jnp.where(2 * place < ranks, 2 * place, 2 * (ranks - 1 - place) + 1)

    def width(name):
        return 2 ** name[1] if name[0] == "A" else 2 ** (name[1] + 1)

    all_names = [("A", level) for level in range(levels)] + [("B", level) for level in range(top)]

    def runs(names):
        found, slot, place = [], 0, 0
        for name in all_names:
            if name in names:
                if found and found[-1][1] == slot:
                    found[-1][1] += width(name)
                else:
                    found.append([slot, slot + width(name), place])
                place += width(name)
            slot += width(name)
        return found

    def assemble(names):
        names = [name for name in all_names if name in names]
        spans = [width(name) for name in names]
        moves = []
        for index, (step, before, part) in enumerate(parts):
            for first, end, place in runs(names):
                low, high = max(first, before), min(end, before + part.shape[0])
                if low < high:
                    moves.append((index, step, low - before, high - before, place + low - first))

        def body(ids_ref, *refs):
            parts_refs, outs = refs[: len(parts)], refs[len(parts) : -2]
            natural, done = refs[-2:]
            group = ids_ref[0]
            copies = []
            for number, (index, step, low, high, place) in enumerate(moves):
                start = pl.multiple_of(source_row(ids_ref[1], step) * piece, 8)
                copies.append(
                    pltpu.make_async_copy(
                        parts_refs[index].at[low:high],
                        natural.at[place : place + high - low, pl.ds(start, piece), :],
                        done.at[number],
                    )
                )
            for copy in copies:
                copy.start()
            for copy in copies:
                copy.wait()
            first = 0
            for index, ((kind, level), span) in enumerate(zip(names, spans)):
                for slot in range(span):
                    block = natural[first + slot]
                    if kind == "A":
                        row_ids = lax.broadcasted_iota(jnp.int32, block.shape, 0) + slot * base
                        col_ids = lax.broadcasted_iota(jnp.int32, block.shape, 1)
                        col_ids = col_ids + group % span * base
                        block = jnp.where(col_ids < row_ids, block, 0.0)
                    high, low = split(block)
                    outs[2 * index][slot] = high.astype(BF16)
                    outs[2 * index + 1][slot] = low.astype(BF16)
                first += span

        outs = [((span, base, base), BF16) for span in spans for _ in range(2)]
        made = call(
            body,
            outs,
            [part for _, _, part in parts],
            (ids,),
            [pltpu.VMEM((sum(spans), base, base), F32), pltpu.SemaphoreType.DMA((len(moves),))],
            remote=len(parts),
            room=24,
        )
        return {name: made[2 * i : 2 * i + 2] for i, name in enumerate(names)}

    start = levels * piece
    beside = start + piece + tiles <= TILE
    number_row, number_lane = (0, start + piece) if beside else (levels, start)
    aux = jnp.zeros((share, TILE), F32)
    aux = lax.dynamic_update_slice(aux, win_pivots, (0, start))
    aux = lax.dynamic_update_slice(aux, pattern[0].astype(F32), (number_row, number_lane))
    aux = jnp.tile(aux, (ranks, 1))
    packed = tiles * TILE + TILE

    def local_forward(rhs_ref, window_ref, aux_ref, inverse_any, coupling_any, *refs):
        solved_ref, terms_ref, held, inverse_ref, coupling_ref, done = refs
        first = pltpu.make_async_copy(inverse_any, inverse_ref, done.at[0])
        second = pltpu.make_async_copy(coupling_any, coupling_ref, done.at[1])
        first.start()
        second.start()
        rhs = rhs_ref[...]
        held[...] = jnp.zeros_like(held)
        for level in range(levels):
            held[level * piece : (level + 1) * piece, :] = window_ref[level]
        terms_ref[:, tiles * TILE :] = held[...].T + aux_ref[...]
        first.wait()
        solved = rhs + times_left(strict_lower(inverse_ref[...]), rhs)
        solved_ref[...] = solved.T
        second.wait()
        terms_ref[:, : tiles * TILE] = times_left(coupling_ref[...], solved).T

    solved_loc, terms = call(
        local_forward,
        [((columns, local), F32), ((columns, packed), F32)],
        (loc_rhs[0, 0], win_rhs, aux, loc_inverse[0, 0], loc_coupling[0, 0]),
        remote=2,
        scratch=[
            pltpu.VMEM((TILE, columns), F32),
            pltpu.VMEM((local, local), F32),
            pltpu.VMEM((tiles * TILE, local), F32),
            pltpu.SemaphoreType.DMA((2,)),
        ],
        work=24 * local * local * columns,
        room=24,
    )
    parts = ring_gather(
        jnp.concatenate([win_inverse[0], win_coupling[0]], 0).reshape(-1, piece, base),
        ranks,
        terms,
    )
    terms = lax.all_to_all(terms.reshape(ranks, share, packed), "row", 0, 0, tiled=True)
    number_lane += tiles * TILE
    known = terms[:, number_row, number_lane : number_lane + tiles].astype(jnp.int32)

    lower = assemble([name for name in all_names if name != ("A", top)])
    upper = assemble([("A", top)])
    blocks = {**lower, **upper}

    def scatter(ids_ref, known_ref, terms_ref, *refs):
        outs, pivots_ref, path = refs[:-2], refs[-2], refs[-1]
        lane = lax.broadcasted_iota(jnp.int32, (share, TILE), 1)
        path[...] = jnp.zeros_like(path)
        for source in range(ranks):
            for tile in range(tiles):
                place = known_ref[source, tile]
                path[place] = path[place] - terms_ref[source, :, tile * TILE : (tile + 1) * TILE]

        def spread(first):
            rows = []
            for half in range(halves):
                row = jnp.zeros((share, TILE), F32)
                for source in range(half * TILE // piece, (half + 1) * TILE // piece):
                    place = source * piece % TILE
                    shift = (TILE + place - first) % TILE
                    turned = pltpu.roll(terms_ref[source, :, tiles * TILE :], shift, 1)
                    row = jnp.where((lane >= place) & (lane < place + piece), turned, row)
                rows.append(row)
            return jnp.concatenate(rows, 1)

        pivots_ref[...] = spread(levels * piece)
        for level in range(levels):
            span = 2**level
            filled = outs[level]
            for slot in range(span):
                first = (span - 1 + slot) * halves
                for half in range(halves):
                    filled[slot, :, half * TILE : (half + 1) * TILE] = path[first + half]
            own = ids_ref[0] % span
            filled[own] = filled[own] + spread(level * piece)

    *rest, pivots = call(
        scatter,
        [((2**level, *wide), F32) for level in range(levels)] + [(wide, F32)],
        (terms,),
        (ids, known),
        [pltpu.VMEM((path_tiles, share, TILE), F32)],
    )

    all_pivots = leaf_swaps([pivots] * leaves)

    def total(refs):
        value = refs[0][0] if len(refs[0].shape) > len(wide) and len(refs) == 1 else refs[0][...]
        for ref in refs[1:]:
            value = value + ref[...]
        return value

    def diagonal(level, chunks, ahead=()):
        span = 2**level
        high, low = blocks["A", level]

        def body(ids_ref, *refs):
            chunk_refs, (high_ref, low_ref) = refs[:span], refs[span : span + 2]
            outs, parts = refs[span + 2 + len(ahead) : -1], refs[-1]
            own = ids_ref[0] % span
            value = total(chunk_refs)
            for slot in range(span):
                parts[slot] = times(value, high_ref[slot], low_ref[slot], 1)
            parts[own] = parts[own] + value
            if level == top:
                outs[0][...] = parts[...]
            else:
                for offset, out in enumerate(outs):
                    out[...] = parts[own ^ offset]

        outs = [((span, *wide), F32)] if level == top else [(wide, F32)] * span
        return call(
            body,
            outs,
            (*chunks, high, low, *ahead),
            (ids,),
            [pltpu.VMEM((span, *wide), F32)],
        )

    def link(level, chunks):
        span, above = 2**level, 2 ** (level + 1)
        high, low = blocks["B", level]
        lowest = () if level else blocks["A", 0]

        def body(ids_ref, *refs):
            chunk_refs, refs = refs[:span], refs[span:]
            value = total(chunk_refs)
            if lowest:
                value = value + times(value, refs[0][0], refs[1][0], 1)
                refs = refs[2:]
            high_ref, low_ref, rest_ref, solved_ref = refs[:4]
            outs, parts = refs[4:-1], refs[-1]
            solved_ref[...] = value
            for slot in range(above):
                parts[slot] = rest_ref[slot] - times(value, high_ref[slot], low_ref[slot], 1)
            own = ids_ref[0] % above
            for offset, out in enumerate(outs):
                out[...] = parts[own ^ offset]

        made = call(
            body,
            [(wide, F32)] * (above + 1),
            (*chunks, *lowest, high, low, rest[level + 1]),
            (ids,),
            [pltpu.VMEM((above, *wide), F32)],
        )
        return made[0], made[1:]

    chunks = [rest[0]]
    solved = []
    for level in range(top):
        if level:
            chunks = leaf_swaps(diagonal(level, chunks, all_pivots if level == 1 else ()))
        value, chunks = link(level, chunks)
        solved.append(value)
        chunks = leaf_swaps(chunks)
    sums = leaf_swaps(diagonal(top, chunks) * leaves)

    def peak(ids_ref, *refs):
        sum_refs, pivot_refs = refs[:leaves], refs[leaves : 2 * leaves]
        high_ref, low_ref, out, wanted = refs[2 * leaves :]
        own = ids_ref[0] % leaves
        wanted[...] = total(sum_refs)
        for offset, ref in enumerate(pivot_refs):
            wanted[own ^ offset] = wanted[own ^ offset] / ref[top : top + 1, :]
        value = wanted[own]
        for slot in range(leaves):
            value = value + times(wanted[slot], high_ref[slot], low_ref[slot], 0)
        out[...] = value

    current = call(
        peak,
        [(wide, F32)],
        (*sums, *all_pivots, *blocks["A", top]),
        (ids,),
        [pltpu.VMEM((leaves, *wide), F32)],
    )

    def ordered(own, refs, held):
        for offset, ref in enumerate(refs):
            held[own ^ offset] = ref[...]

    def against(held, high_ref, low_ref, span):
        value = times(held[0], high_ref[0], low_ref[0], 0)
        for slot in range(1, span):
            value = value + times(held[slot], high_ref[slot], low_ref[slot], 0)
        return value

    def descend(level, parts):
        span = 2**level

        def body(ids_ref, *refs):
            part_refs = refs[:span]
            high_ref, low_ref, solved_ref, pivot_ref, out, held = refs[span:]
            ordered(ids_ref[0] % span, part_refs, held)
            above = against(held, high_ref, low_ref, span)
            out[...] = solved_ref[...] / pivot_ref[level - 1 : level, :] - above

        return call(
            body,
            [(wide, F32)],
            (*parts, *blocks["B", level - 1], solved[level - 1], pivots),
            (ids,),
            [pltpu.VMEM((span, *wide), F32)],
        )

    def transposed(level, parts):
        span = 2**level

        def body(ids_ref, *refs):
            part_refs = refs[:span]
            high_ref, low_ref, out, held = refs[span:]
            ordered(ids_ref[0] % span, part_refs, held)
            out[...] = part_refs[0][...] + against(held, high_ref, low_ref, span)

        return call(
            body,
            [(wide, F32)],
            (*parts, *blocks["A", level]),
            (ids,),
            [pltpu.VMEM((span, *wide), F32)],
        )

    everything = {top: leaf_swaps(current * leaves)}
    for level in range(top, 1, -1):
        wanted = leaf_swaps(descend(level, everything[level]) * 2 ** (level - 1))
        everything[level - 1] = leaf_swaps(transposed(level - 1, wanted) * 2 ** (level - 1))

    def finish(ids_ref, known_ref, *refs):
        refs = list(refs)
        parts = {level: [refs.pop(0) for _ in range(2**level)] for level in range(1, levels)}
        link_high, link_low, solved_ref, pivot_ref, high_ref, low_ref = refs[:6]
        out, path, held = refs[6:]
        group = ids_ref[0]
        ordered(group % 2, parts[1], held)
        wanted = solved_ref[...] / pivot_ref[0:1, :] - against(held, link_high, link_low, 2)
        lowest = wanted + times(wanted, high_ref[0], low_ref[0], 0)
        owned = [lowest]
        for half in range(halves):
            path[half] = lowest[:, half * TILE : (half + 1) * TILE]
        for level in range(1, levels):
            span = 2**level
            owned.append(parts[level][0][...])
            for offset, ref in enumerate(parts[level]):
                first = (span - 1 + (group % span ^ offset)) * halves
                for half in range(halves):
                    path[first + half] = ref[:, half * TILE : (half + 1) * TILE]
        lane = lax.broadcasted_iota(jnp.int32, (share, TILE), 1)
        for target in range(ranks):
            for tile in range(tiles):
                out[target, :, tile * TILE : (tile + 1) * TILE] = path[known_ref[target, tile]]
            pieces = jnp.zeros((share, TILE), F32)
            for level in range(levels):
                shift = (base + level * piece - target * piece) % base
                turned = pltpu.roll(owned[level], shift, 1)[:, :TILE]
                mine = (lane >= level * piece) & (lane < (level + 1) * piece)
                pieces = jnp.where(mine, turned, pieces)
            out[target, :, tiles * TILE :] = pieces

    replies = call(
        finish,
        [((ranks, share, packed), F32)],
        (
            *[part for level in range(1, levels) for part in everything[level]],
            *blocks["B", 0],
            solved[0],
            pivots,
            *blocks["A", 0],
        ),
        (ids, known),
        [pltpu.VMEM((path_tiles, share, TILE), F32), pltpu.VMEM((2, *wide), F32)],
    )
    back = lax.all_to_all(replies[0], "row", 0, 0, tiled=True).reshape(columns, packed)

    def local_backward(back, solved_ref, pivot_ref, inverse_any, coupling_any, *refs):
        out, window_ref, inverse_ref, coupling_ref, done = refs
        first = pltpu.make_async_copy(coupling_any, coupling_ref, done.at[0])
        second = pltpu.make_async_copy(inverse_any, inverse_ref, done.at[1])
        first.start()
        second.start()
        final = back[:, tiles * TILE :].T
        for level in range(levels):
            window_ref[level] = final[level * piece : (level + 1) * piece]
        scaled = solved_ref[...] / pivot_ref[...]
        first.wait()
        high, low = split(coupling_ref[...])
        remainder = scaled - times(back[:, : tiles * TILE], high.astype(BF16), low.astype(BF16), 0)
        second.wait()
        high, low = split(strict_lower(inverse_ref[...]))
        answer = remainder + times(remainder, high.astype(BF16), low.astype(BF16), 0)
        out[...] = answer.T

    answer, window = call(
        local_backward,
        [((local, columns), F32), ((levels, piece, columns), F32)],
        (back, solved_loc, loc_pivots[0], loc_inverse[0, 0], loc_coupling[0, 0]),
        scratch=[
            pltpu.VMEM((local, local), F32),
            pltpu.VMEM((tiles * TILE, local), F32),
            pltpu.SemaphoreType.DMA((2,)),
        ],
        remote=2,
        work=24 * local * local * columns,
        room=24,
    )
    return answer[None, None], window


def solution(mesh):
    return jax.shard_map(
        shards,
        mesh=mesh,
        in_specs=(
            P("leaf", "row", None, None),
            P("leaf", "row", None, None),
            P("leaf", "row", None, None),
            P("leaf", "row", None),
            P("leaf", "row", None),
            P(None, ("leaf", "row"), None),
            P(None, ("leaf", "row")),
            P("row", None, "leaf"),
            P("row", None, "leaf"),
        ),
        out_specs=(P("leaf", "row", None, None), P(None, ("leaf", "row"), None)),
        check_vma=False,
    )
```

```python
import math

import jax
import jax.numpy as jnp
from jax import lax
from jax.experimental import pallas as pl
from jax.experimental.pallas import tpu as pltpu
from jax.sharding import PartitionSpec as P

TILE = 128
F32 = jnp.float32
BF16 = jnp.bfloat16


def swap(value, axis, count, offset):
    return lax.ppermute(value, axis, [(i, i ^ offset) for i in range(count)])


def ring_order(count):
    return list(range(0, count, 2)) + list(range(count - 1, 0, -2))


def ring_gather(blocks, count, ahead):
    order = ring_order(count)
    right = [(order[i], order[(i + 1) % count]) for i in range(count)]
    left = [(target, source) for source, target in right]
    before = (0, blocks[0].shape[0])
    parts = [(0, before[i], blocks[i]) for i in range(2)]
    forward, backward = list(blocks), list(blocks)
    for step in range(1, count // 2 + 1):
        last = 2 * step == count
        for i in range(2):
            if not last or i == 0:
                forward[i] = lax.ppermute(forward[i], "row", right)
            if not last or i == 1:
                backward[i] = lax.ppermute(backward[i], "row", left)
        if step == 1:
            forward, backward, ahead = lax.optimization_barrier((forward, backward, ahead))
        for i in range(2):
            if not last or i == 0:
                parts.append((-step, before[i], forward[i]))
            if not last or i == 1:
                parts.append((step, before[i], backward[i]))
    return parts, ahead


def call(body, outs, arrays, scalars=(), scratch=(), work=0, remote=0, room=16):
    moved = sum(a.size * a.dtype.itemsize for a in arrays)
    moved += sum(math.prod(shape) * jnp.dtype(kind).itemsize for shape, kind in outs)
    return pl.pallas_call(
        body,
        out_shape=[jax.ShapeDtypeStruct(*o) for o in outs],
        in_specs=[pl.BlockSpec(memory_space=pltpu.SMEM)] * len(scalars)
        + [pl.BlockSpec(memory_space=pltpu.VMEM)] * (len(arrays) - remote)
        + [pl.BlockSpec(memory_space=pltpu.HBM)] * remote,
        out_specs=[pl.BlockSpec(memory_space=pltpu.VMEM)] * len(outs),
        scratch_shapes=list(scratch),
        compiler_params=pltpu.CompilerParams(vmem_limit_bytes=room << 20),
        cost_estimate=pl.CostEstimate(flops=work, bytes_accessed=moved, transcendentals=0),
    )(*scalars, *arrays)


def split(value):
    high = value.astype(BF16).astype(F32)
    return high, value - high


def times(value, high, low, right_dim):
    rows = value.shape[0]
    dims = (((1,), (right_dim,)), ((), ()))

    def product(part):
        return lax.dot_general(part, high, dims, preferred_element_type=F32) + lax.dot_general(
            part, low, dims, preferred_element_type=F32
        )

    first, second = split(value)
    if rows % 8:
        return product(first.astype(BF16)) + product(second.astype(BF16))
    both = product(jnp.concatenate([first, second], 0).astype(BF16))
    return both[:rows] + both[rows:]


def times_left(block, value):
    columns = value.shape[1]
    both = jnp.concatenate(split(value), 1).astype(BF16)
    product = sum(
        jnp.dot(part.astype(BF16), both, preferred_element_type=F32) for part in split(block)
    )
    return product[:, :columns] + product[:, columns:]


def strict_lower(block):
    row_ids = lax.broadcasted_iota(jnp.int32, block.shape, 0)
    col_ids = lax.broadcasted_iota(jnp.int32, block.shape, 1)
    return jnp.where(col_ids < row_ids, block, 0.0)


def shards(
    loc_rhs,
    loc_inverse,
    loc_coupling,
    loc_pivots,
    pattern,
    win_rhs,
    win_pivots,
    win_inverse,
    win_coupling,
):
    leaves = lax.axis_size("leaf")
    ranks = lax.axis_size("row")
    leaf = lax.axis_index("leaf")
    rank = lax.axis_index("row")
    levels, piece, columns = win_rhs.shape
    base = piece * ranks
    share = columns // ranks
    halves = base // TILE
    path_tiles = (2 * leaves - 1) * halves
    tiles = pattern.shape[2]
    local = loc_rhs.shape[2]
    top = levels - 1
    ids = jnp.stack([leaf, rank]).astype(jnp.int32)
    wide = (share, base)

    def leaf_swaps(values):
        return [values[0]] + [swap(v, "leaf", leaves, j) for j, v in enumerate(values) if j]

    def source_row(me, step):
        place = jnp.where(me % 2 == 0, me // 2, ranks - 1 - me // 2)
        place = (place + step + ranks) % ranks
        return jnp.where(2 * place < ranks, 2 * place, 2 * (ranks - 1 - place) + 1)

    def width(name):
        return 2 ** name[1] if name[0] == "A" else 2 ** (name[1] + 1)

    all_names = [("A", level) for level in range(levels)] + [("B", level) for level in range(top)]

    def runs(names):
        found, slot, place = [], 0, 0
        for name in all_names:
            if name in names:
                if found and found[-1][1] == slot:
                    found[-1][1] += width(name)
                else:
                    found.append([slot, slot + width(name), place])
                place += width(name)
            slot += width(name)
        return found

    def assemble(names):
        names = [name for name in all_names if name in names]
        spans = [width(name) for name in names]
        moves = []
        for index, (step, before, part) in enumerate(parts):
            for first, end, place in runs(names):
                low, high = max(first, before), min(end, before + part.shape[0])
                if low < high:
                    moves.append((index, step, low - before, high - before, place + low - first))

        def body(ids_ref, *refs):
            parts_refs, outs = refs[: len(parts)], refs[len(parts) : -2]
            natural, done = refs[-2:]
            group = ids_ref[0]
            copies = []
            for number, (index, step, low, high, place) in enumerate(moves):
                start = pl.multiple_of(source_row(ids_ref[1], step) * piece, 8)
                copies.append(
                    pltpu.make_async_copy(
                        parts_refs[index].at[low:high],
                        natural.at[place : place + high - low, pl.ds(start, piece), :],
                        done.at[number],
                    )
                )
            for copy in copies:
                copy.start()
            for copy in copies:
                copy.wait()
            first = 0
            for index, ((kind, level), span) in enumerate(zip(names, spans)):
                for slot in range(span):
                    block = natural[first + slot]
                    if kind == "A":
                        row_ids = lax.broadcasted_iota(jnp.int32, block.shape, 0) + slot * base
                        col_ids = lax.broadcasted_iota(jnp.int32, block.shape, 1)
                        col_ids = col_ids + group % span * base
                        block = jnp.where(col_ids < row_ids, block, 0.0)
                    high, low = split(block)
                    outs[2 * index][slot] = high.astype(BF16)
                    outs[2 * index + 1][slot] = low.astype(BF16)
                first += span

        outs = [((span, base, base), BF16) for span in spans for _ in range(2)]
        made = call(
            body,
            outs,
            [part for _, _, part in parts],
            (ids,),
            [pltpu.VMEM((sum(spans), base, base), F32), pltpu.SemaphoreType.DMA((len(moves),))],
            remote=len(parts),
            room=24,
        )
        return {name: made[2 * i : 2 * i + 2] for i, name in enumerate(names)}

    start = levels * piece
    beside = start + piece + tiles <= TILE
    number_row, number_lane = (0, start + piece) if beside else (levels, start)
    aux = jnp.zeros((share, TILE), F32)
    aux = lax.dynamic_update_slice(aux, win_pivots, (0, start))
    aux = lax.dynamic_update_slice(aux, pattern[0].astype(F32), (number_row, number_lane))
    aux = jnp.tile(aux, (ranks, 1))
    packed = tiles * TILE + TILE

    def local_forward(rhs_ref, window_ref, aux_ref, inverse_any, coupling_any, *refs):
        solved_ref, terms_ref, held, inverse_ref, coupling_ref, done = refs
        first = pltpu.make_async_copy(inverse_any, inverse_ref, done.at[0])
        second = pltpu.make_async_copy(coupling_any, coupling_ref, done.at[1])
        first.start()
        second.start()
        rhs = rhs_ref[...]
        held[...] = jnp.zeros_like(held)
        for level in range(levels):
            held[level * piece : (level + 1) * piece, :] = window_ref[level]
        terms_ref[:, tiles * TILE :] = held[...].T + aux_ref[...]
        first.wait()
        solved = rhs + times_left(strict_lower(inverse_ref[...]), rhs)
        solved_ref[...] = solved.T
        second.wait()
        terms_ref[:, : tiles * TILE] = times_left(coupling_ref[...], solved).T

    solved_loc, terms = call(
        local_forward,
        [((columns, local), F32), ((columns, packed), F32)],
        (loc_rhs[0, 0], win_rhs, aux, loc_inverse[0, 0], loc_coupling[0, 0]),
        remote=2,
        scratch=[
            pltpu.VMEM((TILE, columns), F32),
            pltpu.VMEM((local, local), F32),
            pltpu.VMEM((tiles * TILE, local), F32),
            pltpu.SemaphoreType.DMA((2,)),
        ],
        work=24 * local * local * columns,
        room=24,
    )
    parts, terms = ring_gather(
        [win_inverse[0].reshape(-1, piece, base), win_coupling[0].reshape(-1, piece, base)],
        ranks,
        terms,
    )
    terms = lax.all_to_all(terms.reshape(ranks, share, packed), "row", 0, 0, tiled=True)
    number_lane += tiles * TILE
    known = terms[:, number_row, number_lane : number_lane + tiles].astype(jnp.int32)

    lower = assemble([name for name in all_names if name != ("A", top)])
    upper = assemble([("A", top)])
    blocks = {**lower, **upper}

    def scatter(ids_ref, known_ref, terms_ref, *refs):
        outs, pivots_ref, path = refs[:-2], refs[-2], refs[-1]
        lane = lax.broadcasted_iota(jnp.int32, (share, TILE), 1)
        path[...] = jnp.zeros_like(path)
        for source in range(ranks):
            for tile in range(tiles):
                place = known_ref[source, tile]
                path[place] = path[place] - terms_ref[source, :, tile * TILE : (tile + 1) * TILE]

        def spread(first):
            rows = []
            for half in range(halves):
                row = jnp.zeros((share, TILE), F32)
                for source in range(half * TILE // piece, (half + 1) * TILE // piece):
                    place = source * piece % TILE
                    shift = (TILE + place - first) % TILE
                    turned = pltpu.roll(terms_ref[source, :, tiles * TILE :], shift, 1)
                    row = jnp.where((lane >= place) & (lane < place + piece), turned, row)
                rows.append(row)
            return jnp.concatenate(rows, 1)

        pivots_ref[...] = spread(levels * piece)
        for level in range(levels):
            span = 2**level
            filled = outs[level]
            for slot in range(span):
                first = (span - 1 + slot) * halves
                for half in range(halves):
                    filled[slot, :, half * TILE : (half + 1) * TILE] = path[first + half]
            own = ids_ref[0] % span
            filled[own] = filled[own] + spread(level * piece)

    *rest, pivots = call(
        scatter,
        [((2**level, *wide), F32) for level in range(levels)] + [(wide, F32)],
        (terms,),
        (ids, known),
        [pltpu.VMEM((path_tiles, share, TILE), F32)],
    )

    all_pivots = leaf_swaps([pivots] * leaves)

    def total(refs):
        value = refs[0][0] if len(refs[0].shape) > len(wide) and len(refs) == 1 else refs[0][...]
        for ref in refs[1:]:
            value = value + ref[...]
        return value

    def diagonal(level, chunks, ahead=()):
        span = 2**level
        high, low = blocks["A", level]

        def body(ids_ref, *refs):
            chunk_refs, (high_ref, low_ref) = refs[:span], refs[span : span + 2]
            outs, parts = refs[span + 2 + len(ahead) : -1], refs[-1]
            own = ids_ref[0] % span
            value = total(chunk_refs)
            for slot in range(span):
                parts[slot] = times(value, high_ref[slot], low_ref[slot], 1)
            parts[own] = parts[own] + value
            if level == top:
                outs[0][...] = parts[...]
            else:
                for offset, out in enumerate(outs):
                    out[...] = parts[own ^ offset]

        outs = [((span, *wide), F32)] if level == top else [(wide, F32)] * span
        return call(
            body,
            outs,
            (*chunks, high, low, *ahead),
            (ids,),
            [pltpu.VMEM((span, *wide), F32)],
        )

    def link(level, chunks):
        span, above = 2**level, 2 ** (level + 1)
        high, low = blocks["B", level]
        lowest = () if level else blocks["A", 0]

        def body(ids_ref, *refs):
            chunk_refs, refs = refs[:span], refs[span:]
            value = total(chunk_refs)
            if lowest:
                value = value + times(value, refs[0][0], refs[1][0], 1)
                refs = refs[2:]
            high_ref, low_ref, rest_ref, solved_ref = refs[:4]
            outs, parts = refs[4:-1], refs[-1]
            solved_ref[...] = value
            for slot in range(above):
                parts[slot] = rest_ref[slot] - times(value, high_ref[slot], low_ref[slot], 1)
            own = ids_ref[0] % above
            for offset, out in enumerate(outs):
                out[...] = parts[own ^ offset]

        made = call(
            body,
            [(wide, F32)] * (above + 1),
            (*chunks, *lowest, high, low, rest[level + 1]),
            (ids,),
            [pltpu.VMEM((above, *wide), F32)],
        )
        return made[0], made[1:]

    chunks = [rest[0]]
    solved = []
    for level in range(top):
        if level:
            chunks = leaf_swaps(diagonal(level, chunks, all_pivots if level == 1 else ()))
        value, chunks = link(level, chunks)
        solved.append(value)
        chunks = leaf_swaps(chunks)
    sums = leaf_swaps(diagonal(top, chunks) * leaves)

    def peak(ids_ref, *refs):
        sum_refs, pivot_refs = refs[:leaves], refs[leaves : 2 * leaves]
        high_ref, low_ref, out, wanted = refs[2 * leaves :]
        own = ids_ref[0] % leaves
        wanted[...] = total(sum_refs)
        for offset, ref in enumerate(pivot_refs):
            wanted[own ^ offset] = wanted[own ^ offset] / ref[top : top + 1, :]
        value = wanted[own]
        for slot in range(leaves):
            value = value + times(wanted[slot], high_ref[slot], low_ref[slot], 0)
        out[...] = value

    current = call(
        peak,
        [(wide, F32)],
        (*sums, *all_pivots, *blocks["A", top]),
        (ids,),
        [pltpu.VMEM((leaves, *wide), F32)],
    )

    def ordered(own, refs, held):
        for offset, ref in enumerate(refs):
            held[own ^ offset] = ref[...]

    def against(held, high_ref, low_ref, span):
        value = times(held[0], high_ref[0], low_ref[0], 0)
        for slot in range(1, span):
            value = value + times(held[slot], high_ref[slot], low_ref[slot], 0)
        return value

    def descend(level, parts):
        span = 2**level

        def body(ids_ref, *refs):
            part_refs = refs[:span]
            high_ref, low_ref, solved_ref, pivot_ref, out, held = refs[span:]
            ordered(ids_ref[0] % span, part_refs, held)
            above = against(held, high_ref, low_ref, span)
            out[...] = solved_ref[...] / pivot_ref[level - 1 : level, :] - above

        return call(
            body,
            [(wide, F32)],
            (*parts, *blocks["B", level - 1], solved[level - 1], pivots),
            (ids,),
            [pltpu.VMEM((span, *wide), F32)],
        )

    def transposed(level, parts):
        span = 2**level

        def body(ids_ref, *refs):
            part_refs = refs[:span]
            high_ref, low_ref, out, held = refs[span:]
            ordered(ids_ref[0] % span, part_refs, held)
            out[...] = part_refs[0][...] + against(held, high_ref, low_ref, span)

        return call(
            body,
            [(wide, F32)],
            (*parts, *blocks["A", level]),
            (ids,),
            [pltpu.VMEM((span, *wide), F32)],
        )

    everything = {top: leaf_swaps(current * leaves)}
    for level in range(top, 1, -1):
        wanted = leaf_swaps(descend(level, everything[level]) * 2 ** (level - 1))
        everything[level - 1] = leaf_swaps(transposed(level - 1, wanted) * 2 ** (level - 1))

    def finish(ids_ref, known_ref, *refs):
        refs = list(refs)
        parts = {level: [refs.pop(0) for _ in range(2**level)] for level in range(1, levels)}
        link_high, link_low, solved_ref, pivot_ref, high_ref, low_ref = refs[:6]
        out, path, held = refs[6:]
        group = ids_ref[0]
        ordered(group % 2, parts[1], held)
        wanted = solved_ref[...] / pivot_ref[0:1, :] - against(held, link_high, link_low, 2)
        lowest = wanted + times(wanted, high_ref[0], low_ref[0], 0)
        owned = [lowest]
        for half in range(halves):
            path[half] = lowest[:, half * TILE : (half + 1) * TILE]
        for level in range(1, levels):
            span = 2**level
            owned.append(parts[level][0][...])
            for offset, ref in enumerate(parts[level]):
                first = (span - 1 + (group % span ^ offset)) * halves
                for half in range(halves):
                    path[first + half] = ref[:, half * TILE : (half + 1) * TILE]
        lane = lax.broadcasted_iota(jnp.int32, (share, TILE), 1)
        for target in range(ranks):
            for tile in range(tiles):
                out[target, :, tile * TILE : (tile + 1) * TILE] = path[known_ref[target, tile]]
            pieces = jnp.zeros((share, TILE), F32)
            for level in range(levels):
                shift = (base + level * piece - target * piece) % base
                turned = pltpu.roll(owned[level], shift, 1)[:, :TILE]
                mine = (lane >= level * piece) & (lane < (level + 1) * piece)
                pieces = jnp.where(mine, turned, pieces)
            out[target, :, tiles * TILE :] = pieces

    replies = call(
        finish,
        [((ranks, share, packed), F32)],
        (
            *[part for level in range(1, levels) for part in everything[level]],
            *blocks["B", 0],
            solved[0],
            pivots,
            *blocks["A", 0],
        ),
        (ids, known),
        [pltpu.VMEM((path_tiles, share, TILE), F32), pltpu.VMEM((2, *wide), F32)],
    )
    back = lax.all_to_all(replies[0], "row", 0, 0, tiled=True).reshape(columns, packed)

    def local_backward(back, solved_ref, pivot_ref, inverse_any, coupling_any, *refs):
        out, window_ref, inverse_ref, coupling_ref, done = refs
        first = pltpu.make_async_copy(coupling_any, coupling_ref, done.at[0])
        second = pltpu.make_async_copy(inverse_any, inverse_ref, done.at[1])
        first.start()
        second.start()
        final = back[:, tiles * TILE :].T
        for level in range(levels):
            window_ref[level] = final[level * piece : (level + 1) * piece]
        scaled = solved_ref[...] / pivot_ref[...]
        first.wait()
        high, low = split(coupling_ref[...])
        remainder = scaled - times(back[:, : tiles * TILE], high.astype(BF16), low.astype(BF16), 0)
        second.wait()
        high, low = split(strict_lower(inverse_ref[...]))
        answer = remainder + times(remainder, high.astype(BF16), low.astype(BF16), 0)
        out[...] = answer.T

    answer, window = call(
        local_backward,
        [((local, columns), F32), ((levels, piece, columns), F32)],
        (back, solved_loc, loc_pivots[0], loc_inverse[0, 0], loc_coupling[0, 0]),
        scratch=[
            pltpu.VMEM((local, local), F32),
            pltpu.VMEM((tiles * TILE, local), F32),
            pltpu.SemaphoreType.DMA((2,)),
        ],
        remote=2,
        work=24 * local * local * columns,
        room=24,
    )
    return answer[None, None], window


def solution(mesh):
    return jax.shard_map(
        shards,
        mesh=mesh,
        in_specs=(
            P("leaf", "row", None, None),
            P("leaf", "row", None, None),
            P("leaf", "row", None, None),
            P("leaf", "row", None),
            P("leaf", "row", None),
            P(None, ("leaf", "row"), None),
            P(None, ("leaf", "row")),
            P("row", None, "leaf"),
            P("row", None, "leaf"),
        ),
        out_specs=(P("leaf", "row", None, None), P(None, ("leaf", "row"), None)),
        check_vma=False,
    )
```

```python
import math

import jax
import jax.numpy as jnp
from jax import lax
from jax.experimental import pallas as pl
from jax.experimental.pallas import tpu as pltpu
from jax.sharding import PartitionSpec as P

TILE = 128
F32 = jnp.float32
BF16 = jnp.bfloat16


def swap(value, axis, count, offset):
    return lax.ppermute(value, axis, [(i, i ^ offset) for i in range(count)])


def ring_order(count):
    return list(range(0, count, 2)) + list(range(count - 1, 0, -2))


def ring_gather(block, count, ahead):
    order = ring_order(count)
    right = [(order[i], order[(i + 1) % count]) for i in range(count)]
    left = [(target, source) for source, target in right]
    parts = [(0, 0, block)]
    forward = backward = block
    middle = block.shape[0] // 2
    for step in range(1, count // 2 + 1):
        first = 0
        if 2 * step == count:
            forward, backward, first = forward[:middle], backward[middle:], middle
        forward = lax.ppermute(forward, "row", right)
        backward = lax.ppermute(backward, "row", left)
        if step == 1:
            forward, backward, _ = lax.optimization_barrier((forward, backward, ahead))
        parts += [(-step, 0, forward), (step, first, backward)]
    return parts


def call(body, outs, arrays, scalars=(), scratch=(), work=0, remote=0, room=16):
    moved = sum(a.size * a.dtype.itemsize for a in arrays)
    moved += sum(math.prod(shape) * jnp.dtype(kind).itemsize for shape, kind in outs)
    return pl.pallas_call(
        body,
        out_shape=[jax.ShapeDtypeStruct(*o) for o in outs],
        in_specs=[pl.BlockSpec(memory_space=pltpu.SMEM)] * len(scalars)
        + [pl.BlockSpec(memory_space=pltpu.VMEM)] * (len(arrays) - remote)
        + [pl.BlockSpec(memory_space=pltpu.HBM)] * remote,
        out_specs=[pl.BlockSpec(memory_space=pltpu.VMEM)] * len(outs),
        scratch_shapes=list(scratch),
        compiler_params=pltpu.CompilerParams(vmem_limit_bytes=room << 20),
        cost_estimate=pl.CostEstimate(flops=work, bytes_accessed=moved, transcendentals=0),
    )(*scalars, *arrays)


def split(value):
    high = value.astype(BF16).astype(F32)
    return high, value - high


def times(value, high, low, right_dim):
    rows = value.shape[0]
    dims = (((1,), (right_dim,)), ((), ()))

    def product(part):
        return lax.dot_general(part, high, dims, preferred_element_type=F32) + lax.dot_general(
            part, low, dims, preferred_element_type=F32
        )

    first, second = split(value)
    if rows % 8:
        return product(first.astype(BF16)) + product(second.astype(BF16))
    both = product(jnp.concatenate([first, second], 0).astype(BF16))
    return both[:rows] + both[rows:]


def times_left(block, value):
    columns = value.shape[1]
    both = jnp.concatenate(split(value), 1).astype(BF16)
    product = sum(
        jnp.dot(part.astype(BF16), both, preferred_element_type=F32) for part in split(block)
    )
    return product[:, :columns] + product[:, columns:]


def strict_lower(block):
    row_ids = lax.broadcasted_iota(jnp.int32, block.shape, 0)
    col_ids = lax.broadcasted_iota(jnp.int32, block.shape, 1)
    return jnp.where(col_ids < row_ids, block, 0.0)


def shards(
    loc_rhs,
    loc_inverse,
    loc_coupling,
    loc_pivots,
    pattern,
    win_rhs,
    win_pivots,
    win_inverse,
    win_coupling,
):
    leaves = lax.axis_size("leaf")
    ranks = lax.axis_size("row")
    leaf = lax.axis_index("leaf")
    rank = lax.axis_index("row")
    levels, piece, columns = win_rhs.shape
    base = piece * ranks
    share = columns // ranks
    halves = base // TILE
    path_tiles = (2 * leaves - 1) * halves
    tiles = pattern.shape[2]
    local = loc_rhs.shape[2]
    top = levels - 1
    ids = jnp.stack([leaf, rank]).astype(jnp.int32)
    wide = (share, base)

    def leaf_swaps(values):
        return [values[0]] + [swap(v, "leaf", leaves, j) for j, v in enumerate(values) if j]

    def source_row(me, step):
        place = jnp.where(me % 2 == 0, me // 2, ranks - 1 - me // 2)
        place = (place + step + ranks) % ranks
        return jnp.where(2 * place < ranks, 2 * place, 2 * (ranks - 1 - place) + 1)

    def width(name):
        return 2 ** name[1] if name[0] == "A" else 2 ** (name[1] + 1)

    all_names = [("A", level) for level in range(levels)] + [("B", level) for level in range(top)]

    def runs(names):
        found, slot, place = [], 0, 0
        for name in all_names:
            if name in names:
                if found and found[-1][1] == slot:
                    found[-1][1] += width(name)
                else:
                    found.append([slot, slot + width(name), place])
                place += width(name)
            slot += width(name)
        return found

    def assemble(names):
        names = [name for name in all_names if name in names]
        spans = [width(name) for name in names]
        moves = []
        for index, (step, before, part) in enumerate(parts):
            for first, end, place in runs(names):
                low, high = max(first, before), min(end, before + part.shape[0])
                if low < high:
                    moves.append((index, step, low - before, high - before, place + low - first))

        def body(ids_ref, *refs):
            parts_refs, outs = refs[: len(parts)], refs[len(parts) : -2]
            natural, done = refs[-2:]
            group = ids_ref[0]
            copies = []
            for number, (index, step, low, high, place) in enumerate(moves):
                start = pl.multiple_of(source_row(ids_ref[1], step) * piece, 8)
                copies.append(
                    pltpu.make_async_copy(
                        parts_refs[index].at[low:high],
                        natural.at[place : place + high - low, pl.ds(start, piece), :],
                        done.at[number],
                    )
                )
            for copy in copies:
                copy.start()
            for copy in copies:
                copy.wait()
            first = 0
            for index, ((kind, level), span) in enumerate(zip(names, spans)):
                for slot in range(span):
                    block = natural[first + slot]
                    if kind == "A":
                        row_ids = lax.broadcasted_iota(jnp.int32, block.shape, 0) + slot * base
                        col_ids = lax.broadcasted_iota(jnp.int32, block.shape, 1)
                        col_ids = col_ids + group % span * base
                        block = jnp.where(col_ids < row_ids, block, 0.0)
                    high, low = split(block)
                    outs[2 * index][slot] = high.astype(BF16)
                    outs[2 * index + 1][slot] = low.astype(BF16)
                first += span

        outs = [((span, base, base), BF16) for span in spans for _ in range(2)]
        made = call(
            body,
            outs,
            [part for _, _, part in parts],
            (ids,),
            [pltpu.VMEM((sum(spans), base, base), F32), pltpu.SemaphoreType.DMA((len(moves),))],
            remote=len(parts),
            room=24,
        )
        return {name: made[2 * i : 2 * i + 2] for i, name in enumerate(names)}

    start = levels * piece
    beside = start + piece + tiles <= TILE
    number_row, number_lane = (0, start + piece) if beside else (levels, start)
    aux = jnp.zeros((share, TILE), F32)
    aux = lax.dynamic_update_slice(aux, win_pivots, (0, start))
    aux = lax.dynamic_update_slice(aux, pattern[0].astype(F32), (number_row, number_lane))
    aux = jnp.tile(aux, (ranks, 1))
    packed = tiles * TILE + TILE

    def local_forward(rhs_ref, window_ref, aux_ref, inverse_any, coupling_any, *refs):
        solved_ref, terms_ref, held, inverse_ref, coupling_ref, done = refs
        first = pltpu.make_async_copy(inverse_any, inverse_ref, done.at[0])
        second = pltpu.make_async_copy(coupling_any, coupling_ref, done.at[1])
        first.start()
        second.start()
        rhs = rhs_ref[...]
        held[...] = jnp.zeros_like(held)
        for level in range(levels):
            held[level * piece : (level + 1) * piece, :] = window_ref[level]
        terms_ref[:, tiles * TILE :] = held[...].T + aux_ref[...]
        first.wait()
        solved = rhs + times_left(strict_lower(inverse_ref[...]), rhs)
        solved_ref[...] = solved.T
        second.wait()
        terms_ref[:, : tiles * TILE] = times_left(coupling_ref[...], solved).T

    solved_loc, terms = call(
        local_forward,
        [((columns, local), F32), ((columns, packed), F32)],
        (loc_rhs[0, 0], win_rhs, aux, loc_inverse[0, 0], loc_coupling[0, 0]),
        remote=2,
        scratch=[
            pltpu.VMEM((TILE, columns), F32),
            pltpu.VMEM((local, local), F32),
            pltpu.VMEM((tiles * TILE, local), F32),
            pltpu.SemaphoreType.DMA((2,)),
        ],
        work=24 * local * local * columns,
        room=24,
    )
    parts = ring_gather(
        jnp.concatenate([win_inverse[0], win_coupling[0]], 0).reshape(-1, piece, base),
        ranks,
        terms,
    )
    terms = lax.all_to_all(terms.reshape(ranks, share, packed), "row", 0, 0, tiled=True)
    number_lane += tiles * TILE
    known = terms[:, number_row, number_lane : number_lane + tiles].astype(jnp.int32)

    blocks = assemble([("A", 0), ("B", 0)])
    for name in all_names:
        if name not in blocks:
            blocks.update(assemble([name]))

    def scatter(ids_ref, known_ref, terms_ref, *refs):
        outs, pivots_ref, path = refs[:-2], refs[-2], refs[-1]
        lane = lax.broadcasted_iota(jnp.int32, (share, TILE), 1)
        path[...] = jnp.zeros_like(path)
        for source in range(ranks):
            for tile in range(tiles):
                place = known_ref[source, tile]
                path[place] = path[place] - terms_ref[source, :, tile * TILE : (tile + 1) * TILE]

        def spread(first):
            rows = []
            for half in range(halves):
                row = jnp.zeros((share, TILE), F32)
                for source in range(half * TILE // piece, (half + 1) * TILE // piece):
                    place = source * piece % TILE
                    shift = (TILE + place - first) % TILE
                    turned = pltpu.roll(terms_ref[source, :, tiles * TILE :], shift, 1)
                    row = jnp.where((lane >= place) & (lane < place + piece), turned, row)
                rows.append(row)
            return jnp.concatenate(rows, 1)

        pivots_ref[...] = spread(levels * piece)
        for level in range(levels):
            span = 2**level
            filled = outs[level]
            for slot in range(span):
                first = (span - 1 + slot) * halves
                for half in range(halves):
                    filled[slot, :, half * TILE : (half + 1) * TILE] = path[first + half]
            own = ids_ref[0] % span
            filled[own] = filled[own] + spread(level * piece)

    *rest, pivots = call(
        scatter,
        [((2**level, *wide), F32) for level in range(levels)] + [(wide, F32)],
        (terms,),
        (ids, known),
        [pltpu.VMEM((path_tiles, share, TILE), F32)],
    )

    all_pivots = leaf_swaps([pivots] * leaves)

    def total(refs):
        value = refs[0][0] if len(refs[0].shape) > len(wide) and len(refs) == 1 else refs[0][...]
        for ref in refs[1:]:
            value = value + ref[...]
        return value

    def diagonal(level, chunks, ahead=()):
        span = 2**level
        high, low = blocks["A", level]

        def body(ids_ref, *refs):
            chunk_refs, (high_ref, low_ref) = refs[:span], refs[span : span + 2]
            outs, parts = refs[span + 2 + len(ahead) : -1], refs[-1]
            own = ids_ref[0] % span
            value = total(chunk_refs)
            for slot in range(span):
                parts[slot] = times(value, high_ref[slot], low_ref[slot], 1)
            parts[own] = parts[own] + value
            if level == top:
                outs[0][...] = parts[...]
            else:
                for offset, out in enumerate(outs):
                    out[...] = parts[own ^ offset]

        outs = [((span, *wide), F32)] if level == top else [(wide, F32)] * span
        return call(
            body,
            outs,
            (*chunks, high, low, *ahead),
            (ids,),
            [pltpu.VMEM((span, *wide), F32)],
        )

    def link(level, chunks):
        span, above = 2**level, 2 ** (level + 1)
        high, low = blocks["B", level]
        lowest = () if level else blocks["A", 0]

        def body(ids_ref, *refs):
            chunk_refs, refs = refs[:span], refs[span:]
            value = total(chunk_refs)
            if lowest:
                value = value + times(value, refs[0][0], refs[1][0], 1)
                refs = refs[2:]
            high_ref, low_ref, rest_ref, solved_ref = refs[:4]
            outs, parts = refs[4:-1], refs[-1]
            solved_ref[...] = value
            for slot in range(above):
                parts[slot] = rest_ref[slot] - times(value, high_ref[slot], low_ref[slot], 1)
            own = ids_ref[0] % above
            for offset, out in enumerate(outs):
                out[...] = parts[own ^ offset]

        made = call(
            body,
            [(wide, F32)] * (above + 1),
            (*chunks, *lowest, high, low, rest[level + 1]),
            (ids,),
            [pltpu.VMEM((above, *wide), F32)],
        )
        return made[0], made[1:]

    chunks = [rest[0]]
    solved = []
    for level in range(top):
        if level:
            chunks = leaf_swaps(diagonal(level, chunks, all_pivots if level == 1 else ()))
        value, chunks = link(level, chunks)
        solved.append(value)
        chunks = leaf_swaps(chunks)
    sums = leaf_swaps(diagonal(top, chunks) * leaves)

    def peak(ids_ref, *refs):
        sum_refs, pivot_refs = refs[:leaves], refs[leaves : 2 * leaves]
        high_ref, low_ref, out, wanted = refs[2 * leaves :]
        own = ids_ref[0] % leaves
        wanted[...] = total(sum_refs)
        for offset, ref in enumerate(pivot_refs):
            wanted[own ^ offset] = wanted[own ^ offset] / ref[top : top + 1, :]
        value = wanted[own]
        for slot in range(leaves):
            value = value + times(wanted[slot], high_ref[slot], low_ref[slot], 0)
        out[...] = value

    current = call(
        peak,
        [(wide, F32)],
        (*sums, *all_pivots, *blocks["A", top]),
        (ids,),
        [pltpu.VMEM((leaves, *wide), F32)],
    )

    def ordered(own, refs, held):
        for offset, ref in enumerate(refs):
            held[own ^ offset] = ref[...]

    def against(held, high_ref, low_ref, span):
        value = times(held[0], high_ref[0], low_ref[0], 0)
        for slot in range(1, span):
            value = value + times(held[slot], high_ref[slot], low_ref[slot], 0)
        return value

    def descend(level, parts):
        span = 2**level

        def body(ids_ref, *refs):
            part_refs = refs[:span]
            high_ref, low_ref, solved_ref, pivot_ref, out, held = refs[span:]
            ordered(ids_ref[0] % span, part_refs, held)
            above = against(held, high_ref, low_ref, span)
            out[...] = solved_ref[...] / pivot_ref[level - 1 : level, :] - above

        return call(
            body,
            [(wide, F32)],
            (*parts, *blocks["B", level - 1], solved[level - 1], pivots),
            (ids,),
            [pltpu.VMEM((span, *wide), F32)],
        )

    def transposed(level, parts):
        span = 2**level

        def body(ids_ref, *refs):
            part_refs = refs[:span]
            high_ref, low_ref, out, held = refs[span:]
            ordered(ids_ref[0] % span, part_refs, held)
            out[...] = part_refs[0][...] + against(held, high_ref, low_ref, span)

        return call(
            body,
            [(wide, F32)],
            (*parts, *blocks["A", level]),
            (ids,),
            [pltpu.VMEM((span, *wide), F32)],
        )

    everything = {top: leaf_swaps(current * leaves)}
    for level in range(top, 1, -1):
        wanted = leaf_swaps(descend(level, everything[level]) * 2 ** (level - 1))
        everything[level - 1] = leaf_swaps(transposed(level - 1, wanted) * 2 ** (level - 1))

    def finish(ids_ref, known_ref, *refs):
        refs = list(refs)
        parts = {level: [refs.pop(0) for _ in range(2**level)] for level in range(1, levels)}
        link_high, link_low, solved_ref, pivot_ref, high_ref, low_ref = refs[:6]
        out, path, held = refs[6:]
        group = ids_ref[0]
        ordered(group % 2, parts[1], held)
        wanted = solved_ref[...] / pivot_ref[0:1, :] - against(held, link_high, link_low, 2)
        lowest = wanted + times(wanted, high_ref[0], low_ref[0], 0)
        owned = [lowest]
        for half in range(halves):
            path[half] = lowest[:, half * TILE : (half + 1) * TILE]
        for level in range(1, levels):
            span = 2**level
            owned.append(parts[level][0][...])
            for offset, ref in enumerate(parts[level]):
                first = (span - 1 + (group % span ^ offset)) * halves
                for half in range(halves):
                    path[first + half] = ref[:, half * TILE : (half + 1) * TILE]
        lane = lax.broadcasted_iota(jnp.int32, (share, TILE), 1)
        for target in range(ranks):
            for tile in range(tiles):
                out[target, :, tile * TILE : (tile + 1) * TILE] = path[known_ref[target, tile]]
            pieces = jnp.zeros((share, TILE), F32)
            for level in range(levels):
                shift = (base + level * piece - target * piece) % base
                turned = pltpu.roll(owned[level], shift, 1)[:, :TILE]
                mine = (lane >= level * piece) & (lane < (level + 1) * piece)
                pieces = jnp.where(mine, turned, pieces)
            out[target, :, tiles * TILE :] = pieces

    replies = call(
        finish,
        [((ranks, share, packed), F32)],
        (
            *[part for level in range(1, levels) for part in everything[level]],
            *blocks["B", 0],
            solved[0],
            pivots,
            *blocks["A", 0],
        ),
        (ids, known),
        [pltpu.VMEM((path_tiles, share, TILE), F32), pltpu.VMEM((2, *wide), F32)],
    )
    back = lax.all_to_all(replies[0], "row", 0, 0, tiled=True).reshape(columns, packed)

    def local_backward(back, solved_ref, pivot_ref, inverse_any, coupling_any, *refs):
        out, window_ref, inverse_ref, coupling_ref, done = refs
        first = pltpu.make_async_copy(coupling_any, coupling_ref, done.at[0])
        second = pltpu.make_async_copy(inverse_any, inverse_ref, done.at[1])
        first.start()
        second.start()
        final = back[:, tiles * TILE :].T
        for level in range(levels):
            window_ref[level] = final[level * piece : (level + 1) * piece]
        scaled = solved_ref[...] / pivot_ref[...]
        first.wait()
        high, low = split(coupling_ref[...])
        remainder = scaled - times(back[:, : tiles * TILE], high.astype(BF16), low.astype(BF16), 0)
        second.wait()
        high, low = split(strict_lower(inverse_ref[...]))
        answer = remainder + times(remainder, high.astype(BF16), low.astype(BF16), 0)
        out[...] = answer.T

    answer, window = call(
        local_backward,
        [((local, columns), F32), ((levels, piece, columns), F32)],
        (back, solved_loc, loc_pivots[0], loc_inverse[0, 0], loc_coupling[0, 0]),
        scratch=[
            pltpu.VMEM((local, local), F32),
            pltpu.VMEM((tiles * TILE, local), F32),
            pltpu.SemaphoreType.DMA((2,)),
        ],
        remote=2,
        work=24 * local * local * columns,
        room=24,
    )
    return answer[None, None], window


def solution(mesh):
    return jax.shard_map(
        shards,
        mesh=mesh,
        in_specs=(
            P("leaf", "row", None, None),
            P("leaf", "row", None, None),
            P("leaf", "row", None, None),
            P("leaf", "row", None),
            P("leaf", "row", None),
            P(None, ("leaf", "row"), None),
            P(None, ("leaf", "row")),
            P("row", None, "leaf"),
            P("row", None, "leaf"),
        ),
        out_specs=(P("leaf", "row", None, None), P(None, ("leaf", "row"), None)),
        check_vma=False,
    )
```

```python
import math

import jax
import jax.numpy as jnp
from jax import lax
from jax.experimental import pallas as pl
from jax.experimental.pallas import tpu as pltpu
from jax.sharding import PartitionSpec as P

TILE = 128
F32 = jnp.float32
BF16 = jnp.bfloat16


def swap(value, axis, count, offset):
    return lax.ppermute(value, axis, [(i, i ^ offset) for i in range(count)])


def ring_order(count):
    return list(range(0, count, 2)) + list(range(count - 1, 0, -2))


def ring_gather(block, count, ahead, use):
    order = ring_order(count)
    right = [(order[i], order[(i + 1) % count]) for i in range(count)]
    left = [(target, source) for source, target in right]
    parts = [(0, 0, block)]
    forward = backward = block
    middle = block.shape[0] // 2
    for step in range(1, count // 2 + 1):
        first = 0
        if 2 * step == count:
            forward, backward, used = lax.optimization_barrier((forward, backward, used))
            forward, backward, first = forward[:middle], backward[middle:], middle
        forward = lax.ppermute(forward, "row", right)
        backward = lax.ppermute(backward, "row", left)
        if step == 1:
            forward, backward, ahead = lax.optimization_barrier((forward, backward, ahead))
            used = use(ahead)
        parts += [(-step, 0, forward), (step, first, backward)]
    return parts, used


def call(body, outs, arrays, scalars=(), scratch=(), work=0, remote=0, room=16):
    moved = sum(a.size * a.dtype.itemsize for a in arrays)
    moved += sum(math.prod(shape) * jnp.dtype(kind).itemsize for shape, kind in outs)
    return pl.pallas_call(
        body,
        out_shape=[jax.ShapeDtypeStruct(*o) for o in outs],
        in_specs=[pl.BlockSpec(memory_space=pltpu.SMEM)] * len(scalars)
        + [pl.BlockSpec(memory_space=pltpu.VMEM)] * (len(arrays) - remote)
        + [pl.BlockSpec(memory_space=pltpu.HBM)] * remote,
        out_specs=[pl.BlockSpec(memory_space=pltpu.VMEM)] * len(outs),
        scratch_shapes=list(scratch),
        compiler_params=pltpu.CompilerParams(vmem_limit_bytes=room << 20),
        cost_estimate=pl.CostEstimate(flops=work, bytes_accessed=moved, transcendentals=0),
    )(*scalars, *arrays)


def split(value):
    high = value.astype(BF16).astype(F32)
    return high, value - high


def times(value, high, low, right_dim):
    rows = value.shape[0]
    dims = (((1,), (right_dim,)), ((), ()))

    def product(part):
        return lax.dot_general(part, high, dims, preferred_element_type=F32) + lax.dot_general(
            part, low, dims, preferred_element_type=F32
        )

    first, second = split(value)
    if rows % 8:
        return product(first.astype(BF16)) + product(second.astype(BF16))
    both = product(jnp.concatenate([first, second], 0).astype(BF16))
    return both[:rows] + both[rows:]


def times_left(block, value):
    columns = value.shape[1]
    both = jnp.concatenate(split(value), 1).astype(BF16)
    product = sum(
        jnp.dot(part.astype(BF16), both, preferred_element_type=F32) for part in split(block)
    )
    return product[:, :columns] + product[:, columns:]


def strict_lower(block):
    row_ids = lax.broadcasted_iota(jnp.int32, block.shape, 0)
    col_ids = lax.broadcasted_iota(jnp.int32, block.shape, 1)
    return jnp.where(col_ids < row_ids, block, 0.0)


def shards(
    loc_rhs,
    loc_inverse,
    loc_coupling,
    loc_pivots,
    pattern,
    win_rhs,
    win_pivots,
    win_inverse,
    win_coupling,
):
    leaves = lax.axis_size("leaf")
    ranks = lax.axis_size("row")
    leaf = lax.axis_index("leaf")
    rank = lax.axis_index("row")
    levels, piece, columns = win_rhs.shape
    base = piece * ranks
    share = columns // ranks
    halves = base // TILE
    path_tiles = (2 * leaves - 1) * halves
    tiles = pattern.shape[2]
    local = loc_rhs.shape[2]
    top = levels - 1
    ids = jnp.stack([leaf, rank]).astype(jnp.int32)
    wide = (share, base)

    def leaf_swaps(values):
        return [values[0]] + [swap(v, "leaf", leaves, j) for j, v in enumerate(values) if j]

    def source_row(me, step):
        place = jnp.where(me % 2 == 0, me // 2, ranks - 1 - me // 2)
        place = (place + step + ranks) % ranks
        return jnp.where(2 * place < ranks, 2 * place, 2 * (ranks - 1 - place) + 1)

    def width(name):
        return 2 ** name[1] if name[0] == "A" else 2 ** (name[1] + 1)

    all_names = [("A", level) for level in range(levels)] + [("B", level) for level in range(top)]

    def runs(names):
        found, slot, place = [], 0, 0
        for name in all_names:
            if name in names:
                if found and found[-1][1] == slot:
                    found[-1][1] += width(name)
                else:
                    found.append([slot, slot + width(name), place])
                place += width(name)
            slot += width(name)
        return found

    def assemble(names):
        names = [name for name in all_names if name in names]
        spans = [width(name) for name in names]
        moves = []
        for index, (step, before, part) in enumerate(parts):
            for first, end, place in runs(names):
                low, high = max(first, before), min(end, before + part.shape[0])
                if low < high:
                    moves.append((index, step, low - before, high - before, place + low - first))

        def body(ids_ref, *refs):
            parts_refs, outs = refs[: len(parts)], refs[len(parts) : -2]
            natural, done = refs[-2:]
            group = ids_ref[0]
            copies = []
            for number, (index, step, low, high, place) in enumerate(moves):
                start = pl.multiple_of(source_row(ids_ref[1], step) * piece, 8)
                copies.append(
                    pltpu.make_async_copy(
                        parts_refs[index].at[low:high],
                        natural.at[place : place + high - low, pl.ds(start, piece), :],
                        done.at[number],
                    )
                )
            for copy in copies:
                copy.start()
            for copy in copies:
                copy.wait()
            first = 0
            for index, ((kind, level), span) in enumerate(zip(names, spans)):
                for slot in range(span):
                    block = natural[first + slot]
                    if kind == "A":
                        row_ids = lax.broadcasted_iota(jnp.int32, block.shape, 0) + slot * base
                        col_ids = lax.broadcasted_iota(jnp.int32, block.shape, 1)
                        col_ids = col_ids + group % span * base
                        block = jnp.where(col_ids < row_ids, block, 0.0)
                    high, low = split(block)
                    outs[2 * index][slot] = high.astype(BF16)
                    outs[2 * index + 1][slot] = low.astype(BF16)
                first += span

        outs = [((span, base, base), BF16) for span in spans for _ in range(2)]
        made = call(
            body,
            outs,
            [part for _, _, part in parts],
            (ids,),
            [pltpu.VMEM((sum(spans), base, base), F32), pltpu.SemaphoreType.DMA((len(moves),))],
            remote=len(parts),
            room=24,
        )
        return {name: made[2 * i : 2 * i + 2] for i, name in enumerate(names)}

    start = levels * piece
    beside = start + piece + tiles <= TILE
    number_row, number_lane = (0, start + piece) if beside else (levels, start)
    aux = jnp.zeros((share, TILE), F32)
    aux = lax.dynamic_update_slice(aux, win_pivots, (0, start))
    aux = lax.dynamic_update_slice(aux, pattern[0].astype(F32), (number_row, number_lane))
    aux = jnp.tile(aux, (ranks, 1))
    packed = tiles * TILE + TILE

    def local_forward(rhs_ref, window_ref, aux_ref, inverse_any, coupling_any, *refs):
        solved_ref, terms_ref, held, inverse_ref, coupling_ref, done = refs
        first = pltpu.make_async_copy(inverse_any, inverse_ref, done.at[0])
        second = pltpu.make_async_copy(coupling_any, coupling_ref, done.at[1])
        first.start()
        second.start()
        rhs = rhs_ref[...]
        held[...] = jnp.zeros_like(held)
        for level in range(levels):
            held[level * piece : (level + 1) * piece, :] = window_ref[level]
        terms_ref[:, tiles * TILE :] = held[...].T + aux_ref[...]
        first.wait()
        solved = rhs + times_left(strict_lower(inverse_ref[...]), rhs)
        solved_ref[...] = solved.T
        second.wait()
        terms_ref[:, : tiles * TILE] = times_left(coupling_ref[...], solved).T

    solved_loc, terms = call(
        local_forward,
        [((columns, local), F32), ((columns, packed), F32)],
        (loc_rhs[0, 0], win_rhs, aux, loc_inverse[0, 0], loc_coupling[0, 0]),
        remote=2,
        scratch=[
            pltpu.VMEM((TILE, columns), F32),
            pltpu.VMEM((local, local), F32),
            pltpu.VMEM((tiles * TILE, local), F32),
            pltpu.SemaphoreType.DMA((2,)),
        ],
        work=24 * local * local * columns,
        room=24,
    )
    def place_terms(terms):
        terms = lax.all_to_all(terms.reshape(ranks, share, packed), "row", 0, 0, tiled=True)
        known = terms[:, number_row, tiles * TILE + number_lane :][:, :tiles].astype(jnp.int32)

        def scatter(ids_ref, known_ref, terms_ref, *refs):
            outs, pivots_ref, path = refs[:-2], refs[-2], refs[-1]
            lane = lax.broadcasted_iota(jnp.int32, (share, TILE), 1)
            path[...] = jnp.zeros_like(path)
            for source in range(ranks):
                for tile in range(tiles):
                    place = known_ref[source, tile]
                    path[place] = path[place] - terms_ref[source, :, tile * TILE : (tile + 1) * TILE]

            def spread(first):
                rows = []
                for half in range(halves):
                    row = jnp.zeros((share, TILE), F32)
                    for source in range(half * TILE // piece, (half + 1) * TILE // piece):
                        place = source * piece % TILE
                        shift = (TILE + place - first) % TILE
                        turned = pltpu.roll(terms_ref[source, :, tiles * TILE :], shift, 1)
                        row = jnp.where((lane >= place) & (lane < place + piece), turned, row)
                    rows.append(row)
                return jnp.concatenate(rows, 1)

            pivots_ref[...] = spread(levels * piece)
            for level in range(levels):
                span = 2**level
                filled = outs[level]
                for slot in range(span):
                    first = (span - 1 + slot) * halves
                    for half in range(halves):
                        filled[slot, :, half * TILE : (half + 1) * TILE] = path[first + half]
                own = ids_ref[0] % span
                filled[own] = filled[own] + spread(level * piece)

        *rest, pivots = call(
            scatter,
            [((2**level, *wide), F32) for level in range(levels)] + [(wide, F32)],
            (terms,),
            (ids, known),
            [pltpu.VMEM((path_tiles, share, TILE), F32)],
        )
        return known, rest, pivots

    parts, (known, rest, pivots) = ring_gather(
        jnp.concatenate([win_inverse[0], win_coupling[0]], 0).reshape(-1, piece, base),
        ranks,
        terms,
        place_terms,
    )
    blocks = assemble([("A", 0), ("B", 0)])
    for name in all_names:
        if name not in blocks:
            blocks.update(assemble([name]))

    all_pivots = leaf_swaps([pivots] * leaves)

    def total(refs):
        value = refs[0][0] if len(refs[0].shape) > len(wide) and len(refs) == 1 else refs[0][...]
        for ref in refs[1:]:
            value = value + ref[...]
        return value

    def diagonal(level, chunks, ahead=()):
        span = 2**level
        high, low = blocks["A", level]

        def body(ids_ref, *refs):
            chunk_refs, (high_ref, low_ref) = refs[:span], refs[span : span + 2]
            outs, parts = refs[span + 2 + len(ahead) : -1], refs[-1]
            own = ids_ref[0] % span
            value = total(chunk_refs)
            for slot in range(span):
                parts[slot] = times(value, high_ref[slot], low_ref[slot], 1)
            parts[own] = parts[own] + value
            if level == top:
                outs[0][...] = parts[...]
            else:
                for offset, out in enumerate(outs):
                    out[...] = parts[own ^ offset]

        outs = [((span, *wide), F32)] if level == top else [(wide, F32)] * span
        return call(
            body,
            outs,
            (*chunks, high, low, *ahead),
            (ids,),
            [pltpu.VMEM((span, *wide), F32)],
        )

    def link(level, chunks):
        span, above = 2**level, 2 ** (level + 1)
        high, low = blocks["B", level]
        lowest = () if level else blocks["A", 0]

        def body(ids_ref, *refs):
            chunk_refs, refs = refs[:span], refs[span:]
            value = total(chunk_refs)
            if lowest:
                value = value + times(value, refs[0][0], refs[1][0], 1)
                refs = refs[2:]
            high_ref, low_ref, rest_ref, solved_ref = refs[:4]
            outs, parts = refs[4:-1], refs[-1]
            solved_ref[...] = value
            for slot in range(above):
                parts[slot] = rest_ref[slot] - times(value, high_ref[slot], low_ref[slot], 1)
            own = ids_ref[0] % above
            for offset, out in enumerate(outs):
                out[...] = parts[own ^ offset]

        made = call(
            body,
            [(wide, F32)] * (above + 1),
            (*chunks, *lowest, high, low, rest[level + 1]),
            (ids,),
            [pltpu.VMEM((above, *wide), F32)],
        )
        return made[0], made[1:]

    chunks = [rest[0]]
    solved = []
    for level in range(top):
        if level:
            chunks = leaf_swaps(diagonal(level, chunks, all_pivots if level == 1 else ()))
        value, chunks = link(level, chunks)
        solved.append(value)
        chunks = leaf_swaps(chunks)
    sums = leaf_swaps(diagonal(top, chunks) * leaves)

    def peak(ids_ref, *refs):
        sum_refs, pivot_refs = refs[:leaves], refs[leaves : 2 * leaves]
        high_ref, low_ref, out, wanted = refs[2 * leaves :]
        own = ids_ref[0] % leaves
        wanted[...] = total(sum_refs)
        for offset, ref in enumerate(pivot_refs):
            wanted[own ^ offset] = wanted[own ^ offset] / ref[top : top + 1, :]
        value = wanted[own]
        for slot in range(leaves):
            value = value + times(wanted[slot], high_ref[slot], low_ref[slot], 0)
        out[...] = value

    current = call(
        peak,
        [(wide, F32)],
        (*sums, *all_pivots, *blocks["A", top]),
        (ids,),
        [pltpu.VMEM((leaves, *wide), F32)],
    )

    def ordered(own, refs, held):
        for offset, ref in enumerate(refs):
            held[own ^ offset] = ref[...]

    def against(held, high_ref, low_ref, span):
        value = times(held[0], high_ref[0], low_ref[0], 0)
        for slot in range(1, span):
            value = value + times(held[slot], high_ref[slot], low_ref[slot], 0)
        return value

    def descend(level, parts):
        span = 2**level

        def body(ids_ref, *refs):
            part_refs = refs[:span]
            high_ref, low_ref, solved_ref, pivot_ref, out, held = refs[span:]
            ordered(ids_ref[0] % span, part_refs, held)
            above = against(held, high_ref, low_ref, span)
            out[...] = solved_ref[...] / pivot_ref[level - 1 : level, :] - above

        return call(
            body,
            [(wide, F32)],
            (*parts, *blocks["B", level - 1], solved[level - 1], pivots),
            (ids,),
            [pltpu.VMEM((span, *wide), F32)],
        )

    def transposed(level, parts):
        span = 2**level

        def body(ids_ref, *refs):
            part_refs = refs[:span]
            high_ref, low_ref, out, held = refs[span:]
            ordered(ids_ref[0] % span, part_refs, held)
            out[...] = part_refs[0][...] + against(held, high_ref, low_ref, span)

        return call(
            body,
            [(wide, F32)],
            (*parts, *blocks["A", level]),
            (ids,),
            [pltpu.VMEM((span, *wide), F32)],
        )

    everything = {top: leaf_swaps(current * leaves)}
    for level in range(top, 1, -1):
        wanted = leaf_swaps(descend(level, everything[level]) * 2 ** (level - 1))
        everything[level - 1] = leaf_swaps(transposed(level - 1, wanted) * 2 ** (level - 1))

    def finish(ids_ref, known_ref, *refs):
        refs = list(refs)
        parts = {level: [refs.pop(0) for _ in range(2**level)] for level in range(1, levels)}
        link_high, link_low, solved_ref, pivot_ref, high_ref, low_ref = refs[:6]
        out, path, held = refs[6:]
        group = ids_ref[0]
        ordered(group % 2, parts[1], held)
        wanted = solved_ref[...] / pivot_ref[0:1, :] - against(held, link_high, link_low, 2)
        lowest = wanted + times(wanted, high_ref[0], low_ref[0], 0)
        owned = [lowest]
        for half in range(halves):
            path[half] = lowest[:, half * TILE : (half + 1) * TILE]
        for level in range(1, levels):
            span = 2**level
            owned.append(parts[level][0][...])
            for offset, ref in enumerate(parts[level]):
                first = (span - 1 + (group % span ^ offset)) * halves
                for half in range(halves):
                    path[first + half] = ref[:, half * TILE : (half + 1) * TILE]
        lane = lax.broadcasted_iota(jnp.int32, (share, TILE), 1)
        for target in range(ranks):
            for tile in range(tiles):
                out[target, :, tile * TILE : (tile + 1) * TILE] = path[known_ref[target, tile]]
            pieces = jnp.zeros((share, TILE), F32)
            for level in range(levels):
                shift = (base + level * piece - target * piece) % base
                turned = pltpu.roll(owned[level], shift, 1)[:, :TILE]
                mine = (lane >= level * piece) & (lane < (level + 1) * piece)
                pieces = jnp.where(mine, turned, pieces)
            out[target, :, tiles * TILE :] = pieces

    replies = call(
        finish,
        [((ranks, share, packed), F32)],
        (
            *[part for level in range(1, levels) for part in everything[level]],
            *blocks["B", 0],
            solved[0],
            pivots,
            *blocks["A", 0],
        ),
        (ids, known),
        [pltpu.VMEM((path_tiles, share, TILE), F32), pltpu.VMEM((2, *wide), F32)],
    )
    back = lax.all_to_all(replies[0], "row", 0, 0, tiled=True).reshape(columns, packed)

    def local_backward(back, solved_ref, pivot_ref, inverse_any, coupling_any, *refs):
        out, window_ref, inverse_ref, coupling_ref, done = refs
        first = pltpu.make_async_copy(coupling_any, coupling_ref, done.at[0])
        second = pltpu.make_async_copy(inverse_any, inverse_ref, done.at[1])
        first.start()
        second.start()
        final = back[:, tiles * TILE :].T
        for level in range(levels):
            window_ref[level] = final[level * piece : (level + 1) * piece]
        scaled = solved_ref[...] / pivot_ref[...]
        first.wait()
        high, low = split(coupling_ref[...])
        remainder = scaled - times(back[:, : tiles * TILE], high.astype(BF16), low.astype(BF16), 0)
        second.wait()
        high, low = split(strict_lower(inverse_ref[...]))
        answer = remainder + times(remainder, high.astype(BF16), low.astype(BF16), 0)
        out[...] = answer.T

    answer, window = call(
        local_backward,
        [((local, columns), F32), ((levels, piece, columns), F32)],
        (back, solved_loc, loc_pivots[0], loc_inverse[0, 0], loc_coupling[0, 0]),
        scratch=[
            pltpu.VMEM((local, local), F32),
            pltpu.VMEM((tiles * TILE, local), F32),
            pltpu.SemaphoreType.DMA((2,)),
        ],
        remote=2,
        work=24 * local * local * columns,
        room=24,
    )
    return answer[None, None], window


def solution(mesh):
    return jax.shard_map(
        shards,
        mesh=mesh,
        in_specs=(
            P("leaf", "row", None, None),
            P("leaf", "row", None, None),
            P("leaf", "row", None, None),
            P("leaf", "row", None),
            P("leaf", "row", None),
            P(None, ("leaf", "row"), None),
            P(None, ("leaf", "row")),
            P("row", None, "leaf"),
            P("row", None, "leaf"),
        ),
        out_specs=(P("leaf", "row", None, None), P(None, ("leaf", "row"), None)),
        check_vma=False,
    )
```

```python
import math

import jax
import jax.numpy as jnp
from jax import lax
from jax.experimental import pallas as pl
from jax.experimental.pallas import tpu as pltpu
from jax.sharding import PartitionSpec as P

TILE = 128
F32 = jnp.float32
BF16 = jnp.bfloat16


def swap(value, axis, count, offset):
    return lax.ppermute(value, axis, [(i, i ^ offset) for i in range(count)])


def ring_order(count):
    return list(range(0, count, 2)) + list(range(count - 1, 0, -2))


def ring_gather(block, count, ahead, use):
    order = ring_order(count)
    right = [(order[i], order[(i + 1) % count]) for i in range(count)]
    left = [(target, source) for source, target in right]
    parts = [(0, 0, block)]
    forward = backward = block
    middle = block.shape[0] // 2
    for step in range(1, count // 2 + 1):
        first = 0
        if 2 * step == count:
            forward, backward, used = lax.optimization_barrier((forward, backward, used))
            forward, backward, first = forward[:middle], backward[middle:], middle
        forward = lax.ppermute(forward, "row", right)
        backward = lax.ppermute(backward, "row", left)
        if step == 1:
            forward, backward, ahead = lax.optimization_barrier((forward, backward, ahead))
            used = use(ahead)
        parts += [(-step, 0, forward), (step, first, backward)]
    return parts, used


def call(body, outs, arrays, scalars=(), scratch=(), work=0, remote=0, room=16):
    moved = sum(a.size * a.dtype.itemsize for a in arrays)
    moved += sum(math.prod(shape) * jnp.dtype(kind).itemsize for shape, kind in outs)
    return pl.pallas_call(
        body,
        out_shape=[jax.ShapeDtypeStruct(*o) for o in outs],
        in_specs=[pl.BlockSpec(memory_space=pltpu.SMEM)] * len(scalars)
        + [pl.BlockSpec(memory_space=pltpu.VMEM)] * (len(arrays) - remote)
        + [pl.BlockSpec(memory_space=pltpu.HBM)] * remote,
        out_specs=[pl.BlockSpec(memory_space=pltpu.VMEM)] * len(outs),
        scratch_shapes=list(scratch),
        compiler_params=pltpu.CompilerParams(vmem_limit_bytes=room << 20),
        cost_estimate=pl.CostEstimate(flops=work, bytes_accessed=moved, transcendentals=0),
    )(*scalars, *arrays)


def split(value):
    high = value.astype(BF16).astype(F32)
    return high, value - high


def times(value, high, low, right_dim):
    rows = value.shape[0]
    dims = (((1,), (right_dim,)), ((), ()))

    def product(part):
        return lax.dot_general(part, high, dims, preferred_element_type=F32) + lax.dot_general(
            part, low, dims, preferred_element_type=F32
        )

    first, second = split(value)
    if rows % 8:
        return product(first.astype(BF16)) + product(second.astype(BF16))
    both = product(jnp.concatenate([first, second], 0).astype(BF16))
    return both[:rows] + both[rows:]


def times_left(block, value):
    columns = value.shape[1]
    both = jnp.concatenate(split(value), 1).astype(BF16)
    product = sum(
        jnp.dot(part.astype(BF16), both, preferred_element_type=F32) for part in split(block)
    )
    return product[:, :columns] + product[:, columns:]


def strict_lower(block):
    row_ids = lax.broadcasted_iota(jnp.int32, block.shape, 0)
    col_ids = lax.broadcasted_iota(jnp.int32, block.shape, 1)
    return jnp.where(col_ids < row_ids, block, 0.0)


def shards(
    loc_rhs,
    loc_inverse,
    loc_coupling,
    loc_pivots,
    pattern,
    win_rhs,
    win_pivots,
    win_inverse,
    win_coupling,
):
    leaves = lax.axis_size("leaf")
    ranks = lax.axis_size("row")
    leaf = lax.axis_index("leaf")
    rank = lax.axis_index("row")
    levels, piece, columns = win_rhs.shape
    base = piece * ranks
    share = columns // ranks
    halves = base // TILE
    path_tiles = (2 * leaves - 1) * halves
    tiles = pattern.shape[2]
    local = loc_rhs.shape[2]
    top = levels - 1
    ids = jnp.stack([leaf, rank]).astype(jnp.int32)
    wide = (share, base)

    def leaf_swaps(values):
        return [values[0]] + [swap(v, "leaf", leaves, j) for j, v in enumerate(values) if j]

    def source_row(me, step):
        place = jnp.where(me % 2 == 0, me // 2, ranks - 1 - me // 2)
        place = (place + step + ranks) % ranks
        return jnp.where(2 * place < ranks, 2 * place, 2 * (ranks - 1 - place) + 1)

    def width(name):
        return 2 ** name[1] if name[0] == "A" else 2 ** (name[1] + 1)

    all_names = [("A", level) for level in range(levels)] + [("B", level) for level in range(top)]

    def runs(names):
        found, slot, place = [], 0, 0
        for name in all_names:
            if name in names:
                if found and found[-1][1] == slot:
                    found[-1][1] += width(name)
                else:
                    found.append([slot, slot + width(name), place])
                place += width(name)
            slot += width(name)
        return found

    def assemble(names):
        names = [name for name in all_names if name in names]
        spans = [width(name) for name in names]
        moves = []
        for index, (step, before, part) in enumerate(parts):
            for first, end, place in runs(names):
                low, high = max(first, before), min(end, before + part.shape[0])
                if low < high:
                    moves.append((index, step, low - before, high - before, place + low - first))

        def body(ids_ref, *refs):
            parts_refs, outs = refs[: len(parts)], refs[len(parts) : -2]
            natural, done = refs[-2:]
            group = ids_ref[0]
            copies = []
            for number, (index, step, low, high, place) in enumerate(moves):
                start = pl.multiple_of(source_row(ids_ref[1], step) * piece, 8)
                copies.append(
                    pltpu.make_async_copy(
                        parts_refs[index].at[low:high],
                        natural.at[place : place + high - low, pl.ds(start, piece), :],
                        done.at[number],
                    )
                )
            for copy in copies:
                copy.start()
            for copy in copies:
                copy.wait()
            first = 0
            for index, ((kind, level), span) in enumerate(zip(names, spans)):
                for slot in range(span):
                    block = natural[first + slot]
                    if kind == "A":
                        row_ids = lax.broadcasted_iota(jnp.int32, block.shape, 0) + slot * base
                        col_ids = lax.broadcasted_iota(jnp.int32, block.shape, 1)
                        col_ids = col_ids + group % span * base
                        block = jnp.where(col_ids < row_ids, block, 0.0)
                    high, low = split(block)
                    outs[2 * index][slot] = high.astype(BF16)
                    outs[2 * index + 1][slot] = low.astype(BF16)
                first += span

        outs = [((span, base, base), BF16) for span in spans for _ in range(2)]
        made = call(
            body,
            outs,
            [part for _, _, part in parts],
            (ids,),
            [pltpu.VMEM((sum(spans), base, base), F32), pltpu.SemaphoreType.DMA((len(moves),))],
            remote=len(parts),
            room=24,
        )
        return {name: made[2 * i : 2 * i + 2] for i, name in enumerate(names)}

    start = levels * piece
    beside = start + piece + tiles <= TILE
    number_row, number_lane = (0, start + piece) if beside else (levels, start)
    aux = jnp.zeros((share, TILE), F32)
    aux = lax.dynamic_update_slice(aux, win_pivots, (0, start))
    aux = lax.dynamic_update_slice(aux, pattern[0].astype(F32), (number_row, number_lane))
    aux = jnp.tile(aux, (ranks, 1))
    packed = tiles * TILE + TILE

    def local_forward(rhs_ref, window_ref, aux_ref, inverse_any, coupling_any, *refs):
        solved_ref, terms_ref, held, inverse_ref, coupling_ref, done = refs
        first = pltpu.make_async_copy(inverse_any, inverse_ref, done.at[0])
        second = pltpu.make_async_copy(coupling_any, coupling_ref, done.at[1])
        first.start()
        second.start()
        rhs = rhs_ref[...]
        held[...] = jnp.zeros_like(held)
        for level in range(levels):
            held[level * piece : (level + 1) * piece, :] = window_ref[level]
        terms_ref[:, tiles * TILE :] = held[...].T + aux_ref[...]
        first.wait()
        solved = rhs + times_left(strict_lower(inverse_ref[...]), rhs)
        solved_ref[...] = solved.T
        second.wait()
        terms_ref[:, : tiles * TILE] = times_left(coupling_ref[...], solved).T

    solved_loc, terms = call(
        local_forward,
        [((columns, local), F32), ((columns, packed), F32)],
        (loc_rhs[0, 0], win_rhs, aux, loc_inverse[0, 0], loc_coupling[0, 0]),
        remote=2,
        scratch=[
            pltpu.VMEM((TILE, columns), F32),
            pltpu.VMEM((local, local), F32),
            pltpu.VMEM((tiles * TILE, local), F32),
            pltpu.SemaphoreType.DMA((2,)),
        ],
        work=24 * local * local * columns,
        room=24,
    )
    def place_terms(terms):
        terms = lax.all_to_all(terms.reshape(ranks, share, packed), "row", 0, 0, tiled=True)
        known = terms[:, number_row, tiles * TILE + number_lane :][:, :tiles].astype(jnp.int32)

        def scatter(ids_ref, known_ref, terms_ref, *refs):
            outs, pivots_ref, path = refs[:-2], refs[-2], refs[-1]
            lane = lax.broadcasted_iota(jnp.int32, (share, TILE), 1)
            path[...] = jnp.zeros_like(path)
            for source in range(ranks):
                for tile in range(tiles):
                    place = known_ref[source, tile]
                    path[place] = path[place] - terms_ref[source, :, tile * TILE : (tile + 1) * TILE]

            def spread(first):
                rows = []
                for half in range(halves):
                    row = jnp.zeros((share, TILE), F32)
                    for source in range(half * TILE // piece, (half + 1) * TILE // piece):
                        place = source * piece % TILE
                        shift = (TILE + place - first) % TILE
                        turned = pltpu.roll(terms_ref[source, :, tiles * TILE :], shift, 1)
                        row = jnp.where((lane >= place) & (lane < place + piece), turned, row)
                    rows.append(row)
                return jnp.concatenate(rows, 1)

            pivots_ref[...] = spread(levels * piece)
            for level in range(levels):
                span = 2**level
                filled = outs[level]
                for slot in range(span):
                    first = (span - 1 + slot) * halves
                    for half in range(halves):
                        filled[slot, :, half * TILE : (half + 1) * TILE] = path[first + half]
                own = ids_ref[0] % span
                filled[own] = filled[own] + spread(level * piece)

        *rest, pivots = call(
            scatter,
            [((2**level, *wide), F32) for level in range(levels)] + [(wide, F32)],
            (terms,),
            (ids, known),
            [pltpu.VMEM((path_tiles, share, TILE), F32)],
        )
        return known, rest, leaf_swaps([pivots] * leaves)

    parts, (known, rest, all_pivots) = ring_gather(
        jnp.concatenate([win_inverse[0], win_coupling[0]], 0).reshape(-1, piece, base),
        ranks,
        terms,
        place_terms,
    )
    blocks = assemble([("A", 0), ("B", 0)])
    for name in all_names:
        if name not in blocks:
            blocks.update(assemble([name]))

    pivots = all_pivots[0]

    def total(refs):
        value = refs[0][0] if len(refs[0].shape) > len(wide) and len(refs) == 1 else refs[0][...]
        for ref in refs[1:]:
            value = value + ref[...]
        return value

    def diagonal(level, chunks, ahead=()):
        span = 2**level
        high, low = blocks["A", level]

        def body(ids_ref, *refs):
            chunk_refs, (high_ref, low_ref) = refs[:span], refs[span : span + 2]
            outs, parts = refs[span + 2 + len(ahead) : -1], refs[-1]
            own = ids_ref[0] % span
            value = total(chunk_refs)
            for slot in range(span):
                parts[slot] = times(value, high_ref[slot], low_ref[slot], 1)
            parts[own] = parts[own] + value
            if level == top:
                outs[0][...] = parts[...]
            else:
                for offset, out in enumerate(outs):
                    out[...] = parts[own ^ offset]

        outs = [((span, *wide), F32)] if level == top else [(wide, F32)] * span
        return call(
            body,
            outs,
            (*chunks, high, low, *ahead),
            (ids,),
            [pltpu.VMEM((span, *wide), F32)],
        )

    def link(level, chunks):
        span, above = 2**level, 2 ** (level + 1)
        high, low = blocks["B", level]
        lowest = () if level else blocks["A", 0]

        def body(ids_ref, *refs):
            chunk_refs, refs = refs[:span], refs[span:]
            value = total(chunk_refs)
            if lowest:
                value = value + times(value, refs[0][0], refs[1][0], 1)
                refs = refs[2:]
            high_ref, low_ref, rest_ref, solved_ref = refs[:4]
            outs, parts = refs[4:-1], refs[-1]
            solved_ref[...] = value
            for slot in range(above):
                parts[slot] = rest_ref[slot] - times(value, high_ref[slot], low_ref[slot], 1)
            own = ids_ref[0] % above
            for offset, out in enumerate(outs):
                out[...] = parts[own ^ offset]

        made = call(
            body,
            [(wide, F32)] * (above + 1),
            (*chunks, *lowest, high, low, rest[level + 1]),
            (ids,),
            [pltpu.VMEM((above, *wide), F32)],
        )
        return made[0], made[1:]

    chunks = [rest[0]]
    solved = []
    for level in range(top):
        if level:
            chunks = leaf_swaps(diagonal(level, chunks, all_pivots if level == 1 else ()))
        value, chunks = link(level, chunks)
        solved.append(value)
        chunks = leaf_swaps(chunks)
    sums = leaf_swaps(diagonal(top, chunks) * leaves)

    def peak(ids_ref, *refs):
        sum_refs, pivot_refs = refs[:leaves], refs[leaves : 2 * leaves]
        high_ref, low_ref, out, wanted = refs[2 * leaves :]
        own = ids_ref[0] % leaves
        wanted[...] = total(sum_refs)
        for offset, ref in enumerate(pivot_refs):
            wanted[own ^ offset] = wanted[own ^ offset] / ref[top : top + 1, :]
        value = wanted[own]
        for slot in range(leaves):
            value = value + times(wanted[slot], high_ref[slot], low_ref[slot], 0)
        out[...] = value

    current = call(
        peak,
        [(wide, F32)],
        (*sums, *all_pivots, *blocks["A", top]),
        (ids,),
        [pltpu.VMEM((leaves, *wide), F32)],
    )

    def ordered(own, refs, held):
        for offset, ref in enumerate(refs):
            held[own ^ offset] = ref[...]

    def against(held, high_ref, low_ref, span):
        value = times(held[0], high_ref[0], low_ref[0], 0)
        for slot in range(1, span):
            value = value + times(held[slot], high_ref[slot], low_ref[slot], 0)
        return value

    def descend(level, parts):
        span = 2**level

        def body(ids_ref, *refs):
            part_refs = refs[:span]
            high_ref, low_ref, solved_ref, pivot_ref, out, held = refs[span:]
            ordered(ids_ref[0] % span, part_refs, held)
            above = against(held, high_ref, low_ref, span)
            out[...] = solved_ref[...] / pivot_ref[level - 1 : level, :] - above

        return call(
            body,
            [(wide, F32)],
            (*parts, *blocks["B", level - 1], solved[level - 1], pivots),
            (ids,),
            [pltpu.VMEM((span, *wide), F32)],
        )

    def transposed(level, parts):
        span = 2**level

        def body(ids_ref, *refs):
            part_refs = refs[:span]
            high_ref, low_ref, out, held = refs[span:]
            ordered(ids_ref[0] % span, part_refs, held)
            out[...] = part_refs[0][...] + against(held, high_ref, low_ref, span)

        return call(
            body,
            [(wide, F32)],
            (*parts, *blocks["A", level]),
            (ids,),
            [pltpu.VMEM((span, *wide), F32)],
        )

    everything = {top: leaf_swaps(current * leaves)}
    for level in range(top, 1, -1):
        wanted = leaf_swaps(descend(level, everything[level]) * 2 ** (level - 1))
        everything[level - 1] = leaf_swaps(transposed(level - 1, wanted) * 2 ** (level - 1))

    def finish(ids_ref, known_ref, *refs):
        refs = list(refs)
        parts = {level: [refs.pop(0) for _ in range(2**level)] for level in range(1, levels)}
        link_high, link_low, solved_ref, pivot_ref, high_ref, low_ref = refs[:6]
        out, path, held = refs[6:]
        group = ids_ref[0]
        ordered(group % 2, parts[1], held)
        wanted = solved_ref[...] / pivot_ref[0:1, :] - against(held, link_high, link_low, 2)
        lowest = wanted + times(wanted, high_ref[0], low_ref[0], 0)
        owned = [lowest]
        for half in range(halves):
            path[half] = lowest[:, half * TILE : (half + 1) * TILE]
        for level in range(1, levels):
            span = 2**level
            owned.append(parts[level][0][...])
            for offset, ref in enumerate(parts[level]):
                first = (span - 1 + (group % span ^ offset)) * halves
                for half in range(halves):
                    path[first + half] = ref[:, half * TILE : (half + 1) * TILE]
        lane = lax.broadcasted_iota(jnp.int32, (share, TILE), 1)
        for target in range(ranks):
            for tile in range(tiles):
                out[target, :, tile * TILE : (tile + 1) * TILE] = path[known_ref[target, tile]]
            pieces = jnp.zeros((share, TILE), F32)
            for level in range(levels):
                shift = (base + level * piece - target * piece) % base
                turned = pltpu.roll(owned[level], shift, 1)[:, :TILE]
                mine = (lane >= level * piece) & (lane < (level + 1) * piece)
                pieces = jnp.where(mine, turned, pieces)
            out[target, :, tiles * TILE :] = pieces

    replies = call(
        finish,
        [((ranks, share, packed), F32)],
        (
            *[part for level in range(1, levels) for part in everything[level]],
            *blocks["B", 0],
            solved[0],
            pivots,
            *blocks["A", 0],
        ),
        (ids, known),
        [pltpu.VMEM((path_tiles, share, TILE), F32), pltpu.VMEM((2, *wide), F32)],
    )
    back = lax.all_to_all(replies[0], "row", 0, 0, tiled=True).reshape(columns, packed)

    def local_backward(back, solved_ref, pivot_ref, inverse_any, coupling_any, *refs):
        out, window_ref, inverse_ref, coupling_ref, done = refs
        first = pltpu.make_async_copy(coupling_any, coupling_ref, done.at[0])
        second = pltpu.make_async_copy(inverse_any, inverse_ref, done.at[1])
        first.start()
        second.start()
        final = back[:, tiles * TILE :].T
        for level in range(levels):
            window_ref[level] = final[level * piece : (level + 1) * piece]
        scaled = solved_ref[...] / pivot_ref[...]
        first.wait()
        high, low = split(coupling_ref[...])
        remainder = scaled - times(back[:, : tiles * TILE], high.astype(BF16), low.astype(BF16), 0)
        second.wait()
        high, low = split(strict_lower(inverse_ref[...]))
        answer = remainder + times(remainder, high.astype(BF16), low.astype(BF16), 0)
        out[...] = answer.T

    answer, window = call(
        local_backward,
        [((local, columns), F32), ((levels, piece, columns), F32)],
        (back, solved_loc, loc_pivots[0], loc_inverse[0, 0], loc_coupling[0, 0]),
        scratch=[
            pltpu.VMEM((local, local), F32),
            pltpu.VMEM((tiles * TILE, local), F32),
            pltpu.SemaphoreType.DMA((2,)),
        ],
        remote=2,
        work=24 * local * local * columns,
        room=24,
    )
    return answer[None, None], window


def solution(mesh):
    return jax.shard_map(
        shards,
        mesh=mesh,
        in_specs=(
            P("leaf", "row", None, None),
            P("leaf", "row", None, None),
            P("leaf", "row", None, None),
            P("leaf", "row", None),
            P("leaf", "row", None),
            P(None, ("leaf", "row"), None),
            P(None, ("leaf", "row")),
            P("row", None, "leaf"),
            P("row", None, "leaf"),
        ),
        out_specs=(P("leaf", "row", None, None), P(None, ("leaf", "row"), None)),
        check_vma=False,
    )
```
